512 devices in a mesh: gx: 64 (over z_hi, y, core), gy: 8 (over x, z_lo).
Axes of the slice: x: 4, y: 8, z: 8 (z_hi: 4, z_lo: 2; z = z_hi * 2 + z_lo), core: 2. Of those that a mesh axis runs over, the one named last changes fastest.
Arguments:
- velocity: float32 [3, 1024, 128, 128], P(None, 'gx', 'gy'), may hold values from -6 to 6
- pressure: float32 [1024, 128, 128], P('gx', 'gy'), may hold values from -6 to 6
- land_type: int32 [1024, 128], P('gx', 'gy'), may hold values from 0 to 15
- turbine_cells: int32 [1024, 128, 128], P('gx', 'gy'), may hold values 0 or 1
- surface_drag: float32 [16], replicated, may hold values from 0.2 to 2
Outputs:
- velocity_new: float32 [3, 1024, 128, 128], P(None, 'gx', 'gy')
- pressure_new: float32 [1024, 128, 128], P('gx', 'gy')
The draws below stay inside these ranges and needn't reach their ends.
All inputs are finite; a program needn't handle non-finite values. No bound on the sum of `turbine_cells` on one device may be relied on, other than what follows from the above.
Results may differ from the reference program's by a relative error of at most 0.00002.
Values sent between devices are 32-bit elements; how exact they have to be, the bound alone decides.
No kernel may reach another device: no remote copies, remote signals or barrier semaphores. Data moves between devices by JAX's collectives and lax.ppermute only.
A program may use at most 64 MiB of HBM per device.

```python
import math
import jax
import jax.numpy as jnp
from jax import lax

NZ = 128
TYPES = 16
SWEEPS = 2
COARSE_SWEEPS = 4
NX = 1024
NY = 128


def set_ends(result, rng, low, top_value):
    spot = [jax.random.randint(jax.random.fold_in(rng, axis), (), 0, length) for axis, length in enumerate(result.shape)]
    main_axis = result.shape.index(max(result.shape))
    neighbour = spot[:main_axis] + [(spot[main_axis] + 1) % result.shape[main_axis]] + spot[main_axis + 1:]
    return result.at[tuple(spot)].set(low).at[tuple(neighbour)].set(top_value)


def shard_levels(own_key, shape, shards, low, high):
    def one(position, blocks):
        heights = jax.random.uniform(jax.random.fold_in(jax.random.fold_in(own_key, 6), position), (blocks,), jnp.float32, low / len(shards), high / len(shards))
        return jnp.repeat(jnp.exp(heights), shape[position] // blocks).reshape((-1,) + (1,) * (len(shape) - position - 1))

    factor_of = one(*shards[0])
    for cut in shards[1:]:
        factor_of = factor_of * one(*cut)
    return factor_of


def centred(stream_key, extent, width, reach, split=(), held_as=jnp.bfloat16):
    result = width * jax.random.normal(stream_key, extent, jnp.float32)
    if split:
        result = result * shard_levels(stream_key, extent, split, -0.22, 0.18)
    return jnp.clip(result, -reach, reach).astype(held_as)


def setup_inputs(seed: int = 0) -> dict:
    arg_keys = jax.random.split(jax.random.key(seed), 6)
    return {
        "velocity": centred(arg_keys[0], (3, NX, NY, NZ), 1.0, 6.0, ((1, 64), (2, 8)), jnp.float32),
        "pressure": centred(arg_keys[1], (NX, NY, NZ), 1.0, 6.0, ((0, 64), (1, 8)), jnp.float32),
        "land_type": set_ends(jax.random.randint(arg_keys[2], (NX, NY), 0, TYPES), jax.random.fold_in(arg_keys[2], 1), 0, TYPES - 1).astype(jnp.int32),
        "turbine_cells": set_ends((jax.random.randint(arg_keys[3], (NX, NY, NZ), 0, 8) < 1).astype(jnp.int32), jax.random.fold_in(arg_keys[3], 1), 0, 1),
        "surface_drag": jnp.clip(jnp.exp(jax.random.uniform(arg_keys[4], (TYPES,), jnp.float32, math.log(0.2), math.log(2.0))), 0.2, 2.0),
    }


time_step = 0.1
vertical_step = 0.5
eddy_coeff = 0.03
thrust_factor = 2.0
relax_weight = 0.8
driving_force = 1.0

def shifted(values, axis_pos, offset):
    starts = [1, 1, 1]
    starts[axis_pos] = 1 + offset
    length = [values.shape[-3] - 2, values.shape[-2] - 2, values.shape[-1] - 2]
    return values[..., starts[0]:starts[0] + length[0], starts[1]:starts[1] + length[1], starts[2]:starts[2] + length[2]]

def central(values, axis_pos):
    spacing = vertical_step if axis_pos == 2 else 1.0
    return (shifted(values, axis_pos, 1) - shifted(values, axis_pos, -1)) * (0.5 / spacing)

def surface_field(land_type, turbine_cells, surface_drag):
    kind_ids = jnp.arange(surface_drag.shape[0], dtype=jnp.int32)
    ground = lax.optimization_barrier(jnp.sum(jnp.where(land_type[:, :, None] == kind_ids, surface_drag, 0.0), axis=-1))
    ground_layer = jnp.arange(turbine_cells.shape[2], dtype=jnp.int32) == 0
    return thrust_factor * turbine_cells.astype(jnp.float32) + jnp.where(ground_layer, ground[:, :, None], 0.0)

def advance(padded, drag_field):
    gradient = [central(padded, axis_pos) for axis_pos in range(3)]
    strain = [[0.5 * (gradient[col_idx][row_idx] + gradient[row_idx][col_idx]) for col_idx in range(3)] for row_idx in range(3)]
    square_sum = strain[0][0] * strain[0][0]
    for row_idx in range(3):
        for col_idx in range(3):
            if row_idx + col_idx > 0:
                square_sum = square_sum + strain[row_idx][col_idx] * strain[row_idx][col_idx]
    viscosity = eddy_coeff * jnp.sqrt(2.0 * square_sum)
    centre = padded[:, 2:-2, 2:-2, 2:-2]
    wind_speed = jnp.sqrt(centre[0] * centre[0] + centre[1] * centre[1])
    updated = []
    for row_idx in range(3):
        change = jnp.zeros_like(centre[0])
        for col_idx in range(3):
            stress = 2.0 * viscosity * strain[row_idx][col_idx]
            change = change + central(stress, col_idx) - centre[col_idx] * gradient[col_idx][row_idx][1:-1, 1:-1, 1:-1]
        if row_idx < 2:
            change = change - drag_field * wind_speed * centre[row_idx]
        if row_idx == 0:
            change = change + driving_force
        updated.append(centre[row_idx] + time_step * change)
    return jnp.stack(updated)

def divergence(padded):
    return central(padded[0], 0) + central(padded[1], 1) + central(padded[2], 2)

def laplace(padded, spacing):
    centre = padded[1:-1, 1:-1, 1:-1]
    upright = vertical_step * spacing
    horizontal = (shifted(padded, 0, 1) + shifted(padded, 0, -1) + shifted(padded, 1, 1) + shifted(padded, 1, -1) - 4.0 * centre) / (spacing * spacing)
    vertical = (shifted(padded, 2, 1) + shifted(padded, 2, -1) - 2.0 * centre) / (upright * upright)
    return horizontal + vertical

def diagonal_of(spacing):
    upright = vertical_step * spacing
    return -(4.0 / (spacing * spacing) + 2.0 / (upright * upright))

def relax(pressure, padded, source, spacing):
    return pressure + relax_weight * (source - laplace(padded, spacing)) / diagonal_of(spacing)

def line_correct(pressure, residual, spacing):
    return pressure + relax_weight * lax.optimization_barrier(jnp.mean(residual, axis=1, keepdims=True)) / diagonal_of(spacing)

def periodic(values, pad_width, vertical_mode):
    leading = [(0, 0)] * (values.ndim - 3)
    values = jnp.pad(values, leading + [(pad_width, pad_width), (pad_width, pad_width), (0, 0)], mode='wrap')
    return jnp.pad(values, leading + [(0, 0), (0, 0), (pad_width, pad_width)], mode=vertical_mode)

def coarsen(values):
    return values.reshape(values.shape[0] // 2, 2, values.shape[1] // 2, 2, values.shape[2] // 2, 2).mean(axis=(1, 3, 5))

def refine(values):
    return jnp.repeat(jnp.repeat(jnp.repeat(values, 2, axis=0), 2, axis=1), 2, axis=2)

def cycle(pressure, source, depth_level):
    spacing = 2.0 ** depth_level
    if depth_level == 3:
        for sweep_idx in range(COARSE_SWEEPS):
            pressure = relax(pressure, periodic(pressure, 1, 'edge'), source, spacing)
        residual = source - laplace(periodic(pressure, 1, 'edge'), spacing)
        return line_correct(pressure, residual, spacing)
    for sweep_idx in range(SWEEPS):
        pressure = relax(pressure, periodic(pressure, 1, 'edge'), source, spacing)
    residual = source - laplace(periodic(pressure, 1, 'edge'), spacing)
    coarse_source = coarsen(residual)
    correction = cycle(jnp.zeros_like(coarse_source), coarse_source, depth_level + 1)
    pressure = pressure + refine(correction)
    for sweep_idx in range(SWEEPS):
        pressure = relax(pressure, periodic(pressure, 1, 'edge'), source, spacing)
    return pressure

def reference(velocity, pressure, land_type, turbine_cells, surface_drag):
    drag_field = surface_field(land_type, turbine_cells, surface_drag)
    star_velocity = advance(periodic(velocity, 2, 'constant'), drag_field)
    source = divergence(periodic(star_velocity, 1, 'constant')) / time_step
    pressure_new = cycle(pressure, source, 0)
    padded = periodic(pressure_new, 1, 'edge')
    gradient = jnp.stack([central(padded, 0), central(padded, 1), central(padded, 2)])
    return (star_velocity - time_step * gradient, pressure_new)
```

```python
import jax
import jax.numpy as jnp
from jax import lax
from jax.experimental import pallas as pl
from jax.experimental.pallas import tpu as pltpu
from jax.sharding import PartitionSpec as P

VH = 9
PH = 7
B = 16
VX = B + 2 * VH
PX = B + 2 * PH
SIDE = 3 * VH + 2 * PH
STEP = 0.1
EDDY = 0.03
COEFF = 0.8 / 12.0
WINDOW = 4
VMEM = pl.BlockSpec(memory_space=pltpu.VMEM)
SMEM = pl.BlockSpec(memory_space=pltpu.SMEM)
F32 = jnp.float32


def shape(*dims):
    return jax.ShapeDtypeStruct(dims, F32)


def call(body, outs, specs, scratch=()):
    return pl.pallas_call(
        body,
        out_shape=outs,
        in_specs=specs,
        out_specs=[VMEM] * len(outs),
        scratch_shapes=[pltpu.VMEM(s, F32) for s in scratch],
        compiler_params=pltpu.CompilerParams(vmem_limit_bytes=48 * 1024 * 1024),
    )


def iota(like, dim):
    return lax.broadcasted_iota(jnp.int32, like.shape, dim)


def lane_of(values):
    return iota(values, values.ndim - 1)


def row_of(values):
    return iota(values, values.ndim - 2)


def turn(values, amount, dim):
    return pltpu.roll(values, amount % values.shape[dim], dim)


def pack_x(place, land, drag_table, velocity, pressure, turbine, near, far, drag):
    core = place[0] % 2
    kinds = land[...]
    ground = jnp.zeros(kinds.shape, F32)
    for kind in range(16):
        ground = jnp.where(kinds == kind, drag_table[kind], ground)
    square = lax.broadcasted_iota(jnp.int32, (B, B), 0) == lax.broadcasted_iota(jnp.int32, (B, B), 1)
    for i in range(B):
        row = jnp.broadcast_to(ground[i : i + 1, :], (B, B))
        column = jnp.sum(jnp.where(square, row, 0.0), axis=1, keepdims=True)
        cells = turbine[i].astype(F32)
        drag[i] = 2.0 * cells + jnp.where(lane_of(cells) == 0, column, 0.0)

    def fill(out, high):
        start = B - VH if high else 0
        for a in range(3):
            out[a * VH : (a + 1) * VH] = velocity[a, start : start + VH]
        start = B - PH if high else 0
        out[3 * VH : 3 * VH + PH] = pressure[start : start + PH]
        out[3 * VH + PH : SIDE] = drag[start : start + PH]

    @pl.when(core == 0)
    def _():
        fill(near, True)
        fill(far, False)

    @pl.when(core == 1)
    def _():
        fill(near, False)
        fill(far, True)


def widen_x(place, velocity, pressure, drag, near, far, wide_v, wide_p, wide_d, near_y, far_y):
    core = place[0] % 2
    odd = place[1] % 2
    for a in range(3):
        wide_v[a, VH : VH + B] = velocity[a]
    wide_p[PH : PH + B] = pressure[...]
    wide_d[PH : PH + B] = drag[...]

    def fill(low, high):
        for a in range(3):
            wide_v[a, :VH] = low[a * VH : (a + 1) * VH]
            wide_v[a, VH + B :] = high[a * VH : (a + 1) * VH]
        wide_p[:PH] = low[3 * VH : 3 * VH + PH]
        wide_p[PH + B :] = high[3 * VH : 3 * VH + PH]
        wide_d[:PH] = low[3 * VH + PH :]
        wide_d[PH + B :] = high[3 * VH + PH :]

    @pl.when(core == 0)
    def _():
        fill(far, near)

    @pl.when(core == 1)
    def _():
        fill(near, far)

    def send(up, down):
        up[...] = wide_v[:, :, B - 4 :, :]
        down[...] = wide_v[:, :, :4, :]
        up[0, 2 : 2 + PX, 0:1, :] = wide_d[:, B - 1 :, :]
        down[0, 2 : 2 + PX, 3:4, :] = wide_d[:, 0:1, :]

    @pl.when(odd == 0)
    def _():
        send(near_y, far_y)

    @pl.when(odd == 1)
    def _():
        send(far_y, near_y)


def advance(place, wide_v, wide_p, wide_d, near, far, star, source, near_y, far_y, v, dr, tau, part):
    odd = place[1] % 2
    v[:, :, 0:B, :] = wide_v[...]
    dr[:, 0:B, :] = wide_d[...]

    def fill(low, high):
        v[:, :, B : B + 4, :] = high[...]
        v[:, :, B + 4 : B + 8, :] = low[...]
        dr[:, B : B + 8, :] = jnp.zeros((PX, 8, 128), F32)
        dr[:, B : B + 1, :] = high[0, 2 : 2 + PX, 3:4, :]
        dr[:, B + 7 : B + 8, :] = low[0, 2 : 2 + PX, 0:1, :]

    @pl.when(odd == 0)
    def _():
        fill(far, near)

    @pl.when(odd == 1)
    def _():
        fill(near, far)

    def zero_shifts(values):
        lane = lane_of(values)
        return (
            jnp.where(lane == 127, 0.0, turn(values, -1, 1)),
            jnp.where(lane == 0, 0.0, turn(values, 1, 1)),
        )

    for i in range(1, VX - 1):
        u = [v[a, i] for a in range(3)]
        gx = [0.5 * (v[a, i + 1] - v[a, i - 1]) for a in range(3)]
        gy = [0.5 * (turn(u[a], -1, 0) - turn(u[a], 1, 0)) for a in range(3)]
        gz = []
        for a in range(3):
            above, below = zero_shifts(u[a])
            gz.append(above - below)
        e01 = gx[1] + gy[0]
        e02 = gx[2] + gz[0]
        e12 = gy[2] + gz[1]
        total = 2.0 * (gx[0] * gx[0] + gy[1] * gy[1] + gz[2] * gz[2]) + (
            e01 * e01 + e02 * e02 + e12 * e12
        )
        visc = EDDY * jnp.sqrt(total)
        tau[0, i] = 2.0 * visc * gx[0]
        tau[1, i] = visc * e01
        tau[2, i] = visc * e02
        if i < 2 or i >= VX - 2:
            continue
        along_y = [visc * e01, 2.0 * visc * gy[1], visc * e12]
        along_z = [visc * e02, visc * e12, 2.0 * visc * gz[2]]
        lane = lane_of(u[0])
        ghost = [jnp.where(lane == 0, u[a], -u[a]) for a in range(3)]
        ghost_visc = EDDY * jnp.sqrt(
            ghost[0] * ghost[0] + ghost[1] * ghost[1] + 2.0 * ghost[2] * ghost[2]
        )
        ghost_tau = [ghost_visc * ghost[0], ghost_visc * ghost[1], 2.0 * ghost_visc * ghost[2]]
        wind = dr[i - 2] * jnp.sqrt(u[0] * u[0] + u[1] * u[1])
        for a in range(3):
            change = 0.5 * (turn(along_y[a], -1, 0) - turn(along_y[a], 1, 0))
            above = jnp.where(lane == 127, ghost_tau[a], turn(along_z[a], -1, 1))
            below = jnp.where(lane == 0, ghost_tau[a], turn(along_z[a], 1, 1))
            change = change + (above - below)
            change = change - (u[0] * gx[a] + u[1] * gy[a] + u[2] * gz[a])
            if a < 2:
                change = change - wind * u[a]
            if a == 0:
                change = change + 1.0
            part[a, i] = u[a] + STEP * change
    for i in range(2, VX - 2):
        for a in range(3):
            part[a, i] = part[a, i] + (0.5 * STEP) * (tau[a, i + 1] - tau[a, i - 1])
    for a in range(3):
        star[a] = part[a, VH : VH + B, 0:B, :]
    for i in range(3, VX - 3):
        along_x = 0.5 * (part[0, i + 1] - part[0, i - 1])
        s1 = part[1, i]
        along_y = 0.5 * (turn(s1, -1, 0) - turn(s1, 1, 0))
        above, below = zero_shifts(part[2, i])
        source[i - 3] = ((along_x + along_y + (above - below)) / STEP)[0:B]

    def send(up, down):
        up[0 : PX - 2] = source[:, B - 8 :, :]
        up[PX - 2 :] = wide_p[:, B - 8 :, :]
        down[0 : PX - 2] = source[:, :8, :]
        down[PX - 2 :] = wide_p[:, :8, :]

    @pl.when(odd == 0)
    def _():
        send(near_y, far_y)

    @pl.when(odd == 1)
    def _():
        send(far_y, near_y)


def neighbours(ref, start, count, dy, dz):
    p = ref[start : start + count]
    lane = lane_of(p)
    below = jnp.where(lane < dz, p, turn(p, dz, 2))
    above = jnp.where(lane >= 128 - dz, p, turn(p, -dz, 2))
    sides = ref[start - 1 : start - 1 + count] + ref[start + 1 : start + 1 + count]
    return p, sides + (turn(p, dy, 1) + turn(p, -dy, 1)) + 4.0 * (below + above)


def chunks(first, last, size=2):
    return [(i, min(size, last - i)) for i in range(first, last, size)]


def sweep(dst, src, right, first, last, dy, dz, offset=0):
    for i, n in chunks(first, last):
        p, around = neighbours(src, i, n, dy, dz)
        dst[i : i + n] = 0.2 * p + COEFF * (around - right[i - offset : i - offset + n])


def scaled_residual(src, right, i, n, dy, dz):
    p, around = neighbours(src, i, n, dy, dz)
    return right[i : i + n] - around + 12.0 * p


def coarsen_pair(pair, dy, dz):
    total = pair[0] + pair[1]
    lane = lane_of(total)
    total = total + jnp.where((lane & dz) == 0, turn(total, -dz, 1), turn(total, dz, 1))
    row = row_of(total)
    total = total + jnp.where((row & dy) == 0, turn(total, -dy, 0), turn(total, dy, 0))
    return 0.5 * total


def presmooth(place, source, wide_p, near, far, finest, right, packed_one, packed_two, p, s, q, f1, a1, b1):
    odd = place[1] % 2
    nx = PX - 2
    p[:, 0:B, :] = wide_p[...]
    s[1 : PX - 1, 0:B, :] = source[...]

    def fill(low, high):
        s[1 : PX - 1, B : B + 8, :] = high[:nx]
        s[1 : PX - 1, B + 8 : B + 16, :] = low[:nx]
        p[:, B : B + 8, :] = high[nx:]
        p[:, B + 8 : B + 16, :] = low[nx:]

    @pl.when(odd == 0)
    def _():
        fill(far, near)

    @pl.when(odd == 1)
    def _():
        fill(near, far)

    sweep(q, p, s, 1, PX - 1, 1, 1)
    sweep(p, q, s, 2, PX - 2, 1, 1)
    finest[...] = p[4 : PX - 4]
    right[...] = s[5 : PX - 5]
    for k in range(12):
        f1[k] = coarsen_pair(scaled_residual(p, s, 3 + 2 * k, 2, 1, 1), 1, 1)
    a1[...] = -COEFF * f1[...]
    sweep(b1, a1, f1, 1, 11, 2, 2)
    f2 = [coarsen_pair(scaled_residual(b1, f1, 2 + 2 * k, 2, 2, 2), 2, 2) for k in range(4)]
    lane = lane_of(f2[0]) & 3
    two = jnp.where(lane == 0, f2[0], jnp.where(lane == 1, f2[1], jnp.where(lane == 2, f2[2], f2[3])))
    for y in range(4):
        packed_two[y : y + 1, :] = two[4 * y : 4 * y + 1, :]
    for g in range(2):
        rows = [f1[2 + 4 * g + j][0:B] for j in range(4)]
        slot = 2 * (row_of(rows[0]) & 1) + (lane_of(rows[0]) & 1)
        packed_one[g] = jnp.where(
            slot == 0, rows[0], jnp.where(slot == 1, rows[1], jnp.where(slot == 2, rows[2], rows[3]))
        )


def pack_y(peers, place, blocks, own, near, far, out):
    core = place[0] % 2
    for j in range(2 * WINDOW + 1):
        piece = blocks[(place[0] + (peers - WINDOW + j)) % peers]
        for k in range(8):
            out[k, 96 + 4 * j : 100 + 4 * j, :] = piece
    for k in range(8):
        out[k, 132:136, :] = jnp.zeros((4, 128), F32)

    def fill(low, high):
        for k in range(8):
            for g in range(2):
                out[k, 16 * g : 16 * g + 16, :] = low[g]
                out[k, 32 + 16 * g : 48 + 16 * g, :] = own[g]
                out[k, 64 + 16 * g : 80 + 16 * g, :] = high[g]

    @pl.when(core == 0)
    def _():
        fill(far, near)

    @pl.when(core == 1)
    def _():
        fill(near, far)


def finish(place, pieces, finest, right, star, velocity_new, pressure_new, z2, f2, a2, b2, f3, a3, b3, f1, a1, b1, e1, p0, q0):
    gy = place[1]
    for j in range(8):
        peer = (gy + j) % 8
        for b in range(9):
            z2[b, 4 * j : 4 * j + 4, :] = pieces[peer, 96 + 4 * b : 100 + 4 * b, :]
    for b in range(9):
        packed = z2[b]
        lane = lane_of(packed) & 3
        for slot in range(4):
            part = jnp.where(lane == slot, packed, 0.0)
            part = part + turn(part, 1 if slot % 2 == 0 else -1, 1)
            part = part + turn(part, 2 if slot < 2 else -2, 1)
            f2[4 * b + slot] = part
            a2[4 * b + slot] = -COEFF * part
    sweep(b2, a2, f2, 1, 35, 1, 4)
    for k in range(2, 16):
        f3[k] = coarsen_pair(scaled_residual(b2, f2, 2 * k, 2, 1, 4), 1, 4)
        a3[k] = -COEFF * f3[k]
    sweep(b3, a3, f3, 3, 15, 2, 8)
    sweep(a3, b3, f3, 4, 14, 2, 8)
    sweep(b3, a3, f3, 5, 13, 2, 8)
    for i in range(6, 12):
        r3 = scaled_residual(b3, f3, i, 1, 2, 8)[0]
        line = jnp.sum(r3, axis=0, keepdims=True) * (COEFF / 32.0)
        fixed = b3[i] - line
        for r in (2 * i, 2 * i + 1):
            a2[r] = b2[r] + fixed
    sweep(b2, a2, f2, 13, 23, 1, 4)
    sweep(a2, b2, f2, 14, 22, 1, 4)
    for place_y, j in ((0, 0), (16, 1), (32, 7)):
        peer = (gy + j) % 8
        for g in range(6):
            packed = pieces[peer, 16 * g : 16 * g + 16, :]
            slots = 2 * (row_of(packed) & 1) + (lane_of(packed) & 1)
            for slot in range(4):
                x = 4 * g + slot
                if x < 3 or x > 20:
                    continue
                part = jnp.where(slots == slot, packed, 0.0)
                part = part + turn(part, 1 if slot % 2 == 0 else -1, 1)
                part = part + turn(part, 1 if slot < 2 else -1, 0)
                f1[x, place_y : place_y + 16, :] = part
                a1[x, place_y : place_y + 16, :] = -COEFF * part
    sweep(b1, a1, f1, 4, 20, 2, 2)
    for q in range(12):
        y = q if q < 8 else q + 20
        e1[:, 4 * q : 4 * q + 4, :] = jnp.broadcast_to(a2[14:22, y : y + 1, :], (8, 4, 128))
    for r in range(4, 20):
        a1[r] = b1[r] + e1[(r - 4) // 2]
    sweep(b1, a1, f1, 5, 19, 2, 2)
    sweep(a1, b1, f1, 6, 18, 2, 2)
    for i in range(22):
        coarse = a1[6 + (i + 1) // 2]
        p0[i, 0:24, :] = finest[i, 0:24, :] + coarse[0:24]
        p0[i, 24:32, :] = finest[i, 24:32, :] + coarse[40:48]
    sweep(q0, p0, right, 1, 21, 1, 1, 1)
    sweep(p0, q0, right, 2, 20, 1, 1, 1)
    for i in range(B):
        p = p0[3 + i]
        lane = lane_of(p)
        above = jnp.where(lane == 127, p, turn(p, -1, 1))
        below = jnp.where(lane == 0, p, turn(p, 1, 1))
        along_x = p0[4 + i] - p0[2 + i]
        along_y = turn(p, -1, 0) - turn(p, 1, 0)
        velocity_new[0, i] = star[0, i] - (0.5 * STEP) * along_x[0:B]
        velocity_new[1, i] = star[1, i] - (0.5 * STEP) * along_y[0:B]
        velocity_new[2, i] = star[2, i] - STEP * (above - below)[0:B]
        pressure_new[i] = p[0:B]


def swaps(count):
    near = [(i, i ^ 1) for i in range(count)]
    far = [(i, (((i + 1) ^ 1) - 1) % count) for i in range(count)]
    return near, far


def exchange(near_block, far_block, axis):
    near, far = swaps(lax.axis_size(axis))
    far_block = lax.ppermute(far_block, axis, far)
    return lax.ppermute(near_block, axis, near), far_block


def per_device(velocity, pressure, land_type, turbine_cells, surface_drag):
    gx = lax.axis_size("gx")
    gy = lax.axis_size("gy")
    place = jnp.stack([lax.axis_index("gx"), lax.axis_index("gy")]).astype(jnp.int32)
    near, far, drag = call(
        pack_x,
        [shape(SIDE, B, 128), shape(SIDE, B, 128), shape(B, B, 128)],
        [SMEM, VMEM, SMEM, VMEM, VMEM, VMEM],
    )(place, land_type, surface_drag, velocity, pressure, turbine_cells)
    near, far = exchange(near, far, "gx")
    wide_v, wide_p, wide_d, near, far = call(
        widen_x,
        [shape(3, VX, B, 128), shape(PX, B, 128), shape(PX, B, 128), shape(3, VX, 4, 128), shape(3, VX, 4, 128)],
        [SMEM] + [VMEM] * 5,
    )(place, velocity, pressure, drag, near, far)
    near, far = exchange(near, far, "gy")
    star, source, near, far = call(
        advance,
        [shape(3, B, B, 128), shape(PX - 2, B, 128), shape(2 * PX - 2, 8, 128), shape(2 * PX - 2, 8, 128)],
        [SMEM] + [VMEM] * 5,
        [(3, VX, 24, 128), (PX, 24, 128), (3, VX, 24, 128), (3, VX, 24, 128)],
    )(place, wide_v, wide_p, wide_d, near, far)
    near, far = exchange(near, far, "gy")
    finest, right, packed_one, packed_two = call(
        presmooth,
        [shape(22, 32, 128), shape(20, 32, 128), shape(2, B, 128), shape(4, 128)],
        [SMEM] + [VMEM] * 4,
        [(PX, 32, 128)] * 3 + [(12, 32, 128)] * 3,
    )(place, source, wide_p, near, far)
    near, far = exchange(packed_one, packed_one, "gx")
    blocks = lax.all_to_all(jnp.broadcast_to(packed_two[None], (gx, 4, 128)), "gx", 0, 0, tiled=True)
    (pieces,) = call(
        lambda *refs: pack_y(gx, *refs), [shape(gy, 136, 128)], [SMEM] + [VMEM] * 4
    )(place, blocks, packed_one, near, far)
    pieces = lax.all_to_all(pieces, "gy", 0, 0, tiled=True)
    velocity_new, pressure_new = call(
        finish,
        [shape(3, B, B, 128), shape(B, B, 128)],
        [SMEM] + [VMEM] * 4,
        [(9, 32, 128)]
        + [(36, 32, 128)] * 3
        + [(18, 32, 128)] * 3
        + [(24, 48, 128)] * 3
        + [(8, 48, 128)]
        + [(22, 32, 128)] * 2,
    )(place, pieces, finest, right, star)
    return velocity_new, pressure_new


def solution(mesh):
    in_specs = (
        P(None, "gx", "gy", None),
        P("gx", "gy", None),
        P("gx", "gy"),
        P("gx", "gy", None),
        P(),
    )
    out_specs = (P(None, "gx", "gy", None), P("gx", "gy", None))
    return jax.shard_map(
        per_device, mesh=mesh, in_specs=in_specs, out_specs=out_specs, check_vma=False
    )
```

```python
import jax
import jax.numpy as jnp
from jax import lax
from jax.experimental import pallas as pl
from jax.experimental.pallas import tpu as pltpu
from jax.sharding import PartitionSpec as P

VH = 9
PH = 7
B = 16
VX = B + 2 * VH
PX = B + 2 * PH
SIDE = 3 * VH + 2 * PH
STEP = 0.1
EDDY = 0.03
COEFF = 0.8 / 12.0
WINDOW = 4
VMEM = pl.BlockSpec(memory_space=pltpu.VMEM)
SMEM = pl.BlockSpec(memory_space=pltpu.SMEM)
ANY = pl.BlockSpec(memory_space=pl.ANY)
UNITS = (
    (0, 0, 5, 18, True),
    (18, 0, 5, 18, False),
    (36, 0, 1, 4, False),
    (40, 0, 23, 4, False),
    (44, 1, 5, 20, True),
    (64, 1, 5, 20, False),
    (84, 1, 1, 4, False),
    (88, 1, 25, 4, False),
)
N_UNITS = 92
F32 = jnp.float32


def shape(*dims):
    return jax.ShapeDtypeStruct(dims, F32)


def call(body, outs, specs, scratch=()):
    return pl.pallas_call(
        body,
        out_shape=outs,
        in_specs=specs,
        out_specs=[VMEM] * len(outs),
        scratch_shapes=[pltpu.VMEM(s, F32) if isinstance(s, tuple) else s for s in scratch],
        compiler_params=pltpu.CompilerParams(vmem_limit_bytes=48 * 1024 * 1024),
    )


def iota(like, dim):
    return lax.broadcasted_iota(jnp.int32, like.shape, dim)


def lane_of(values):
    return iota(values, values.ndim - 1)


def row_of(values):
    return iota(values, values.ndim - 2)


def turn(values, amount, dim):
    return pltpu.roll(values, amount % values.shape[dim], dim)


def pack_x(place, drag_table, land, velocity, pressure, turbine, near, far, drag, kinds_ref, cells_ref, sems):
    core = place[0] % 2
    copies = [
        pltpu.make_async_copy(land, kinds_ref, sems.at[0]),
        pltpu.make_async_copy(turbine, cells_ref, sems.at[1]),
    ]
    for side, out in ((0, near), (1, far)):
        high = (core + side) % 2 == 0
        start = jnp.where(high, B - VH, 0)
        for a in range(3):
            copies.append(
                pltpu.make_async_copy(
                    velocity.at[a, pl.ds(start, VH)], out.at[pl.ds(a * VH, VH)], sems.at[2 + 4 * side + a]
                )
            )
        start = jnp.where(high, B - PH, 0)
        copies.append(
            pltpu.make_async_copy(
                pressure.at[pl.ds(start, PH)], out.at[pl.ds(3 * VH, PH)], sems.at[5 + 4 * side]
            )
        )
    for copy in copies:
        copy.start()
    copies[0].wait()
    kinds = kinds_ref[...]
    ground = jnp.zeros(kinds.shape, F32)
    for kind in range(16):
        ground = jnp.where(kinds == kind, drag_table[kind], ground)
    square = lax.broadcasted_iota(jnp.int32, (B, B), 0) == lax.broadcasted_iota(jnp.int32, (B, B), 1)
    copies[1].wait()
    for i in range(B):
        row = jnp.broadcast_to(ground[i : i + 1, :], (B, B))
        column = jnp.sum(jnp.where(square, row, 0.0), axis=1, keepdims=True)
        cells = cells_ref[i].astype(F32)
        drag[i] = 2.0 * cells + jnp.where(lane_of(cells) == 0, column, 0.0)

    @pl.when(core == 0)
    def _():
        near[3 * VH + PH : SIDE] = drag[B - PH :]
        far[3 * VH + PH : SIDE] = drag[:PH]

    @pl.when(core == 1)
    def _():
        near[3 * VH + PH : SIDE] = drag[:PH]
        far[3 * VH + PH : SIDE] = drag[B - PH :]

    for copy in copies[2:]:
        copy.wait()


def widen_x(place, velocity, pressure, drag, near, far, wide_v, wide_p, wide_d, near_y, far_y):
    core = place[0] % 2
    odd = place[1] % 2
    for a in range(3):
        wide_v[a, VH : VH + B] = velocity[a]
    wide_p[PH : PH + B] = pressure[...]
    wide_d[PH : PH + B] = drag[...]

    def fill(low, high):
        for a in range(3):
            wide_v[a, :VH] = low[a * VH : (a + 1) * VH]
            wide_v[a, VH + B :] = high[a * VH : (a + 1) * VH]
        wide_p[:PH] = low[3 * VH : 3 * VH + PH]
        wide_p[PH + B :] = high[3 * VH : 3 * VH + PH]
        wide_d[:PH] = low[3 * VH + PH :]
        wide_d[PH + B :] = high[3 * VH + PH :]

    @pl.when(core == 0)
    def _():
        fill(far, near)

    @pl.when(core == 1)
    def _():
        fill(near, far)

    def send(up, down):
        for g in range(8):
            for j in range(4):
                x = 1 + 4 * g + j
                for a in range(3):
                    rows = slice(10 * j + 3 * a, 10 * j + 3 * a + 3)
                    up[g, rows, :] = wide_v[a, x, B - 3 :, :]
                    down[g, rows, :] = wide_v[a, x, :3, :]
                row = slice(10 * j + 9, 10 * j + 10)
                d = min(max(x - 2, 0), PX - 1)
                up[g, row, :] = wide_d[d, B - 1 :, :]
                down[g, row, :] = wide_d[d, 0:1, :]

    @pl.when(odd == 0)
    def _():
        send(near_y, far_y)

    @pl.when(odd == 1)
    def _():
        send(far_y, near_y)


def advance(place, wide_v, wide_p, wide_d, near, far, star, source, near_y, far_y, v, dr, tau, part):
    odd = place[1] % 2
    v[:, :, 0:B, :] = wide_v[...]
    dr[:, 0:B, :] = wide_d[...]

    def fill(low, high):
        for g in range(8):
            for j in range(4):
                x = 1 + 4 * g + j
                for a in range(3):
                    rows = slice(10 * j + 3 * a, 10 * j + 3 * a + 3)
                    v[a, x, B : B + 3, :] = high[g, rows, :]
                    v[a, x, B + 5 : B + 8, :] = low[g, rows, :]
                if 2 <= x < 2 + PX:
                    row = slice(10 * j + 9, 10 * j + 10)
                    dr[x - 2, B : B + 1, :] = high[g, row, :]
                    dr[x - 2, B + 7 : B + 8, :] = low[g, row, :]

    @pl.when(odd == 0)
    def _():
        fill(far, near)

    @pl.when(odd == 1)
    def _():
        fill(near, far)

    def zero_shifts(values):
        lane = lane_of(values)
        return (
            jnp.where(lane == 127, 0.0, turn(values, -1, 1)),
            jnp.where(lane == 0, 0.0, turn(values, 1, 1)),
        )

    for i in range(1, VX - 1):
        u = [v[a, i] for a in range(3)]
        gx = [0.5 * (v[a, i + 1] - v[a, i - 1]) for a in range(3)]
        gy = [0.5 * (turn(u[a], -1, 0) - turn(u[a], 1, 0)) for a in range(3)]
        gz = []
        for a in range(3):
            above, below = zero_shifts(u[a])
            gz.append(above - below)
        e01 = gx[1] + gy[0]
        e02 = gx[2] + gz[0]
        e12 = gy[2] + gz[1]
        total = 2.0 * (gx[0] * gx[0] + gy[1] * gy[1] + gz[2] * gz[2]) + (
            e01 * e01 + e02 * e02 + e12 * e12
        )
        visc = EDDY * jnp.sqrt(total)
        tau[0, i] = 2.0 * visc * gx[0]
        tau[1, i] = visc * e01
        tau[2, i] = visc * e02
        if i < 2 or i >= VX - 2:
            continue
        along_y = [visc * e01, 2.0 * visc * gy[1], visc * e12]
        along_z = [visc * e02, visc * e12, 2.0 * visc * gz[2]]
        lane = lane_of(u[0])
        ghost = [jnp.where(lane == 0, u[a], -u[a]) for a in range(3)]
        ghost_visc = EDDY * jnp.sqrt(
            ghost[0] * ghost[0] + ghost[1] * ghost[1] + 2.0 * ghost[2] * ghost[2]
        )
        ghost_tau = [ghost_visc * ghost[0], ghost_visc * ghost[1], 2.0 * ghost_visc * ghost[2]]
        wind = dr[i - 2] * jnp.sqrt(u[0] * u[0] + u[1] * u[1])
        for a in range(3):
            change = 0.5 * (turn(along_y[a], -1, 0) - turn(along_y[a], 1, 0))
            above = jnp.where(lane == 127, ghost_tau[a], turn(along_z[a], -1, 1))
            below = jnp.where(lane == 0, ghost_tau[a], turn(along_z[a], 1, 1))
            change = change + (above - below)
            change = change - (u[0] * gx[a] + u[1] * gy[a] + u[2] * gz[a])
            if a < 2:
                change = change - wind * u[a]
            if a == 0:
                change = change + 1.0
            part[a, i] = u[a] + STEP * change
    for i in range(2, VX - 2):
        for a in range(3):
            part[a, i] = part[a, i] + (0.5 * STEP) * (tau[a, i + 1] - tau[a, i - 1])
    for a in range(3):
        star[a] = part[a, VH : VH + B, 0:B, :]
    for i in range(3, VX - 3):
        along_x = 0.5 * (part[0, i + 1] - part[0, i - 1])
        s1 = part[1, i]
        along_y = 0.5 * (turn(s1, -1, 0) - turn(s1, 1, 0))
        above, below = zero_shifts(part[2, i])
        source[i - 3] = ((along_x + along_y + (above - below)) / STEP)[0:B]

    def send(up, down):
        for message, outer, inner in ((up, B - 4, B - 8), (down, 0, 4)):
            for unit, kind, start, count, deep in UNITS:
                field = source if kind == 0 else wide_p
                first = inner if deep else outer
                message[unit : unit + count] = field[start : start + count, first : first + 4, :]

    @pl.when(odd == 0)
    def _():
        send(near_y, far_y)

    @pl.when(odd == 1)
    def _():
        send(far_y, near_y)


def neighbours(ref, start, count, dy, dz):
    p = ref[start : start + count]
    lane = lane_of(p)
    below = jnp.where(lane < dz, p, turn(p, dz, 2))
    above = jnp.where(lane >= 128 - dz, p, turn(p, -dz, 2))
    sides = ref[start - 1 : start - 1 + count] + ref[start + 1 : start + 1 + count]
    return p, sides + (turn(p, dy, 1) + turn(p, -dy, 1)) + 4.0 * (below + above)


def chunks(first, last, size=2):
    return [(i, min(size, last - i)) for i in range(first, last, size)]


def sweep(dst, src, right, first, last, dy, dz, offset=0):
    for i, n in chunks(first, last):
        p, around = neighbours(src, i, n, dy, dz)
        dst[i : i + n] = 0.2 * p + COEFF * (around - right[i - offset : i - offset + n])


def scaled_residual(src, right, i, n, dy, dz):
    p, around = neighbours(src, i, n, dy, dz)
    return right[i : i + n] - around + 12.0 * p


def coarsen_pair(pair, dy, dz):
    total = pair[0] + pair[1]
    lane = lane_of(total)
    total = total + jnp.where((lane & dz) == 0, turn(total, -dz, 1), turn(total, dz, 1))
    row = row_of(total)
    total = total + jnp.where((row & dy) == 0, turn(total, -dy, 0), turn(total, dy, 0))
    return 0.5 * total


def presmooth(place, source, wide_p, near, far, finest, right, packed_one, packed_two, p, s, q, f1, a1, b1):
    odd = place[1] % 2
    p[:, 0:B, :] = wide_p[...]
    s[1 : PX - 1, 0:B, :] = source[...]

    def fill(low, high):
        for unit, kind, start, count, deep in UNITS:
            field = s if kind == 0 else p
            rows = slice(start + 1 - kind, start + 1 - kind + count)
            first = B + 4 if deep else B
            field[rows, first : first + 4, :] = high[unit : unit + count]
            first = B + 8 if deep else B + 12
            field[rows, first : first + 4, :] = low[unit : unit + count]

    @pl.when(odd == 0)
    def _():
        fill(far, near)

    @pl.when(odd == 1)
    def _():
        fill(near, far)

    sweep(q, p, s, 1, PX - 1, 1, 1)
    sweep(p, q, s, 2, PX - 2, 1, 1)
    for out, field, first in ((finest, p, 4), (right, s, 5)):
        out[:, 0:B, :] = field[first : PX - first, 0:B, :]
        out[:, B : B + 4, :] = field[first : PX - first, B : B + 4, :]
        out[:, B + 4 : B + 8, :] = field[first : PX - first, B + 12 : B + 16, :]
    for k in range(12):
        f1[k] = coarsen_pair(scaled_residual(p, s, 3 + 2 * k, 2, 1, 1), 1, 1)
    a1[...] = -COEFF * f1[...]
    sweep(b1, a1, f1, 1, 11, 2, 2)
    f2 = [coarsen_pair(scaled_residual(b1, f1, 2 + 2 * k, 2, 2, 2), 2, 2) for k in range(4)]
    lane = lane_of(f2[0]) & 3
    two = jnp.where(lane == 0, f2[0], jnp.where(lane == 1, f2[1], jnp.where(lane == 2, f2[2], f2[3])))
    four = jnp.concatenate([two[4 * y : 4 * y + 1, :] for y in range(4)], axis=0)
    for k in range(packed_two.shape[0]):
        packed_two[k] = four
    for g in range(2):
        rows = [f1[2 + 4 * g + j][0:B] for j in range(4)]
        slot = 2 * (row_of(rows[0]) & 1) + (lane_of(rows[0]) & 1)
        packed_one[g] = jnp.where(
            slot == 0, rows[0], jnp.where(slot == 1, rows[1], jnp.where(slot == 2, rows[2], rows[3]))
        )


def pack_y(peers, place, blocks, own, near, far, strips, window, near_y, far_y):
    core = place[0] % 2
    odd = place[1] % 2
    for j in range(2 * WINDOW + 1):
        piece = blocks[(place[0] + (peers - WINDOW + j)) % peers]
        for k in range(8):
            strips[k, j] = piece
    window[2:4] = own[...]

    def fill(low, high):
        window[0:2] = low[...]
        window[4:6] = high[...]

    @pl.when(core == 0)
    def _():
        fill(far, near)

    @pl.when(core == 1)
    def _():
        fill(near, far)

    def send(up, down):
        up[...] = window[:, 4:16, :]
        down[...] = window[:, 0:12, :]

    @pl.when(odd == 0)
    def _():
        send(near_y, far_y)

    @pl.when(odd == 1)
    def _():
        send(far_y, near_y)


def packed_neighbours(ref, b, dx, dy, dz):
    p = ref[b]
    before = ref[max(b - 1, 0)]
    after = ref[min(b + 1, 2 * WINDOW)]
    lane = lane_of(p)
    slot = lane & 3
    left = jnp.where(slot < dx, turn(before, dx - 4, 1), turn(p, dx, 1))
    right = jnp.where(slot >= 4 - dx, turn(after, 4 - dx, 1), turn(p, -dx, 1))
    below = jnp.where(lane < dz, p, turn(p, dz, 1))
    above = jnp.where(lane >= 128 - dz, p, turn(p, -dz, 1))
    return p, (left + right) + (turn(p, dy, 0) + turn(p, -dy, 0)) + 4.0 * (below + above)


def packed_sweep(dst, src, right, blocks, dx, dy, dz):
    for b in blocks:
        p, around = packed_neighbours(src, b, dx, dy, dz)
        dst[b] = 0.2 * p + COEFF * (around - right[b])


def packed_residual(src, right, b, dx, dy, dz):
    p, around = packed_neighbours(src, b, dx, dy, dz)
    return right[b] - around + 12.0 * p


def without_middle(values):
    return jnp.concatenate([values[..., 0:24, :], values[..., 32:40, :]], axis=-2)


def finish(place, strips, window, near, far, finest, right, star, velocity_new, pressure_new, f2, a2, b2, f3, a3, b3, g1, f1, a1, b1, c1, d1, e1, p0, q0):
    gy = place[1]
    odd = gy % 2
    for j in range(8):
        peer = (gy + j) % 8
        for b in range(2 * WINDOW + 1):
            f2[b, 4 * j : 4 * j + 4, :] = strips[peer, b]
    for b in range(9):
        a2[b] = -COEFF * f2[b]
    packed_sweep(b2, a2, f2, range(9), 1, 1, 4)
    for b in range(1, 8):
        total = packed_residual(b2, f2, b, 1, 1, 4)
        lane = lane_of(total)
        total = total + jnp.where((lane & 1) == 0, turn(total, -1, 1), turn(total, 1, 1))
        total = total + jnp.where((lane & 4) == 0, turn(total, -4, 1), turn(total, 4, 1))
        row = row_of(total)
        total = total + jnp.where((row & 1) == 0, turn(total, -1, 0), turn(total, 1, 0))
        f3[b] = 0.5 * total
        a3[b] = (-0.5 * COEFF) * total
    packed_sweep(b3, a3, f3, range(1, 8), 2, 2, 8)
    packed_sweep(a3, b3, f3, range(2, 7), 2, 2, 8)
    packed_sweep(b3, a3, f3, range(2, 7), 2, 2, 8)
    for b in range(3, 6):
        line = jnp.sum(packed_residual(b3, f3, b, 2, 2, 8), axis=0, keepdims=True) * (COEFF / 32.0)
        a2[b] = b2[b] + (b3[b] - line)
    packed_sweep(b2, a2, f2, range(3, 6), 1, 1, 4)
    packed_sweep(a2, b2, f2, range(3, 6), 1, 1, 4)
    g1[:, 0:B, :] = window[...]

    def fill(low, high):
        g1[:, B : B + 12, :] = high[...]
        g1[:, B + 12 : B + 24, :] = low[...]

    @pl.when(odd == 0)
    def _():
        fill(far, near)

    @pl.when(odd == 1)
    def _():
        fill(near, far)

    for x in range(3, 21):
        packed = g1[x // 4]
        slots = 2 * (row_of(packed) & 1) + (lane_of(packed) & 1)
        slot = x % 4
        part = jnp.where(slots == slot, packed, 0.0)
        part = part + turn(part, 1 if slot % 2 == 0 else -1, 1)
        part = part + turn(part, 1 if slot < 2 else -1, 0)
        f1[x] = part
        a1[x] = -COEFF * part
    sweep(b1, a1, f1, 4, 20, 2, 2)
    for k in range(8):
        block = a2[3 + (k + 2) // 4]
        slot = (k + 2) % 4
        low, high = block[0:8], block[24:32]
        part = jnp.where(row_of(low) < 6, low, high)
        part = jnp.where((lane_of(part) & 3) == slot, part, 0.0)
        part = part + turn(part, 1 if slot % 2 == 0 else -1, 1)
        part = part + turn(part, 2 if slot < 2 else -2, 1)
        for q in range(8):
            e1[k, 4 * q : 4 * q + 4, :] = jnp.broadcast_to(part[q : q + 1, :], (4, 128))
    for r in range(4, 20):
        c1[r] = without_middle(b1[r]) + e1[(r - 4) // 2]
    for dst, src, first, last in ((d1, c1, 5, 19), (c1, d1, 6, 18)):
        for i, n in chunks(first, last):
            p, around = neighbours(src, i, n, 2, 2)
            dst[i : i + n] = 0.2 * p + COEFF * (around - without_middle(f1[i : i + n]))
    for i in range(22):
        coarse = c1[6 + (i + 1) // 2]
        edge = coarse[16:24]
        p0[i, 0:B, :] = finest[i, 0:B, :] + coarse[0:B]
        p0[i, B:, :] = finest[i, B:, :] + jnp.where(row_of(edge) < 4, edge, coarse[24:32])
    sweep(q0, p0, right, 1, 21, 1, 1, 1)
    sweep(p0, q0, right, 2, 20, 1, 1, 1)
    for i in range(B):
        p = p0[3 + i]
        lane = lane_of(p)
        above = jnp.where(lane == 127, p, turn(p, -1, 1))
        below = jnp.where(lane == 0, p, turn(p, 1, 1))
        along_x = p0[4 + i] - p0[2 + i]
        along_y = turn(p, -1, 0) - turn(p, 1, 0)
        velocity_new[0, i] = star[0, i] - (0.5 * STEP) * along_x[0:B]
        velocity_new[1, i] = star[1, i] - (0.5 * STEP) * along_y[0:B]
        velocity_new[2, i] = star[2, i] - STEP * (above - below)[0:B]
        pressure_new[i] = p[0:B]


def swaps(count):
    near = [(i, i ^ 1) for i in range(count)]
    far = [(i, (((i + 1) ^ 1) - 1) % count) for i in range(count)]
    return near, far


def exchange(near_block, far_block, axis):
    near, far = swaps(lax.axis_size(axis))
    far_block = lax.ppermute(far_block, axis, far)
    return lax.ppermute(near_block, axis, near), far_block


def per_device(velocity, pressure, land_type, turbine_cells, surface_drag):
    gx = lax.axis_size("gx")
    gy = lax.axis_size("gy")
    place = jnp.stack([lax.axis_index("gx"), lax.axis_index("gy")]).astype(jnp.int32)
    near, far, drag = call(
        pack_x,
        [shape(SIDE, B, 128), shape(SIDE, B, 128), shape(B, B, 128)],
        [SMEM, SMEM] + [ANY] * 4,
        [pltpu.VMEM((B, B), jnp.int32), pltpu.VMEM((B, B, 128), jnp.int32), pltpu.SemaphoreType.DMA((10,))],
    )(place, surface_drag, land_type, velocity, pressure, turbine_cells)
    near, far = exchange(near, far, "gx")
    wide_v, wide_p, wide_d, near, far = call(
        widen_x,
        [shape(3, VX, B, 128), shape(PX, B, 128), shape(PX, B, 128), shape(8, 40, 128), shape(8, 40, 128)],
        [SMEM] + [VMEM] * 5,
    )(place, velocity, pressure, drag, near, far)
    near, far = exchange(near, far, "gy")
    star, source, near, far = call(
        advance,
        [shape(3, B, B, 128), shape(PX - 2, B, 128), shape(N_UNITS, 4, 128), shape(N_UNITS, 4, 128)],
        [SMEM] + [VMEM] * 5,
        [(3, VX, 24, 128), (PX, 24, 128), (3, VX, 24, 128), (3, VX, 24, 128)],
    )(place, wide_v, wide_p, wide_d, near, far)
    near, far = exchange(near, far, "gy")
    finest, right, packed_one, packed_two = call(
        presmooth,
        [shape(22, 24, 128), shape(20, 24, 128), shape(2, B, 128), shape(gx, 4, 128)],
        [SMEM] + [VMEM] * 4,
        [(PX, 32, 128)] * 3 + [(12, 32, 128)] * 3,
    )(place, source, wide_p, near, far)
    near, far = exchange(packed_one, packed_one, "gx")
    blocks = lax.all_to_all(packed_two, "gx", 0, 0, tiled=True)
    strips, window, near, far = call(
        lambda *refs: pack_y(gx, *refs),
        [shape(gy, 9, 4, 128), shape(6, B, 128), shape(6, 12, 128), shape(6, 12, 128)],
        [SMEM] + [VMEM] * 4,
    )(place, blocks, packed_one, near, far)
    strips = lax.all_to_all(strips, "gy", 0, 0, tiled=True)
    near, far = exchange(near, far, "gy")
    velocity_new, pressure_new = call(
        finish,
        [shape(3, B, B, 128), shape(B, B, 128)],
        [SMEM] + [VMEM] * 7,
        [(9, 32, 128)] * 6
        + [(6, 40, 128)]
        + [(24, 40, 128)] * 3
        + [(24, 32, 128)] * 2
        + [(8, 32, 128)]
        + [(22, 24, 128)] * 2,
    )(place, strips, window, near, far, finest, right, star)
    return velocity_new, pressure_new


def solution(mesh):
    in_specs = (
        P(None, "gx", "gy", None),
        P("gx", "gy", None),
        P("gx", "gy"),
        P("gx", "gy", None),
        P(),
    )
    out_specs = (P(None, "gx", "gy", None), P("gx", "gy", None))
    return jax.shard_map(
        per_device, mesh=mesh, in_specs=in_specs, out_specs=out_specs, check_vma=False
    )
```

```python
import jax
import jax.numpy as jnp
from jax import lax
from jax.experimental import pallas as pl
from jax.experimental.pallas import tpu as pltpu
from jax.sharding import PartitionSpec as P

VH = 9
PH = 7
B = 16
VX = B + 2 * VH
PX = B + 2 * PH
SIDE = 3 * VH + 2 * PH
STEP = 0.1
EDDY = 0.03
COEFF = 0.8 / 12.0
WINDOW = 4
VMEM = pl.BlockSpec(memory_space=pltpu.VMEM)
SMEM = pl.BlockSpec(memory_space=pltpu.SMEM)
HBM = pl.BlockSpec(memory_space=pltpu.HBM)
UNITS = (
    (0, 0, 5, 18, True),
    (18, 0, 5, 18, False),
    (36, 0, 1, 4, False),
    (40, 0, 23, 4, False),
    (44, 1, 5, 20, True),
    (64, 1, 5, 20, False),
    (84, 1, 1, 4, False),
    (88, 1, 25, 4, False),
)
N_UNITS = 92
F32 = jnp.float32


def shape(*dims):
    return jax.ShapeDtypeStruct(dims, F32)


def call(body, outs, specs, scratch=()):
    return pl.pallas_call(
        body,
        out_shape=outs,
        in_specs=specs,
        out_specs=[VMEM] * len(outs),
        scratch_shapes=[pltpu.VMEM(s, F32) if isinstance(s, tuple) else s for s in scratch],
        compiler_params=pltpu.CompilerParams(vmem_limit_bytes=48 * 1024 * 1024),
    )


def iota(like, dim):
    return lax.broadcasted_iota(jnp.int32, like.shape, dim)


def lane_of(values):
    return iota(values, values.ndim - 1)


def row_of(values):
    return iota(values, values.ndim - 2)


def turn(values, amount, dim):
    return pltpu.roll(values, amount % values.shape[dim], dim)


def pack_x(place, drag_table, land, velocity, pressure, turbine, near, far, drag, kinds_ref, cells_ref, sems):
    core = place[0] % 2
    copies = [
        pltpu.make_async_copy(land, kinds_ref, sems.at[0]),
        pltpu.make_async_copy(turbine, cells_ref, sems.at[1]),
    ]
    for side, out in ((0, near), (1, far)):
        high = (core + side) % 2 == 0
        start = jnp.where(high, B - VH, 0)
        for a in range(3):
            copies.append(
                pltpu.make_async_copy(
                    velocity.at[a, pl.ds(start, VH)], out.at[pl.ds(a * VH, VH)], sems.at[2 + 4 * side + a]
                )
            )
        start = jnp.where(high, B - PH, 0)
        copies.append(
            pltpu.make_async_copy(
                pressure.at[pl.ds(start, PH)], out.at[pl.ds(3 * VH, PH)], sems.at[5 + 4 * side]
            )
        )
    for copy in copies:
        copy.start()
    copies[0].wait()
    kinds = kinds_ref[...]
    ground = jnp.zeros(kinds.shape, F32)
    for kind in range(16):
        ground = jnp.where(kinds == kind, drag_table[kind], ground)
    square = lax.broadcasted_iota(jnp.int32, (B, B), 0) == lax.broadcasted_iota(jnp.int32, (B, B), 1)
    copies[1].wait()
    for i in range(B):
        row = jnp.broadcast_to(ground[i : i + 1, :], (B, B))
        column = jnp.sum(jnp.where(square, row, 0.0), axis=1, keepdims=True)
        cells = cells_ref[i].astype(F32)
        drag[i] = 2.0 * cells + jnp.where(lane_of(cells) == 0, column, 0.0)

    @pl.when(core == 0)
    def _():
        near[3 * VH + PH : SIDE] = drag[B - PH :]
        far[3 * VH + PH : SIDE] = drag[:PH]

    @pl.when(core == 1)
    def _():
        near[3 * VH + PH : SIDE] = drag[:PH]
        far[3 * VH + PH : SIDE] = drag[B - PH :]

    for copy in copies[2:]:
        copy.wait()


def widen_x(place, velocity, pressure, drag, near, far, wide_v, wide_p, wide_d, near_y, far_y):
    core = place[0] % 2
    odd = place[1] % 2
    for a in range(3):
        wide_v[a, VH : VH + B] = velocity[a]
    wide_p[PH : PH + B] = pressure[...]
    wide_d[PH : PH + B] = drag[...]

    def fill(low, high):
        for a in range(3):
            wide_v[a, :VH] = low[a * VH : (a + 1) * VH]
            wide_v[a, VH + B :] = high[a * VH : (a + 1) * VH]
        wide_p[:PH] = low[3 * VH : 3 * VH + PH]
        wide_p[PH + B :] = high[3 * VH : 3 * VH + PH]
        wide_d[:PH] = low[3 * VH + PH :]
        wide_d[PH + B :] = high[3 * VH + PH :]

    @pl.when(core == 0)
    def _():
        fill(far, near)

    @pl.when(core == 1)
    def _():
        fill(near, far)

    def send(up, down):
        for g in range(8):
            for j in range(4):
                x = 1 + 4 * g + j
                for a in range(3):
                    rows = slice(10 * j + 3 * a, 10 * j + 3 * a + 3)
                    up[g, rows, :] = wide_v[a, x, B - 3 :, :]
                    down[g, rows, :] = wide_v[a, x, :3, :]
                row = slice(10 * j + 9, 10 * j + 10)
                d = min(max(x - 2, 0), PX - 1)
                up[g, row, :] = wide_d[d, B - 1 :, :]
                down[g, row, :] = wide_d[d, 0:1, :]

    @pl.when(odd == 0)
    def _():
        send(near_y, far_y)

    @pl.when(odd == 1)
    def _():
        send(far_y, near_y)


def advance(place, wide_v, wide_p, wide_d, near, far, star, source, near_y, far_y, v, dr, tau, part):
    odd = place[1] % 2
    v[:, :, 0:B, :] = wide_v[...]
    dr[:, 0:B, :] = wide_d[...]

    def fill(low, high):
        for g in range(8):
            for j in range(4):
                x = 1 + 4 * g + j
                for a in range(3):
                    rows = slice(10 * j + 3 * a, 10 * j + 3 * a + 3)
                    v[a, x, B : B + 3, :] = high[g, rows, :]
                    v[a, x, B + 5 : B + 8, :] = low[g, rows, :]
                if 2 <= x < 2 + PX:
                    row = slice(10 * j + 9, 10 * j + 10)
                    dr[x - 2, B : B + 1, :] = high[g, row, :]
                    dr[x - 2, B + 7 : B + 8, :] = low[g, row, :]

    @pl.when(odd == 0)
    def _():
        fill(far, near)

    @pl.when(odd == 1)
    def _():
        fill(near, far)

    def zero_shifts(values):
        lane = lane_of(values)
        return (
            jnp.where(lane == 127, 0.0, turn(values, -1, 1)),
            jnp.where(lane == 0, 0.0, turn(values, 1, 1)),
        )

    for i in range(1, VX - 1):
        u = [v[a, i] for a in range(3)]
        gx = [0.5 * (v[a, i + 1] - v[a, i - 1]) for a in range(3)]
        gy = [0.5 * (turn(u[a], -1, 0) - turn(u[a], 1, 0)) for a in range(3)]
        gz = []
        for a in range(3):
            above, below = zero_shifts(u[a])
            gz.append(above - below)
        e01 = gx[1] + gy[0]
        e02 = gx[2] + gz[0]
        e12 = gy[2] + gz[1]
        total = 2.0 * (gx[0] * gx[0] + gy[1] * gy[1] + gz[2] * gz[2]) + (
            e01 * e01 + e02 * e02 + e12 * e12
        )
        visc = EDDY * jnp.sqrt(total)
        tau[0, i] = 2.0 * visc * gx[0]
        tau[1, i] = visc * e01
        tau[2, i] = visc * e02
        if i < 2 or i >= VX - 2:
            continue
        along_y = [visc * e01, 2.0 * visc * gy[1], visc * e12]
        along_z = [visc * e02, visc * e12, 2.0 * visc * gz[2]]
        lane = lane_of(u[0])
        flat = u[0] * u[0] + u[1] * u[1]
        edge = jnp.where((lane == 0) | (lane == 127), EDDY * jnp.sqrt(flat + 2.0 * (u[2] * u[2])), 0.0)
        wind = dr[i - 2] * jnp.sqrt(flat)
        for a in range(3):
            change = 0.5 * (turn(along_y[a], -1, 0) - turn(along_y[a], 1, 0))
            above, below = zero_shifts(along_z[a])
            change = change + ((above - below) - (edge * u[a] if a < 2 else 2.0 * (edge * u[a])))
            change = change - (u[0] * gx[a] + u[1] * gy[a] + u[2] * gz[a])
            if a < 2:
                change = change - wind * u[a]
            if a == 0:
                change = change + 1.0
            part[a, i] = u[a] + STEP * change
    for i in range(2, VX - 2):
        for a in range(3):
            part[a, i] = part[a, i] + (0.5 * STEP) * (tau[a, i + 1] - tau[a, i - 1])
    for a in range(3):
        star[a] = part[a, VH : VH + B, 0:B, :]
    for i in range(3, VX - 3):
        along_x = 0.5 * (part[0, i + 1] - part[0, i - 1])
        s1 = part[1, i]
        along_y = 0.5 * (turn(s1, -1, 0) - turn(s1, 1, 0))
        above, below = zero_shifts(part[2, i])
        source[i - 3] = ((along_x + along_y + (above - below)) / STEP)[0:B]

    def send(up, down):
        for message, outer, inner in ((up, B - 4, B - 8), (down, 0, 4)):
            for unit, kind, start, count, deep in UNITS:
                field = source if kind == 0 else wide_p
                first = inner if deep else outer
                message[unit : unit + count] = field[start : start + count, first : first + 4, :]

    @pl.when(odd == 0)
    def _():
        send(near_y, far_y)

    @pl.when(odd == 1)
    def _():
        send(far_y, near_y)


def column_sum(dz, halves):
    i = lax.broadcasted_iota(jnp.int32, (128, 128), 0)
    j = lax.broadcasted_iota(jnp.int32, (128, 128), 1)
    hit = (i - j == dz) | (j - i == dz) | ((i == j) & ((j < dz) | (j >= 128 - dz)))
    return jnp.concatenate([jnp.where(hit, 4.0, 0.0).astype(jnp.bfloat16)] * halves, axis=0)


def exact_product(values, matrix):
    flat = values.reshape(-1, 128)
    high = flat.astype(jnp.bfloat16)
    rest = flat - high.astype(F32)
    middle = rest.astype(jnp.bfloat16)
    low = (rest - middle.astype(F32)).astype(jnp.bfloat16)
    parts = jnp.concatenate([high, middle, low], axis=1)
    return jnp.dot(parts, matrix, preferred_element_type=F32).reshape(values.shape)


def neighbours(ref, start, count, dy, dz, matrix=None):
    p = ref[start : start + count]
    sides = ref[start - 1 : start - 1 + count] + ref[start + 1 : start + 1 + count]
    sides = sides + (turn(p, dy, 1) + turn(p, -dy, 1))
    if matrix is not None:
        return p, sides + exact_product(p, matrix)
    lane = lane_of(p)
    below = jnp.where(lane < dz, p, turn(p, dz, 2))
    above = jnp.where(lane >= 128 - dz, p, turn(p, -dz, 2))
    return p, sides + 4.0 * (below + above)


def chunks(first, last, size=2):
    return [(i, min(size, last - i)) for i in range(first, last, size)]


def sweep(dst, src, right, first, last, dy, dz, offset=0, matrix=None):
    for i, n in chunks(first, last, 2 if matrix is None else 4):
        p, around = neighbours(src, i, n, dy, dz, matrix)
        dst[i : i + n] = 0.2 * p + COEFF * (around - right[i - offset : i - offset + n])


def scaled_residual(src, right, i, n, dy, dz, matrix=None):
    p, around = neighbours(src, i, n, dy, dz, matrix)
    return right[i : i + n] - around + 12.0 * p


def coarsen_pair(pair, dy, dz):
    total = pair[0] + pair[1]
    lane = lane_of(total)
    total = total + jnp.where((lane & dz) == 0, turn(total, -dz, 1), turn(total, dz, 1))
    row = row_of(total)
    total = total + jnp.where((row & dy) == 0, turn(total, -dy, 0), turn(total, dy, 0))
    return 0.5 * total


def presmooth(place, source, wide_p, near, far, finest, right, packed_one, packed_two, p, s, q, f1, a1, b1):
    odd = place[1] % 2
    p[:, 0:B, :] = wide_p[...]
    s[1 : PX - 1, 0:B, :] = source[...]

    def fill(low, high):
        for unit, kind, start, count, deep in UNITS:
            field = s if kind == 0 else p
            rows = slice(start + 1 - kind, start + 1 - kind + count)
            first = B + 4 if deep else B
            field[rows, first : first + 4, :] = high[unit : unit + count]
            first = B + 8 if deep else B + 12
            field[rows, first : first + 4, :] = low[unit : unit + count]

    @pl.when(odd == 0)
    def _():
        fill(far, near)

    @pl.when(odd == 1)
    def _():
        fill(near, far)

    fine = column_sum(1, 3)
    coarse = column_sum(2, 3)
    sweep(q, p, s, 1, PX - 1, 1, 1, 0, fine)
    sweep(p, q, s, 2, PX - 2, 1, 1, 0, fine)
    for out, field, first in ((finest, p, 4), (right, s, 5)):
        out[:, 0:B, :] = field[first : PX - first, 0:B, :]
        out[:, B : B + 4, :] = field[first : PX - first, B : B + 4, :]
        out[:, B + 4 : B + 8, :] = field[first : PX - first, B + 12 : B + 16, :]
    for k in range(0, 12, 2):
        rows = scaled_residual(p, s, 3 + 2 * k, 4, 1, 1, fine)
        f1[k] = coarsen_pair(rows[0:2], 1, 1)
        f1[k + 1] = coarsen_pair(rows[2:4], 1, 1)
    a1[...] = -COEFF * f1[...]
    sweep(b1, a1, f1, 1, 11, 2, 2, 0, coarse)
    rows = scaled_residual(b1, f1, 2, 8, 2, 2, coarse)
    f2 = [coarsen_pair(rows[2 * k : 2 * k + 2], 2, 2) for k in range(4)]
    lane = lane_of(f2[0]) & 3
    two = jnp.where(lane == 0, f2[0], jnp.where(lane == 1, f2[1], jnp.where(lane == 2, f2[2], f2[3])))
    four = jnp.concatenate([two[4 * y : 4 * y + 1, :] for y in range(4)], axis=0)
    for k in range(packed_two.shape[0]):
        packed_two[k] = four
    for g in range(2):
        rows = [f1[2 + 4 * g + j][0:B] for j in range(4)]
        slot = 2 * (row_of(rows[0]) & 1) + (lane_of(rows[0]) & 1)
        packed_one[g] = jnp.where(
            slot == 0, rows[0], jnp.where(slot == 1, rows[1], jnp.where(slot == 2, rows[2], rows[3]))
        )


GROUPS = ((9, 1, 2), (11, 2, 3), (14, 3, 3), (17, 4, 2))
N_STRIP = 19


def pack_y(peers, place, blocks, own, near, far, strips, window):
    core = place[0] % 2
    gy = place[1]
    for j in range(2 * WINDOW + 1):
        piece = blocks[(place[0] + (peers - WINDOW + j)) % peers]
        for k in range(8):
            strips[k, j] = piece
    window[2:4] = own[...]

    def fill(low, high):
        window[0:2] = low[...]
        window[4:6] = high[...]

    @pl.when(core == 0)
    def _():
        fill(far, near)

    @pl.when(core == 1)
    def _():
        fill(near, far)

    for step in range(1, 8):
        peer = (gy + step) % 8
        for unit, group, count in GROUPS:
            for k in range(count):
                first = 4 * k if step == 7 else B - 4 * (count - k)
                strips[peer, unit + k] = window[group, first : first + 4, :]
    for k in range(9, N_STRIP):
        strips[gy, k] = jnp.zeros((4, 128), F32)


def packed_neighbours(ref, b, dx, dy, dz):
    p = ref[b]
    before = ref[max(b - 1, 0)]
    after = ref[min(b + 1, 2 * WINDOW)]
    lane = lane_of(p)
    slot = lane & 3
    left = jnp.where(slot < dx, turn(before, dx - 4, 1), turn(p, dx, 1))
    right = jnp.where(slot >= 4 - dx, turn(after, 4 - dx, 1), turn(p, -dx, 1))
    below = jnp.where(lane < dz, p, turn(p, dz, 1))
    above = jnp.where(lane >= 128 - dz, p, turn(p, -dz, 1))
    return p, (left + right) + (turn(p, dy, 0) + turn(p, -dy, 0)) + 4.0 * (below + above)


def packed_sweep(dst, src, right, blocks, dx, dy, dz):
    for b in blocks:
        p, around = packed_neighbours(src, b, dx, dy, dz)
        dst[b] = 0.2 * p + COEFF * (around - right[b])


def packed_residual(src, right, b, dx, dy, dz):
    p, around = packed_neighbours(src, b, dx, dy, dz)
    return right[b] - around + 12.0 * p


def without_middle(values):
    return jnp.concatenate([values[..., 0:24, :], values[..., 32:40, :]], axis=-2)


def finish(place, strips, window, finest, right, star, velocity_new, pressure_new, f2, a2, b2, f3, a3, b3, g1, f1, a1, b1, c1, d1, e1, p0, q0):
    gy = place[1]
    for j in range(8):
        peer = (gy + j) % 8
        for b in range(2 * WINDOW + 1):
            f2[b, 4 * j : 4 * j + 4, :] = strips[peer, b]
    for b in range(9):
        a2[b] = -COEFF * f2[b]
    packed_sweep(b2, a2, f2, range(9), 1, 1, 4)
    for b in range(1, 8):
        total = packed_residual(b2, f2, b, 1, 1, 4)
        lane = lane_of(total)
        total = total + jnp.where((lane & 1) == 0, turn(total, -1, 1), turn(total, 1, 1))
        total = total + jnp.where((lane & 4) == 0, turn(total, -4, 1), turn(total, 4, 1))
        row = row_of(total)
        total = total + jnp.where((row & 1) == 0, turn(total, -1, 0), turn(total, 1, 0))
        f3[b] = 0.5 * total
        a3[b] = (-0.5 * COEFF) * total
    packed_sweep(b3, a3, f3, range(1, 8), 2, 2, 8)
    packed_sweep(a3, b3, f3, range(2, 7), 2, 2, 8)
    packed_sweep(b3, a3, f3, range(2, 7), 2, 2, 8)
    for b in range(3, 6):
        line = jnp.sum(packed_residual(b3, f3, b, 2, 2, 8), axis=0, keepdims=True) * (COEFF / 32.0)
        a2[b] = b2[b] + (b3[b] - line)
    packed_sweep(b2, a2, f2, range(3, 6), 1, 1, 4)
    packed_sweep(a2, b2, f2, range(3, 6), 1, 1, 4)
    g1[:, 0:B, :] = window[...]
    for unit, group, count in GROUPS:
        for k in range(count):
            first = B + 4 * k
            g1[group, first : first + 4, :] = strips[(gy + 1) % 8, unit + k]
            first = B + 24 - 4 * (count - k)
            g1[group, first : first + 4, :] = strips[(gy + 7) % 8, unit + k]
    for x in range(3, 21):
        packed = g1[x // 4]
        slots = 2 * (row_of(packed) & 1) + (lane_of(packed) & 1)
        slot = x % 4
        part = jnp.where(slots == slot, packed, 0.0)
        part = part + turn(part, 1 if slot % 2 == 0 else -1, 1)
        part = part + turn(part, 1 if slot < 2 else -1, 0)
        f1[x] = part
        a1[x] = -COEFF * part
    sweep(b1, a1, f1, 4, 20, 2, 2)
    for k in range(8):
        block = a2[3 + (k + 2) // 4]
        slot = (k + 2) % 4
        low, high = block[0:8], block[24:32]
        part = jnp.where(row_of(low) < 6, low, high)
        part = jnp.where((lane_of(part) & 3) == slot, part, 0.0)
        part = part + turn(part, 1 if slot % 2 == 0 else -1, 1)
        part = part + turn(part, 2 if slot < 2 else -2, 1)
        for q in range(8):
            e1[k, 4 * q : 4 * q + 4, :] = jnp.broadcast_to(part[q : q + 1, :], (4, 128))
    for r in range(4, 20):
        c1[r] = without_middle(b1[r]) + e1[(r - 4) // 2]
    for dst, src, first, last in ((d1, c1, 5, 19), (c1, d1, 6, 18)):
        for i, n in chunks(first, last):
            p, around = neighbours(src, i, n, 2, 2)
            dst[i : i + n] = 0.2 * p + COEFF * (around - without_middle(f1[i : i + n]))
    for i in range(22):
        coarse = c1[6 + (i + 1) // 2]
        edge = coarse[16:24]
        p0[i, 0:B, :] = finest[i, 0:B, :] + coarse[0:B]
        p0[i, B:, :] = finest[i, B:, :] + jnp.where(row_of(edge) < 4, edge, coarse[24:32])
    sweep(q0, p0, right, 1, 21, 1, 1, 1)
    sweep(p0, q0, right, 2, 20, 1, 1, 1)
    for i in range(B):
        p = p0[3 + i]
        lane = lane_of(p)
        above = jnp.where(lane == 127, p, turn(p, -1, 1))
        below = jnp.where(lane == 0, p, turn(p, 1, 1))
        along_x = p0[4 + i] - p0[2 + i]
        along_y = turn(p, -1, 0) - turn(p, 1, 0)
        velocity_new[0, i] = star[0, i] - (0.5 * STEP) * along_x[0:B]
        velocity_new[1, i] = star[1, i] - (0.5 * STEP) * along_y[0:B]
        velocity_new[2, i] = star[2, i] - STEP * (above - below)[0:B]
        pressure_new[i] = p[0:B]


def swaps(count):
    near = [(i, i ^ 1) for i in range(count)]
    far = [(i, (((i + 1) ^ 1) - 1) % count) for i in range(count)]
    return near, far


def exchange(near_block, far_block, axis):
    near, far = swaps(lax.axis_size(axis))
    far_block = lax.ppermute(far_block, axis, far)
    return lax.ppermute(near_block, axis, near), far_block


def per_device(velocity, pressure, land_type, turbine_cells, surface_drag):
    gx = lax.axis_size("gx")
    gy = lax.axis_size("gy")
    place = jnp.stack([lax.axis_index("gx"), lax.axis_index("gy")]).astype(jnp.int32)
    near, far, drag = call(
        pack_x,
        [shape(SIDE, B, 128), shape(SIDE, B, 128), shape(B, B, 128)],
        [SMEM, SMEM] + [HBM] * 4,
        [pltpu.VMEM((B, B), jnp.int32), pltpu.VMEM((B, B, 128), jnp.int32), pltpu.SemaphoreType.DMA((10,))],
    )(place, surface_drag, land_type, velocity, pressure, turbine_cells)
    near, far = exchange(near, far, "gx")
    wide_v, wide_p, wide_d, near, far = call(
        widen_x,
        [shape(3, VX, B, 128), shape(PX, B, 128), shape(PX, B, 128), shape(8, 40, 128), shape(8, 40, 128)],
        [SMEM] + [VMEM] * 5,
    )(place, velocity, pressure, drag, near, far)
    near, far = exchange(near, far, "gy")
    star, source, near, far = call(
        advance,
        [shape(3, B, B, 128), shape(PX - 2, B, 128), shape(N_UNITS, 4, 128), shape(N_UNITS, 4, 128)],
        [SMEM] + [VMEM] * 5,
        [(3, VX, 24, 128), (PX, 24, 128), (3, VX, 24, 128), (3, VX, 24, 128)],
    )(place, wide_v, wide_p, wide_d, near, far)
    near, far = exchange(near, far, "gy")
    finest, right, packed_one, packed_two = call(
        presmooth,
        [shape(22, 24, 128), shape(20, 24, 128), shape(2, B, 128), shape(gx, 4, 128)],
        [SMEM] + [VMEM] * 4,
        [(PX, 32, 128)] * 3 + [(12, 32, 128)] * 3,
    )(place, source, wide_p, near, far)
    near, far = exchange(packed_one, packed_one, "gx")
    blocks = lax.all_to_all(packed_two, "gx", 0, 0, tiled=True)
    strips, window = call(
        lambda *refs: pack_y(gx, *refs),
        [shape(gy, N_STRIP, 4, 128), shape(6, B, 128)],
        [SMEM] + [VMEM] * 4,
    )(place, blocks, packed_one, near, far)
    strips = lax.all_to_all(strips, "gy", 0, 0, tiled=True)
    velocity_new, pressure_new = call(
        finish,
        [shape(3, B, B, 128), shape(B, B, 128)],
        [SMEM] + [VMEM] * 5,
        [(9, 32, 128)] * 6
        + [(6, 40, 128)]
        + [(24, 40, 128)] * 3
        + [(24, 32, 128)] * 2
        + [(8, 32, 128)]
        + [(22, 24, 128)] * 2,
    )(place, strips, window, finest, right, star)
    return velocity_new, pressure_new


def solution(mesh):
    in_specs = (
        P(None, "gx", "gy", None),
        P("gx", "gy", None),
        P("gx", "gy"),
        P("gx", "gy", None),
        P(),
    )
    out_specs = (P(None, "gx", "gy", None), P("gx", "gy", None))
    return jax.shard_map(
        per_device, mesh=mesh, in_specs=in_specs, out_specs=out_specs, check_vma=False
    )
```

```python
import jax
import jax.numpy as jnp
from jax import lax
from jax.experimental import pallas as pl
from jax.experimental.pallas import tpu as pltpu
from jax.sharding import PartitionSpec as P

VH = 9
PH = 7
B = 16
VX = B + 2 * VH
PX = B + 2 * PH
SIDE = 3 * VH + 2 * PH
STEP = 0.1
ROWS = 8
EDDY = 0.03
COEFF = 0.8 / 12.0
WINDOW = 4
VMEM = pl.BlockSpec(memory_space=pltpu.VMEM)
SMEM = pl.BlockSpec(memory_space=pltpu.SMEM)
HBM = pl.BlockSpec(memory_space=pltpu.HBM)
UNITS = (
    (0, 0, 5, 18, True),
    (18, 0, 5, 18, False),
    (36, 0, 1, 4, False),
    (40, 0, 23, 4, False),
    (44, 1, 5, 20, True),
    (64, 1, 5, 20, False),
    (84, 1, 1, 4, False),
    (88, 1, 25, 4, False),
)
N_UNITS = 92
F32 = jnp.float32


def shape(*dims):
    return jax.ShapeDtypeStruct(dims, F32)


def call(body, outs, specs, scratch=(), grant=48, out_space=None):
    return pl.pallas_call(
        body,
        out_shape=outs,
        in_specs=specs,
        out_specs=[out_space or VMEM] * len(outs),
        scratch_shapes=[pltpu.VMEM(s, F32) if isinstance(s, tuple) else s for s in scratch],
        compiler_params=pltpu.CompilerParams(vmem_limit_bytes=grant * 1024 * 1024),
    )


def iota(like, dim):
    return lax.broadcasted_iota(jnp.int32, like.shape, dim)


def lane_of(values):
    return iota(values, values.ndim - 1)


def row_of(values):
    return iota(values, values.ndim - 2)


def turn(values, amount, dim):
    return pltpu.roll(values, amount % values.shape[dim], dim)


def pack_x(place, drag_table, land, velocity, pressure, turbine, near, far, drag, kinds_ref, cells_ref, sems):
    core = place[0] % 2
    copies = [
        pltpu.make_async_copy(turbine, cells_ref, sems.at[0]),
        pltpu.make_async_copy(land, kinds_ref, sems.at[1]),
    ]
    for side, out in ((0, near), (1, far)):
        high = (core + side) % 2 == 0
        start = jnp.where(high, B - VH, 0)
        for a in range(3):
            copies.append(
                pltpu.make_async_copy(
                    velocity.at[a, pl.ds(start, VH)], out.at[pl.ds(a * VH, VH)], sems.at[2 + 4 * side + a]
                )
            )
        start = jnp.where(high, B - PH, 0)
        copies.append(
            pltpu.make_async_copy(
                pressure.at[pl.ds(start, PH)], out.at[pl.ds(3 * VH, PH)], sems.at[5 + 4 * side]
            )
        )
    for copy in copies:
        copy.start()
    copies[1].wait()
    kinds = kinds_ref[...]
    ground = jnp.zeros(kinds.shape, F32)
    for kind in range(16):
        ground = jnp.where(kinds == kind, drag_table[kind], ground)
    square = lax.broadcasted_iota(jnp.int32, (B, B), 0) == lax.broadcasted_iota(jnp.int32, (B, B), 1)
    columns = []
    for i in range(B):
        row = jnp.broadcast_to(ground[i : i + 1, :], (B, B))
        columns.append(jnp.sum(jnp.where(square, row, 0.0), axis=1, keepdims=True))
    copies[0].wait()
    for i in range(B):
        cells = cells_ref[i].astype(F32)
        drag[i] = 2.0 * cells + jnp.where(lane_of(cells) == 0, columns[i], 0.0)

    @pl.when(core == 0)
    def _():
        near[3 * VH + PH : SIDE] = drag[B - PH :]
        far[3 * VH + PH : SIDE] = drag[:PH]

    @pl.when(core == 1)
    def _():
        near[3 * VH + PH : SIDE] = drag[:PH]
        far[3 * VH + PH : SIDE] = drag[B - PH :]

    for copy in copies[2:]:
        copy.wait()


def widen_x(place, velocity, pressure, drag, near, far, wide_v, wide_p, wide_d, near_y, far_y):
    core = place[0] % 2
    odd = place[1] % 2
    for a in range(3):
        wide_v[a, VH : VH + B] = velocity[a]
    wide_p[PH : PH + B] = pressure[...]
    wide_d[PH : PH + B] = drag[...]

    def fill(low, high):
        for a in range(3):
            wide_v[a, :VH] = low[a * VH : (a + 1) * VH]
            wide_v[a, VH + B :] = high[a * VH : (a + 1) * VH]
        wide_p[:PH] = low[3 * VH : 3 * VH + PH]
        wide_p[PH + B :] = high[3 * VH : 3 * VH + PH]
        wide_d[:PH] = low[3 * VH + PH :]
        wide_d[PH + B :] = high[3 * VH + PH :]

    @pl.when(core == 0)
    def _():
        fill(far, near)

    @pl.when(core == 1)
    def _():
        fill(near, far)

    def send(up, down):
        for g in range(8):
            for j in range(4):
                x = 1 + 4 * g + j
                for a in range(3):
                    rows = slice(10 * j + 3 * a, 10 * j + 3 * a + 3)
                    up[g, rows, :] = wide_v[a, x, B - 3 :, :]
                    down[g, rows, :] = wide_v[a, x, :3, :]
                row = slice(10 * j + 9, 10 * j + 10)
                d = min(max(x - 2, 0), PX - 1)
                up[g, row, :] = wide_d[d, B - 1 :, :]
                down[g, row, :] = wide_d[d, 0:1, :]

    @pl.when(odd == 0)
    def _():
        send(near_y, far_y)

    @pl.when(odd == 1)
    def _():
        send(far_y, near_y)


def exact_product(values, matrix):
    flat = values.reshape(-1, 128)
    high = flat.astype(jnp.bfloat16)
    rest = flat - high.astype(F32)
    middle = rest.astype(jnp.bfloat16)
    low = (rest - middle.astype(F32)).astype(jnp.bfloat16)
    parts = jnp.concatenate([high, middle, low], axis=1)
    return jnp.dot(parts, matrix, preferred_element_type=F32).reshape(values.shape)


def column_difference():
    i = lax.broadcasted_iota(jnp.int32, (128, 128), 0)
    j = lax.broadcasted_iota(jnp.int32, (128, 128), 1)
    one = jnp.where(i - j == 1, 1.0, jnp.where(j - i == 1, -1.0, 0.0))
    return jnp.concatenate([one.astype(jnp.bfloat16)] * 3, axis=0)


def advance(place, wide_v, wide_p, wide_d, near, far, star, source, near_y, far_y, v, dr, tau, part):
    odd = place[1] % 2
    v[:, :, 0:B, :] = wide_v[...]
    dr[2 : 2 + PX, 0:B, :] = wide_d[...]

    def fill(low, high):
        for g in range(8):
            for j in range(4):
                x = 1 + 4 * g + j
                for a in range(3):
                    rows = slice(10 * j + 3 * a, 10 * j + 3 * a + 3)
                    v[a, x, B : B + 3, :] = high[g, rows, :]
                    v[a, x, B + 5 : B + 8, :] = low[g, rows, :]
                if 2 <= x < 2 + PX:
                    row = slice(10 * j + 9, 10 * j + 10)
                    dr[x, B : B + 1, :] = high[g, row, :]
                    dr[x, B + 7 : B + 8, :] = low[g, row, :]

    @pl.when(odd == 0)
    def _():
        fill(far, near)

    @pl.when(odd == 1)
    def _():
        fill(near, far)

    difference = column_difference()

    def along_column(fields):
        n = fields[0].shape[0]
        whole = exact_product(jnp.concatenate(fields, axis=0), difference)
        return [whole[k * n : (k + 1) * n] for k in range(len(fields))]

    def along_row(values):
        return 0.5 * (turn(values, -1, 1) - turn(values, 1, 1))

    for i in range(1, VX - 1, ROWS):
        here = slice(i, i + ROWS)
        u = [v[a, here] for a in range(3)]
        gx = [0.5 * (v[a, i + 1 : i + 1 + ROWS] - v[a, i - 1 : i - 1 + ROWS]) for a in range(3)]
        gy = [along_row(u[a]) for a in range(3)]
        gz = along_column(u)
        e01 = gx[1] + gy[0]
        e02 = gx[2] + gz[0]
        e12 = gy[2] + gz[1]
        total = 2.0 * (gx[0] * gx[0] + gy[1] * gy[1] + gz[2] * gz[2]) + (
            e01 * e01 + e02 * e02 + e12 * e12
        )
        visc = EDDY * jnp.sqrt(total)
        t01 = visc * e01
        t02 = visc * e02
        t12 = visc * e12
        tau[0, here] = 2.0 * visc * gx[0]
        tau[1, here] = t01
        tau[2, here] = t02
        along_y = [along_row(t) for t in (t01, 2.0 * visc * gy[1], t12)]
        along_z = along_column([t02, t12, 2.0 * visc * gz[2]])
        lane = lane_of(u[0])
        flat = u[0] * u[0] + u[1] * u[1]
        edge = jnp.where((lane == 0) | (lane == 127), EDDY * jnp.sqrt(flat + 2.0 * (u[2] * u[2])), 0.0)
        wind = dr[here] * jnp.sqrt(flat)
        for a in range(3):
            change = along_y[a] + (along_z[a] - (edge * u[a] if a < 2 else 2.0 * (edge * u[a])))
            change = change - (u[0] * gx[a] + u[1] * gy[a] + u[2] * gz[a])
            if a < 2:
                change = change - wind * u[a]
            if a == 0:
                change = change + 1.0
            part[a, here] = u[a] + STEP * change
    for i in range(2, VX - 2):
        for a in range(3):
            part[a, i] = part[a, i] + (0.5 * STEP) * (tau[a, i + 1] - tau[a, i - 1])
    for a in range(3):
        star[a] = part[a, VH : VH + B, 0:B, :]
    for i in range(3, VX - 3, 4):
        along_x = 0.5 * (part[0, i + 1 : i + 5] - part[0, i - 1 : i + 3])
        along_y = along_row(part[1, i : i + 4])
        (along_z,) = along_column([part[2, i : i + 4, 0:B, :]])
        source[i - 3 : i + 1] = ((along_x + along_y)[:, 0:B] + along_z) / STEP

    def send(up, down):
        for message, outer, inner in ((up, B - 4, B - 8), (down, 0, 4)):
            for unit, kind, start, count, deep in UNITS:
                field = source if kind == 0 else wide_p
                first = inner if deep else outer
                message[unit : unit + count] = field[start : start + count, first : first + 4, :]

    @pl.when(odd == 0)
    def _():
        send(near_y, far_y)

    @pl.when(odd == 1)
    def _():
        send(far_y, near_y)


def column_sum(dz, halves):
    i = lax.broadcasted_iota(jnp.int32, (128, 128), 0)
    j = lax.broadcasted_iota(jnp.int32, (128, 128), 1)
    hit = (i - j == dz) | (j - i == dz) | ((i == j) & ((j < dz) | (j >= 128 - dz)))
    return jnp.concatenate([jnp.where(hit, 4.0, 0.0).astype(jnp.bfloat16)] * halves, axis=0)


def neighbours(ref, start, count, dy, dz, matrix=None):
    p = ref[start : start + count]
    sides = ref[start - 1 : start - 1 + count] + ref[start + 1 : start + 1 + count]
    sides = sides + (turn(p, dy, 1) + turn(p, -dy, 1))
    if matrix is not None:
        return p, sides + exact_product(p, matrix)
    lane = lane_of(p)
    below = jnp.where(lane < dz, p, turn(p, dz, 2))
    above = jnp.where(lane >= 128 - dz, p, turn(p, -dz, 2))
    return p, sides + 4.0 * (below + above)


def chunks(first, last, size=2):
    return [(i, min(size, last - i)) for i in range(first, last, size)]


def sweep(dst, src, right, first, last, dy, dz, offset=0, matrix=None):
    for i, n in chunks(first, last, 2 if matrix is None else 4):
        p, around = neighbours(src, i, n, dy, dz, matrix)
        dst[i : i + n] = 0.2 * p + COEFF * (around - right[i - offset : i - offset + n])


def scaled_residual(src, right, i, n, dy, dz, matrix=None):
    p, around = neighbours(src, i, n, dy, dz, matrix)
    return right[i : i + n] - around + 12.0 * p


def coarsen_pair(pair, dy, dz):
    total = pair[0] + pair[1]
    lane = lane_of(total)
    total = total + jnp.where((lane & dz) == 0, turn(total, -dz, 1), turn(total, dz, 1))
    row = row_of(total)
    total = total + jnp.where((row & dy) == 0, turn(total, -dy, 0), turn(total, dy, 0))
    return 0.5 * total


def presmooth(place, source, wide_p, near, far, finest, right, packed_one, packed_two, p, s, q, f1, a1, b1):
    odd = place[1] % 2
    p[:, 0:B, :] = wide_p[...]
    s[1 : PX - 1, 0:B, :] = source[...]

    def fill(low, high):
        for unit, kind, start, count, deep in UNITS:
            field = s if kind == 0 else p
            rows = slice(start + 1 - kind, start + 1 - kind + count)
            first = B + 4 if deep else B
            field[rows, first : first + 4, :] = high[unit : unit + count]
            first = B + 8 if deep else B + 12
            field[rows, first : first + 4, :] = low[unit : unit + count]

    @pl.when(odd == 0)
    def _():
        fill(far, near)

    @pl.when(odd == 1)
    def _():
        fill(near, far)

    fine = column_sum(1, 3)
    coarse = column_sum(2, 3)
    sweep(q, p, s, 1, PX - 1, 1, 1, 0, fine)
    sweep(p, q, s, 2, PX - 2, 1, 1, 0, fine)
    for out, field, first in ((finest, p, 4), (right, s, 5)):
        out[:, 0:B, :] = field[first : PX - first, 0:B, :]
        out[:, B : B + 4, :] = field[first : PX - first, B : B + 4, :]
        out[:, B + 4 : B + 8, :] = field[first : PX - first, B + 12 : B + 16, :]
    for k in range(0, 12, 2):
        rows = scaled_residual(p, s, 3 + 2 * k, 4, 1, 1, fine)
        f1[k] = coarsen_pair(rows[0:2], 1, 1)
        f1[k + 1] = coarsen_pair(rows[2:4], 1, 1)
    a1[...] = -COEFF * f1[...]
    sweep(b1, a1, f1, 1, 11, 2, 2, 0, coarse)
    rows = scaled_residual(b1, f1, 2, 8, 2, 2, coarse)
    f2 = [coarsen_pair(rows[2 * k : 2 * k + 2], 2, 2) for k in range(4)]
    lane = lane_of(f2[0]) & 3
    two = jnp.where(lane == 0, f2[0], jnp.where(lane == 1, f2[1], jnp.where(lane == 2, f2[2], f2[3])))
    four = jnp.concatenate([two[4 * y : 4 * y + 1, :] for y in range(4)], axis=0)
    for k in range(packed_two.shape[0]):
        packed_two[k] = four
    for g in range(2):
        rows = [f1[2 + 4 * g + j][0:B] for j in range(4)]
        slot = 2 * (row_of(rows[0]) & 1) + (lane_of(rows[0]) & 1)
        packed_one[g] = jnp.where(
            slot == 0, rows[0], jnp.where(slot == 1, rows[1], jnp.where(slot == 2, rows[2], rows[3]))
        )


GROUPS = ((9, 1, 2), (11, 2, 3), (14, 3, 3), (17, 4, 2))
N_STRIP = 19


def pack_y(peers, place, blocks, own, near, far, strips, window):
    core = place[0] % 2
    gy = place[1]
    for j in range(2 * WINDOW + 1):
        piece = blocks[(place[0] + (peers - WINDOW + j)) % peers]
        for k in range(8):
            strips[k, j] = piece
    window[2:4] = own[...]

    def fill(low, high):
        window[0:2] = low[...]
        window[4:6] = high[...]

    @pl.when(core == 0)
    def _():
        fill(far, near)

    @pl.when(core == 1)
    def _():
        fill(near, far)

    for step in range(1, 8):
        peer = (gy + step) % 8
        for unit, group, count in GROUPS:
            for k in range(count):
                first = 4 * k if step == 7 else B - 4 * (count - k)
                strips[peer, unit + k] = window[group, first : first + 4, :]
    for k in range(9, N_STRIP):
        strips[gy, k] = jnp.zeros((4, 128), F32)


def packed_neighbours(ref, b, dx, dy, dz):
    p = ref[b]
    before = ref[max(b - 1, 0)]
    after = ref[min(b + 1, 2 * WINDOW)]
    lane = lane_of(p)
    slot = lane & 3
    left = jnp.where(slot < dx, turn(before, dx - 4, 1), turn(p, dx, 1))
    right = jnp.where(slot >= 4 - dx, turn(after, 4 - dx, 1), turn(p, -dx, 1))
    below = jnp.where(lane < dz, p, turn(p, dz, 1))
    above = jnp.where(lane >= 128 - dz, p, turn(p, -dz, 1))
    return p, (left + right) + (turn(p, dy, 0) + turn(p, -dy, 0)) + 4.0 * (below + above)


def packed_sweep(dst, src, right, blocks, dx, dy, dz):
    for b in blocks:
        p, around = packed_neighbours(src, b, dx, dy, dz)
        dst[b] = 0.2 * p + COEFF * (around - right[b])


def packed_residual(src, right, b, dx, dy, dz):
    p, around = packed_neighbours(src, b, dx, dy, dz)
    return right[b] - around + 12.0 * p


def without_middle(values):
    return jnp.concatenate([values[..., 0:24, :], values[..., 32:40, :]], axis=-2)


def finish(place, strips, window, finest, right, star, velocity_new, pressure_new, f2, a2, b2, f3, a3, b3, g1, f1, a1, b1, c1, d1, e1, p0, q0):
    gy = place[1]
    for j in range(8):
        peer = (gy + j) % 8
        for b in range(2 * WINDOW + 1):
            f2[b, 4 * j : 4 * j + 4, :] = strips[peer, b]
    for b in range(9):
        a2[b] = -COEFF * f2[b]
    packed_sweep(b2, a2, f2, range(9), 1, 1, 4)
    for b in range(1, 8):
        total = packed_residual(b2, f2, b, 1, 1, 4)
        lane = lane_of(total)
        total = total + jnp.where((lane & 1) == 0, turn(total, -1, 1), turn(total, 1, 1))
        total = total + jnp.where((lane & 4) == 0, turn(total, -4, 1), turn(total, 4, 1))
        row = row_of(total)
        total = total + jnp.where((row & 1) == 0, turn(total, -1, 0), turn(total, 1, 0))
        f3[b] = 0.5 * total
        a3[b] = (-0.5 * COEFF) * total
    packed_sweep(b3, a3, f3, range(1, 8), 2, 2, 8)
    packed_sweep(a3, b3, f3, range(2, 7), 2, 2, 8)
    packed_sweep(b3, a3, f3, range(2, 7), 2, 2, 8)
    for b in range(3, 6):
        line = jnp.sum(packed_residual(b3, f3, b, 2, 2, 8), axis=0, keepdims=True) * (COEFF / 32.0)
        a2[b] = b2[b] + (b3[b] - line)
    packed_sweep(b2, a2, f2, range(3, 6), 1, 1, 4)
    packed_sweep(a2, b2, f2, range(3, 6), 1, 1, 4)
    g1[:, 0:B, :] = window[...]
    for unit, group, count in GROUPS:
        for k in range(count):
            first = B + 4 * k
            g1[group, first : first + 4, :] = strips[(gy + 1) % 8, unit + k]
            first = B + 24 - 4 * (count - k)
            g1[group, first : first + 4, :] = strips[(gy + 7) % 8, unit + k]
    for x in range(3, 21):
        packed = g1[x // 4]
        slots = 2 * (row_of(packed) & 1) + (lane_of(packed) & 1)
        slot = x % 4
        part = jnp.where(slots == slot, packed, 0.0)
        part = part + turn(part, 1 if slot % 2 == 0 else -1, 1)
        part = part + turn(part, 1 if slot < 2 else -1, 0)
        f1[x] = part
        a1[x] = -COEFF * part
    sweep(b1, a1, f1, 4, 20, 2, 2)
    for k in range(8):
        block = a2[3 + (k + 2) // 4]
        slot = (k + 2) % 4
        low, high = block[0:8], block[24:32]
        part = jnp.where(row_of(low) < 6, low, high)
        part = jnp.where((lane_of(part) & 3) == slot, part, 0.0)
        part = part + turn(part, 1 if slot % 2 == 0 else -1, 1)
        part = part + turn(part, 2 if slot < 2 else -2, 1)
        for q in range(8):
            e1[k, 4 * q : 4 * q + 4, :] = jnp.broadcast_to(part[q : q + 1, :], (4, 128))
    for r in range(4, 20):
        c1[r] = without_middle(b1[r]) + e1[(r - 4) // 2]
    for dst, src, first, last in ((d1, c1, 5, 19), (c1, d1, 6, 18)):
        for i, n in chunks(first, last):
            p, around = neighbours(src, i, n, 2, 2)
            dst[i : i + n] = 0.2 * p + COEFF * (around - without_middle(f1[i : i + n]))
    for i in range(22):
        coarse = c1[6 + (i + 1) // 2]
        edge = coarse[16:24]
        p0[i, 0:B, :] = finest[i, 0:B, :] + coarse[0:B]
        p0[i, B:, :] = finest[i, B:, :] + jnp.where(row_of(edge) < 4, edge, coarse[24:32])
    sweep(q0, p0, right, 1, 21, 1, 1, 1)
    sweep(p0, q0, right, 2, 20, 1, 1, 1)
    for i in range(B):
        p = p0[3 + i]
        lane = lane_of(p)
        above = jnp.where(lane == 127, p, turn(p, -1, 1))
        below = jnp.where(lane == 0, p, turn(p, 1, 1))
        along_x = p0[4 + i] - p0[2 + i]
        along_y = turn(p, -1, 0) - turn(p, 1, 0)
        velocity_new[0, i] = star[0, i] - (0.5 * STEP) * along_x[0:B]
        velocity_new[1, i] = star[1, i] - (0.5 * STEP) * along_y[0:B]
        velocity_new[2, i] = star[2, i] - STEP * (above - below)[0:B]
        pressure_new[i] = p[0:B]


def swaps(count):
    near = [(i, i ^ 1) for i in range(count)]
    far = [(i, (((i + 1) ^ 1) - 1) % count) for i in range(count)]
    return near, far


def exchange(near_block, far_block, axis):
    near, far = swaps(lax.axis_size(axis))
    far_block = lax.ppermute(far_block, axis, far)
    return lax.ppermute(near_block, axis, near), far_block


def per_device(velocity, pressure, land_type, turbine_cells, surface_drag):
    gx = lax.axis_size("gx")
    gy = lax.axis_size("gy")
    place = jnp.stack([lax.axis_index("gx"), lax.axis_index("gy")]).astype(jnp.int32)
    near, far, drag = call(
        pack_x,
        [shape(SIDE, B, 128), shape(SIDE, B, 128), shape(B, B, 128)],
        [SMEM, SMEM] + [HBM] * 4,
        [
            pltpu.VMEM((B, B), jnp.int32),
            pltpu.VMEM((B, B, 128), jnp.int32),
            pltpu.SemaphoreType.DMA((10,)),
        ],
        60,
    )(place, surface_drag, land_type, velocity, pressure, turbine_cells)
    near, far = exchange(near, far, "gx")
    wide_v, wide_p, wide_d, near, far = call(
        widen_x,
        [shape(3, VX, B, 128), shape(PX, B, 128), shape(PX, B, 128), shape(8, 40, 128), shape(8, 40, 128)],
        [SMEM] + [VMEM] * 5,
    )(place, velocity, pressure, drag, near, far)
    near, far = exchange(near, far, "gy")
    star, source, near, far = call(
        advance,
        [shape(3, B, B, 128), shape(PX - 2, B, 128), shape(N_UNITS, 4, 128), shape(N_UNITS, 4, 128)],
        [SMEM] + [VMEM] * 5,
        [(3, VX, 24, 128), (VX, 24, 128), (3, VX, 24, 128), (3, VX, 24, 128)],
    )(place, wide_v, wide_p, wide_d, near, far)
    near, far = exchange(near, far, "gy")
    finest, right, packed_one, packed_two = call(
        presmooth,
        [shape(22, 24, 128), shape(20, 24, 128), shape(2, B, 128), shape(gx, 4, 128)],
        [SMEM] + [VMEM] * 4,
        [(PX, 32, 128)] * 3 + [(12, 32, 128)] * 3,
    )(place, source, wide_p, near, far)
    near, far = exchange(packed_one, packed_one, "gx")
    blocks = lax.all_to_all(packed_two, "gx", 0, 0, tiled=True)
    strips, window = call(
        lambda *refs: pack_y(gx, *refs),
        [shape(gy, N_STRIP, 4, 128), shape(6, B, 128)],
        [SMEM] + [VMEM] * 4,
    )(place, blocks, packed_one, near, far)
    strips = lax.all_to_all(strips, "gy", 0, 0, tiled=True)
    velocity_new, pressure_new = call(
        finish,
        [shape(3, B, B, 128), shape(B, B, 128)],
        [SMEM] + [VMEM] * 5,
        [(9, 32, 128)] * 6
        + [(6, 40, 128)]
        + [(24, 40, 128)] * 3
        + [(24, 32, 128)] * 2
        + [(8, 32, 128)]
        + [(22, 24, 128)] * 2,
    )(place, strips, window, finest, right, star)
    return velocity_new, pressure_new


def solution(mesh):
    in_specs = (
        P(None, "gx", "gy", None),
        P("gx", "gy", None),
        P("gx", "gy"),
        P("gx", "gy", None),
        P(),
    )
    out_specs = (P(None, "gx", "gy", None), P("gx", "gy", None))
    return jax.shard_map(
        per_device, mesh=mesh, in_specs=in_specs, out_specs=out_specs, check_vma=False
    )
```

```python
import jax
import jax.numpy as jnp
from jax import lax
from jax.experimental import pallas as pl
from jax.experimental.pallas import tpu as pltpu
from jax.sharding import PartitionSpec as P

VH = 9
PH = 7
B = 16
VX = B + 2 * VH
PX = B + 2 * PH
SIDE = 3 * VH + 2 * PH
STEP = 0.1
ROWS = 8
EDDY = 0.03
COEFF = 0.8 / 12.0
WINDOW = 4
VMEM = pl.BlockSpec(memory_space=pltpu.VMEM)
SMEM = pl.BlockSpec(memory_space=pltpu.SMEM)
HBM = pl.BlockSpec(memory_space=pltpu.HBM)
S_UNITS = ((0, 5, 18, True), (18, 5, 18, False), (36, 1, 4, False), (40, 23, 4, False))
P_UNITS = ((0, 5, 20, True), (20, 5, 20, False), (40, 1, 4, False), (44, 25, 4, False))
N_S = 44
N_P = 48
F32 = jnp.float32


def shape(*dims):
    return jax.ShapeDtypeStruct(dims, F32)


def call(body, outs, specs, scratch=(), grant=48, out_space=None):
    return pl.pallas_call(
        body,
        out_shape=outs,
        in_specs=specs,
        out_specs=[out_space or VMEM] * len(outs),
        scratch_shapes=[pltpu.VMEM(s, F32) if isinstance(s, tuple) else s for s in scratch],
        compiler_params=pltpu.CompilerParams(vmem_limit_bytes=grant * 1024 * 1024),
    )


def iota(like, dim):
    return lax.broadcasted_iota(jnp.int32, like.shape, dim)


def lane_of(values):
    return iota(values, values.ndim - 1)


def row_of(values):
    return iota(values, values.ndim - 2)


def turn(values, amount, dim):
    return pltpu.roll(values, amount % values.shape[dim], dim)


def ground_columns(kinds, drag_table):
    ground = jnp.zeros(kinds.shape, F32)
    for kind in range(16):
        ground = jnp.where(kinds == kind, drag_table[kind], ground)
    square = lax.broadcasted_iota(jnp.int32, (B, B), 0) == lax.broadcasted_iota(jnp.int32, (B, B), 1)
    columns = []
    for i in range(B):
        row = jnp.broadcast_to(ground[i : i + 1, :], (B, B))
        columns.append(jnp.sum(jnp.where(square, row, 0.0), axis=1, keepdims=True))
    return columns


def drag_row(cells, column):
    return 2.0 * cells.astype(F32) + jnp.where(lane_of(cells) == 0, column, 0.0)


def edge_units(units, field, up, down):
    for message, outer, inner in ((up, B - 4, B - 8), (down, 0, 4)):
        for unit, start, count, deep in units:
            first = inner if deep else outer
            message[unit : unit + count] = field[start : start + count, first : first + 4, :]


def place_units(units, field, shift, low, high):
    for unit, start, count, deep in units:
        rows = slice(start + shift, start + shift + count)
        first = B + 4 if deep else B
        field[rows, first : first + 4, :] = high[unit : unit + count]
        first = B + 8 if deep else B + 12
        field[rows, first : first + 4, :] = low[unit : unit + count]


def pack_x(drag_table, land, velocity, pressure, turbine, near, far, kinds_ref, cells_ref, drag, sems):
    core = lax.axis_index("gx") % 2
    copies = [
        pltpu.make_async_copy(turbine, cells_ref, sems.at[0]),
        pltpu.make_async_copy(land, kinds_ref, sems.at[1]),
    ]
    for side, out in ((0, near), (1, far)):
        high = (core + side) % 2 == 0
        start = jnp.where(high, B - VH, 0)
        for a in range(3):
            copies.append(
                pltpu.make_async_copy(
                    velocity.at[a, pl.ds(start, VH)], out.at[pl.ds(a * VH, VH)], sems.at[2 + 4 * side + a]
                )
            )
        start = jnp.where(high, B - PH, 0)
        copies.append(
            pltpu.make_async_copy(
                pressure.at[pl.ds(start, PH)], out.at[pl.ds(3 * VH, PH)], sems.at[5 + 4 * side]
            )
        )
    for copy in copies:
        copy.start()
    copies[1].wait()
    columns = ground_columns(kinds_ref[...], drag_table)
    copies[0].wait()
    for i in range(B):
        drag[i] = drag_row(cells_ref[i], columns[i])

    @pl.when(core == 0)
    def _():
        near[3 * VH + PH : SIDE] = drag[B - PH :]
        far[3 * VH + PH : SIDE] = drag[:PH]

    @pl.when(core == 1)
    def _():
        near[3 * VH + PH : SIDE] = drag[:PH]
        far[3 * VH + PH : SIDE] = drag[B - PH :]

    for copy in copies[2:]:
        copy.wait()


def widen_x(place, drag_table, land, velocity, pressure, turbine, near, far, wide_v, wide_p, wide_d, near_y, far_y, near_p, far_p):
    core = place[0] % 2
    odd = place[1] % 2
    columns = ground_columns(land[...], drag_table)
    for i in range(B):
        wide_d[PH + i] = drag_row(turbine[i], columns[i])
    for a in range(3):
        wide_v[a, VH : VH + B] = velocity[a]
    wide_p[PH : PH + B] = pressure[...]

    def fill(low, high):
        for a in range(3):
            wide_v[a, :VH] = low[a * VH : (a + 1) * VH]
            wide_v[a, VH + B :] = high[a * VH : (a + 1) * VH]
        wide_p[:PH] = low[3 * VH : 3 * VH + PH]
        wide_p[PH + B :] = high[3 * VH : 3 * VH + PH]
        wide_d[:PH] = low[3 * VH + PH :]
        wide_d[PH + B :] = high[3 * VH + PH :]

    @pl.when(core == 0)
    def _():
        fill(far, near)

    @pl.when(core == 1)
    def _():
        fill(near, far)

    def send(up, down):
        for g in range(8):
            for j in range(4):
                x = 1 + 4 * g + j
                for a in range(3):
                    rows = slice(10 * j + 3 * a, 10 * j + 3 * a + 3)
                    up[g, rows, :] = wide_v[a, x, B - 3 :, :]
                    down[g, rows, :] = wide_v[a, x, :3, :]
                row = slice(10 * j + 9, 10 * j + 10)
                d = min(max(x - 2, 0), PX - 1)
                up[g, row, :] = wide_d[d, B - 1 :, :]
                down[g, row, :] = wide_d[d, 0:1, :]

    @pl.when(odd == 0)
    def _():
        send(near_y, far_y)
        edge_units(P_UNITS, wide_p, near_p, far_p)

    @pl.when(odd == 1)
    def _():
        send(far_y, near_y)
        edge_units(P_UNITS, wide_p, far_p, near_p)


def exact_product(values, matrix):
    flat = values.reshape(-1, 128)
    high = flat.astype(jnp.bfloat16)
    rest = flat - high.astype(F32)
    middle = rest.astype(jnp.bfloat16)
    low = (rest - middle.astype(F32)).astype(jnp.bfloat16)
    parts = jnp.concatenate([high, middle, low], axis=1)
    return jnp.dot(parts, matrix, preferred_element_type=F32).reshape(values.shape)


def column_difference():
    i = lax.broadcasted_iota(jnp.int32, (128, 128), 0)
    j = lax.broadcasted_iota(jnp.int32, (128, 128), 1)
    one = jnp.where(i - j == 1, 1.0, jnp.where(j - i == 1, -1.0, 0.0))
    return jnp.concatenate([one.astype(jnp.bfloat16)] * 3, axis=0)


def advance(place, wide_v, wide_d, near, far, star, source, near_y, far_y, v, dr, tau, part):
    odd = place[1] % 2
    v[:, :, 0:B, :] = wide_v[...]
    dr[2 : 2 + PX, 0:B, :] = wide_d[...]

    def fill(low, high):
        for g in range(8):
            for j in range(4):
                x = 1 + 4 * g + j
                for a in range(3):
                    rows = slice(10 * j + 3 * a, 10 * j + 3 * a + 3)
                    v[a, x, B : B + 3, :] = high[g, rows, :]
                    v[a, x, B + 5 : B + 8, :] = low[g, rows, :]
                if 2 <= x < 2 + PX:
                    row = slice(10 * j + 9, 10 * j + 10)
                    dr[x, B : B + 1, :] = high[g, row, :]
                    dr[x, B + 7 : B + 8, :] = low[g, row, :]

    @pl.when(odd == 0)
    def _():
        fill(far, near)

    @pl.when(odd == 1)
    def _():
        fill(near, far)

    difference = column_difference()

    def along_column(fields):
        n = fields[0].shape[0]
        whole = exact_product(jnp.concatenate(fields, axis=0), difference)
        return [whole[k * n : (k + 1) * n] for k in range(len(fields))]

    def along_row(values):
        return 0.5 * (turn(values, -1, 1) - turn(values, 1, 1))

    for i in range(1, VX - 1, ROWS):
        here = slice(i, i + ROWS)
        u = [v[a, here] for a in range(3)]
        gx = [0.5 * (v[a, i + 1 : i + 1 + ROWS] - v[a, i - 1 : i - 1 + ROWS]) for a in range(3)]
        gy = [along_row(u[a]) for a in range(3)]
        gz = along_column(u)
        e01 = gx[1] + gy[0]
        e02 = gx[2] + gz[0]
        e12 = gy[2] + gz[1]
        total = 2.0 * (gx[0] * gx[0] + gy[1] * gy[1] + gz[2] * gz[2]) + (
            e01 * e01 + e02 * e02 + e12 * e12
        )
        visc = EDDY * jnp.sqrt(total)
        t01 = visc * e01
        t02 = visc * e02
        t12 = visc * e12
        tau[0, here] = 2.0 * visc * gx[0]
        tau[1, here] = t01
        tau[2, here] = t02
        along_y = [along_row(t) for t in (t01, 2.0 * visc * gy[1], t12)]
        along_z = along_column([t02, t12, 2.0 * visc * gz[2]])
        lane = lane_of(u[0])
        flat = u[0] * u[0] + u[1] * u[1]
        edge = jnp.where((lane == 0) | (lane == 127), EDDY * jnp.sqrt(flat + 2.0 * (u[2] * u[2])), 0.0)
        wind = dr[here] * jnp.sqrt(flat)
        for a in range(3):
            change = along_y[a] + (along_z[a] - (edge * u[a] if a < 2 else 2.0 * (edge * u[a])))
            change = change - (u[0] * gx[a] + u[1] * gy[a] + u[2] * gz[a])
            if a < 2:
                change = change - wind * u[a]
            if a == 0:
                change = change + 1.0
            part[a, here] = u[a] + STEP * change
    for i in range(2, VX - 2):
        for a in range(3):
            part[a, i] = part[a, i] + (0.5 * STEP) * (tau[a, i + 1] - tau[a, i - 1])
    for a in range(3):
        star[a] = part[a, VH : VH + B, 0:B, :]
    for i in range(3, VX - 3, 4):
        along_x = 0.5 * (part[0, i + 1 : i + 5] - part[0, i - 1 : i + 3])
        along_y = along_row(part[1, i : i + 4])
        (along_z,) = along_column([part[2, i : i + 4, 0:B, :]])
        source[i - 3 : i + 1] = ((along_x + along_y)[:, 0:B] + along_z) / STEP

    @pl.when(odd == 0)
    def _():
        edge_units(S_UNITS, source, near_y, far_y)

    @pl.when(odd == 1)
    def _():
        edge_units(S_UNITS, source, far_y, near_y)


def column_sum(dz, halves):
    i = lax.broadcasted_iota(jnp.int32, (128, 128), 0)
    j = lax.broadcasted_iota(jnp.int32, (128, 128), 1)
    hit = (i - j == dz) | (j - i == dz) | ((i == j) & ((j < dz) | (j >= 128 - dz)))
    return jnp.concatenate([jnp.where(hit, 4.0, 0.0).astype(jnp.bfloat16)] * halves, axis=0)


def neighbours(ref, start, count, dy, dz, matrix=None):
    p = ref[start : start + count]
    sides = ref[start - 1 : start - 1 + count] + ref[start + 1 : start + 1 + count]
    sides = sides + (turn(p, dy, 1) + turn(p, -dy, 1))
    if matrix is not None:
        return p, sides + exact_product(p, matrix)
    lane = lane_of(p)
    below = jnp.where(lane < dz, p, turn(p, dz, 2))
    above = jnp.where(lane >= 128 - dz, p, turn(p, -dz, 2))
    return p, sides + 4.0 * (below + above)


def chunks(first, last, size=2):
    return [(i, min(size, last - i)) for i in range(first, last, size)]


def sweep(dst, src, right, first, last, dy, dz, offset=0, matrix=None):
    for i, n in chunks(first, last, 2 if matrix is None else 4):
        p, around = neighbours(src, i, n, dy, dz, matrix)
        dst[i : i + n] = 0.2 * p + COEFF * (around - right[i - offset : i - offset + n])


def scaled_residual(src, right, i, n, dy, dz, matrix=None):
    p, around = neighbours(src, i, n, dy, dz, matrix)
    return right[i : i + n] - around + 12.0 * p


def coarsen_pair(pair, dy, dz):
    total = pair[0] + pair[1]
    lane = lane_of(total)
    total = total + jnp.where((lane & dz) == 0, turn(total, -dz, 1), turn(total, dz, 1))
    row = row_of(total)
    total = total + jnp.where((row & dy) == 0, turn(total, -dy, 0), turn(total, dy, 0))
    return 0.5 * total


def presmooth(place, source, wide_p, near, far, near_p, far_p, finest, right, packed_one, packed_two, p, s, q, f1, a1, b1):
    odd = place[1] % 2
    p[:, 0:B, :] = wide_p[...]
    s[1 : PX - 1, 0:B, :] = source[...]

    @pl.when(odd == 0)
    def _():
        place_units(S_UNITS, s, 1, far, near)
        place_units(P_UNITS, p, 0, far_p, near_p)

    @pl.when(odd == 1)
    def _():
        place_units(S_UNITS, s, 1, near, far)
        place_units(P_UNITS, p, 0, near_p, far_p)

    fine = column_sum(1, 3)
    coarse = column_sum(2, 3)
    sweep(q, p, s, 1, PX - 1, 1, 1, 0, fine)
    sweep(p, q, s, 2, PX - 2, 1, 1, 0, fine)
    for out, field, first in ((finest, p, 4), (right, s, 5)):
        out[:, 0:B, :] = field[first : PX - first, 0:B, :]
        out[:, B : B + 4, :] = field[first : PX - first, B : B + 4, :]
        out[:, B + 4 : B + 8, :] = field[first : PX - first, B + 12 : B + 16, :]
    for k in range(0, 12, 2):
        rows = scaled_residual(p, s, 3 + 2 * k, 4, 1, 1, fine)
        f1[k] = coarsen_pair(rows[0:2], 1, 1)
        f1[k + 1] = coarsen_pair(rows[2:4], 1, 1)
    a1[...] = -COEFF * f1[...]
    sweep(b1, a1, f1, 1, 11, 2, 2, 0, coarse)
    rows = scaled_residual(b1, f1, 2, 8, 2, 2, coarse)
    f2 = [coarsen_pair(rows[2 * k : 2 * k + 2], 2, 2) for k in range(4)]
    lane = lane_of(f2[0]) & 3
    two = jnp.where(lane == 0, f2[0], jnp.where(lane == 1, f2[1], jnp.where(lane == 2, f2[2], f2[3])))
    four = jnp.concatenate([two[4 * y : 4 * y + 1, :] for y in range(4)], axis=0)
    for k in range(packed_two.shape[0]):
        packed_two[k] = four
    for g in range(2):
        rows = [f1[2 + 4 * g + j][0:B] for j in range(4)]
        slot = 2 * (row_of(rows[0]) & 1) + (lane_of(rows[0]) & 1)
        packed_one[g] = jnp.where(
            slot == 0, rows[0], jnp.where(slot == 1, rows[1], jnp.where(slot == 2, rows[2], rows[3]))
        )


GROUPS = ((9, 1, 2), (11, 2, 3), (14, 3, 3), (17, 4, 2))
N_STRIP = 19


def pack_y(peers, place, blocks, own, near, far, strips, window):
    core = place[0] % 2
    gy = place[1]
    for j in range(2 * WINDOW + 1):
        piece = blocks[(place[0] + (peers - WINDOW + j)) % peers]
        for k in range(8):
            strips[k, j] = piece
    window[2:4] = own[...]

    def fill(low, high):
        window[0:2] = low[...]
        window[4:6] = high[...]

    @pl.when(core == 0)
    def _():
        fill(far, near)

    @pl.when(core == 1)
    def _():
        fill(near, far)

    for step in range(1, 8):
        peer = (gy + step) % 8
        for unit, group, count in GROUPS:
            for k in range(count):
                first = 4 * k if step == 7 else B - 4 * (count - k)
                strips[peer, unit + k] = window[group, first : first + 4, :]
    for k in range(9, N_STRIP):
        strips[gy, k] = jnp.zeros((4, 128), F32)


def packed_neighbours(ref, b, dx, dy, dz):
    p = ref[b]
    before = ref[max(b - 1, 0)]
    after = ref[min(b + 1, 2 * WINDOW)]
    lane = lane_of(p)
    slot = lane & 3
    left = jnp.where(slot < dx, turn(before, dx - 4, 1), turn(p, dx, 1))
    right = jnp.where(slot >= 4 - dx, turn(after, 4 - dx, 1), turn(p, -dx, 1))
    below = jnp.where(lane < dz, p, turn(p, dz, 1))
    above = jnp.where(lane >= 128 - dz, p, turn(p, -dz, 1))
    return p, (left + right) + (turn(p, dy, 0) + turn(p, -dy, 0)) + 4.0 * (below + above)


def packed_sweep(dst, src, right, blocks, dx, dy, dz):
    for b in blocks:
        p, around = packed_neighbours(src, b, dx, dy, dz)
        dst[b] = 0.2 * p + COEFF * (around - right[b])


def packed_residual(src, right, b, dx, dy, dz):
    p, around = packed_neighbours(src, b, dx, dy, dz)
    return right[b] - around + 12.0 * p


def without_middle(values):
    return jnp.concatenate([values[..., 0:24, :], values[..., 32:40, :]], axis=-2)


def finish(place, strips, window, finest, right, star, velocity_new, pressure_new, f2, a2, b2, f3, a3, b3, g1, f1, a1, b1, c1, d1, e1, p0, q0):
    gy = place[1]
    for j in range(8):
        peer = (gy + j) % 8
        for b in range(2 * WINDOW + 1):
            f2[b, 4 * j : 4 * j + 4, :] = strips[peer, b]
    for b in range(9):
        a2[b] = -COEFF * f2[b]
    packed_sweep(b2, a2, f2, range(9), 1, 1, 4)
    for b in range(1, 8):
        total = packed_residual(b2, f2, b, 1, 1, 4)
        lane = lane_of(total)
        total = total + jnp.where((lane & 1) == 0, turn(total, -1, 1), turn(total, 1, 1))
        total = total + jnp.where((lane & 4) == 0, turn(total, -4, 1), turn(total, 4, 1))
        row = row_of(total)
        total = total + jnp.where((row & 1) == 0, turn(total, -1, 0), turn(total, 1, 0))
        f3[b] = 0.5 * total
        a3[b] = (-0.5 * COEFF) * total
    packed_sweep(b3, a3, f3, range(1, 8), 2, 2, 8)
    packed_sweep(a3, b3, f3, range(2, 7), 2, 2, 8)
    packed_sweep(b3, a3, f3, range(2, 7), 2, 2, 8)
    for b in range(3, 6):
        line = jnp.sum(packed_residual(b3, f3, b, 2, 2, 8), axis=0, keepdims=True) * (COEFF / 32.0)
        a2[b] = b2[b] + (b3[b] - line)
    packed_sweep(b2, a2, f2, range(3, 6), 1, 1, 4)
    packed_sweep(a2, b2, f2, range(3, 6), 1, 1, 4)
    g1[:, 0:B, :] = window[...]
    for unit, group, count in GROUPS:
        for k in range(count):
            first = B + 4 * k
            g1[group, first : first + 4, :] = strips[(gy + 1) % 8, unit + k]
            first = B + 24 - 4 * (count - k)
            g1[group, first : first + 4, :] = strips[(gy + 7) % 8, unit + k]
    for x in range(3, 21):
        packed = g1[x // 4]
        slots = 2 * (row_of(packed) & 1) + (lane_of(packed) & 1)
        slot = x % 4
        part = jnp.where(slots == slot, packed, 0.0)
        part = part + turn(part, 1 if slot % 2 == 0 else -1, 1)
        part = part + turn(part, 1 if slot < 2 else -1, 0)
        f1[x] = part
        a1[x] = -COEFF * part
    sweep(b1, a1, f1, 4, 20, 2, 2)
    for k in range(8):
        block = a2[3 + (k + 2) // 4]
        slot = (k + 2) % 4
        low, high = block[0:8], block[24:32]
        part = jnp.where(row_of(low) < 6, low, high)
        part = jnp.where((lane_of(part) & 3) == slot, part, 0.0)
        part = part + turn(part, 1 if slot % 2 == 0 else -1, 1)
        part = part + turn(part, 2 if slot < 2 else -2, 1)
        for q in range(8):
            e1[k, 4 * q : 4 * q + 4, :] = jnp.broadcast_to(part[q : q + 1, :], (4, 128))
    for r in range(4, 20):
        c1[r] = without_middle(b1[r]) + e1[(r - 4) // 2]
    for dst, src, first, last in ((d1, c1, 5, 19), (c1, d1, 6, 18)):
        for i, n in chunks(first, last):
            p, around = neighbours(src, i, n, 2, 2)
            dst[i : i + n] = 0.2 * p + COEFF * (around - without_middle(f1[i : i + n]))
    for i in range(22):
        coarse = c1[6 + (i + 1) // 2]
        edge = coarse[16:24]
        p0[i, 0:B, :] = finest[i, 0:B, :] + coarse[0:B]
        p0[i, B:, :] = finest[i, B:, :] + jnp.where(row_of(edge) < 4, edge, coarse[24:32])
    sweep(q0, p0, right, 1, 21, 1, 1, 1)
    sweep(p0, q0, right, 2, 20, 1, 1, 1)
    for i in range(B):
        p = p0[3 + i]
        lane = lane_of(p)
        above = jnp.where(lane == 127, p, turn(p, -1, 1))
        below = jnp.where(lane == 0, p, turn(p, 1, 1))
        along_x = p0[4 + i] - p0[2 + i]
        along_y = turn(p, -1, 0) - turn(p, 1, 0)
        velocity_new[0, i] = star[0, i] - (0.5 * STEP) * along_x[0:B]
        velocity_new[1, i] = star[1, i] - (0.5 * STEP) * along_y[0:B]
        velocity_new[2, i] = star[2, i] - STEP * (above - below)[0:B]
        pressure_new[i] = p[0:B]


def swaps(count):
    near = [(i, i ^ 1) for i in range(count)]
    far = [(i, (((i + 1) ^ 1) - 1) % count) for i in range(count)]
    return near, far


def exchange(near_block, far_block, axis):
    near, far = swaps(lax.axis_size(axis))
    far_block = lax.ppermute(far_block, axis, far)
    return lax.ppermute(near_block, axis, near), far_block


def per_device(velocity, pressure, land_type, turbine_cells, surface_drag):
    gx = lax.axis_size("gx")
    gy = lax.axis_size("gy")
    place = jnp.stack([lax.axis_index("gx"), lax.axis_index("gy")]).astype(jnp.int32)
    near, far = call(
        pack_x,
        [shape(SIDE, B, 128), shape(SIDE, B, 128)],
        [SMEM] + [HBM] * 4,
        [
            pltpu.VMEM((B, B), jnp.int32),
            pltpu.VMEM((B, B, 128), jnp.int32),
            (B, B, 128),
            pltpu.SemaphoreType.DMA((10,)),
        ],
        60,
    )(surface_drag, land_type, velocity, pressure, turbine_cells)
    near, far = exchange(near, far, "gx")
    wide_v, wide_p, wide_d, near, far, near_p, far_p = call(
        widen_x,
        [shape(3, VX, B, 128), shape(PX, B, 128), shape(PX, B, 128)]
        + [shape(8, 40, 128)] * 2
        + [shape(N_P, 4, 128)] * 2,
        [SMEM, SMEM] + [VMEM] * 6,
    )(place, surface_drag, land_type, velocity, pressure, turbine_cells, near, far)
    near, far = exchange(near, far, "gy")
    near_p, far_p = exchange(near_p, far_p, "gy")
    star, source, near, far = call(
        advance,
        [shape(3, B, B, 128), shape(PX - 2, B, 128), shape(N_S, 4, 128), shape(N_S, 4, 128)],
        [SMEM] + [VMEM] * 4,
        [(3, VX, 24, 128), (VX, 24, 128), (3, VX, 24, 128), (3, VX, 24, 128)],
    )(place, wide_v, wide_d, near, far)
    near, far = exchange(near, far, "gy")
    finest, right, packed_one, packed_two = call(
        presmooth,
        [shape(22, 24, 128), shape(20, 24, 128), shape(2, B, 128), shape(gx, 4, 128)],
        [SMEM] + [VMEM] * 6,
        [(PX, 32, 128)] * 3 + [(12, 32, 128)] * 3,
    )(place, source, wide_p, near, far, near_p, far_p)
    near, far = exchange(packed_one, packed_one, "gx")
    blocks = lax.all_to_all(packed_two, "gx", 0, 0, tiled=True)
    strips, window = call(
        lambda *refs: pack_y(gx, *refs),
        [shape(gy, N_STRIP, 4, 128), shape(6, B, 128)],
        [SMEM] + [VMEM] * 4,
    )(place, blocks, packed_one, near, far)
    strips = lax.all_to_all(strips, "gy", 0, 0, tiled=True)
    velocity_new, pressure_new = call(
        finish,
        [shape(3, B, B, 128), shape(B, B, 128)],
        [SMEM] + [VMEM] * 5,
        [(9, 32, 128)] * 6
        + [(6, 40, 128)]
        + [(24, 40, 128)] * 3
        + [(24, 32, 128)] * 2
        + [(8, 32, 128)]
        + [(22, 24, 128)] * 2,
    )(place, strips, window, finest, right, star)
    return velocity_new, pressure_new


def solution(mesh):
    in_specs = (
        P(None, "gx", "gy", None),
        P("gx", "gy", None),
        P("gx", "gy"),
        P("gx", "gy", None),
        P(),
    )
    out_specs = (P(None, "gx", "gy", None), P("gx", "gy", None))
    return jax.shard_map(
        per_device, mesh=mesh, in_specs=in_specs, out_specs=out_specs, check_vma=False
    )
```

```python
import jax
import jax.numpy as jnp
from jax import lax
from jax.experimental import pallas as pl
from jax.experimental.pallas import tpu as pltpu
from jax.sharding import PartitionSpec as P

VH = 9
PH = 7
B = 16
VX = B + 2 * VH
PX = B + 2 * PH
SIDE = 3 * VH + 2 * PH
STEP = 0.1
ROWS = 8
EDDY = 0.03
COEFF = 0.8 / 12.0
WINDOW = 4
VMEM = pl.BlockSpec(memory_space=pltpu.VMEM)
SMEM = pl.BlockSpec(memory_space=pltpu.SMEM)
HBM = pl.BlockSpec(memory_space=pltpu.HBM)
S_UNITS = ((0, 5, 18, True), (18, 5, 18, False), (36, 1, 4, False), (40, 23, 4, False))
P_UNITS = ((0, 5, 20, True), (20, 5, 20, False), (40, 1, 4, False), (44, 25, 4, False))
N_S = 44
N_P = 48
F32 = jnp.float32


def shape(*dims):
    return jax.ShapeDtypeStruct(dims, F32)


def call(body, outs, specs, scratch=(), grant=48, out_space=None):
    return pl.pallas_call(
        body,
        out_shape=outs,
        in_specs=specs,
        out_specs=[out_space or VMEM] * len(outs),
        scratch_shapes=[pltpu.VMEM(s, F32) if isinstance(s, tuple) else s for s in scratch],
        compiler_params=pltpu.CompilerParams(vmem_limit_bytes=grant * 1024 * 1024),
    )


def iota(like, dim):
    return lax.broadcasted_iota(jnp.int32, like.shape, dim)


def lane_of(values):
    return iota(values, values.ndim - 1)


def row_of(values):
    return iota(values, values.ndim - 2)


def turn(values, amount, dim):
    return pltpu.roll(values, amount % values.shape[dim], dim)


def ground_columns(kinds, drag_table):
    ground = jnp.zeros(kinds.shape, F32)
    for kind in range(16):
        ground = jnp.where(kinds == kind, drag_table[kind], ground)
    square = lax.broadcasted_iota(jnp.int32, (B, B), 0) == lax.broadcasted_iota(jnp.int32, (B, B), 1)
    columns = []
    for i in range(B):
        row = jnp.broadcast_to(ground[i : i + 1, :], (B, B))
        columns.append(jnp.sum(jnp.where(square, row, 0.0), axis=1, keepdims=True))
    return columns


def drag_row(cells, column):
    return 2.0 * cells.astype(F32) + jnp.where(lane_of(cells) == 0, column, 0.0)


def edge_units(units, field, up, down):
    for message, outer, inner in ((up, B - 4, B - 8), (down, 0, 4)):
        for unit, start, count, deep in units:
            first = inner if deep else outer
            message[unit : unit + count] = field[start : start + count, first : first + 4, :]


def place_units(units, field, shift, low, high):
    for unit, start, count, deep in units:
        rows = slice(start + shift, start + shift + count)
        first = B + 4 if deep else B
        field[rows, first : first + 4, :] = high[unit : unit + count]
        first = B + 8 if deep else B + 12
        field[rows, first : first + 4, :] = low[unit : unit + count]


def pack_x(drag_hbm, land, velocity, pressure, turbine, near, far, drag_table, kinds_ref, cells_ref, drag, sems):
    core = lax.axis_index("gx") % 2
    copies = [
        pltpu.make_async_copy(turbine, cells_ref, sems.at[0]),
        pltpu.make_async_copy(land, kinds_ref, sems.at[1]),
        pltpu.make_async_copy(drag_hbm, drag_table, sems.at[10]),
    ]
    for side, out in ((0, near), (1, far)):
        high = (core + side) % 2 == 0
        start = jnp.where(high, B - VH, 0)
        for a in range(3):
            copies.append(
                pltpu.make_async_copy(
                    velocity.at[a, pl.ds(start, VH)], out.at[pl.ds(a * VH, VH)], sems.at[2 + 4 * side + a]
                )
            )
        start = jnp.where(high, B - PH, 0)
        copies.append(
            pltpu.make_async_copy(
                pressure.at[pl.ds(start, PH)], out.at[pl.ds(3 * VH, PH)], sems.at[5 + 4 * side]
            )
        )
    for copy in copies:
        copy.start()
    copies[1].wait()
    copies[2].wait()
    columns = ground_columns(kinds_ref[...], drag_table)
    copies[0].wait()
    for i in range(B):
        drag[i] = drag_row(cells_ref[i], columns[i])

    @pl.when(core == 0)
    def _():
        near[3 * VH + PH : SIDE] = drag[B - PH :]
        far[3 * VH + PH : SIDE] = drag[:PH]

    @pl.when(core == 1)
    def _():
        near[3 * VH + PH : SIDE] = drag[:PH]
        far[3 * VH + PH : SIDE] = drag[B - PH :]

    for copy in copies[3:]:
        copy.wait()


def widen_x(place, drag_table, land, velocity, pressure, turbine, near, far, wide_v, wide_p, wide_d, near_y, far_y, near_p, far_p):
    core = place[0] % 2
    odd = place[1] % 2
    columns = ground_columns(land[...], drag_table)
    for i in range(B):
        wide_d[PH + i] = drag_row(turbine[i], columns[i])
    for a in range(3):
        wide_v[a, VH : VH + B] = velocity[a]
    wide_p[PH : PH + B] = pressure[...]

    def fill(low, high):
        for a in range(3):
            wide_v[a, :VH] = low[a * VH : (a + 1) * VH]
            wide_v[a, VH + B :] = high[a * VH : (a + 1) * VH]
        wide_p[:PH] = low[3 * VH : 3 * VH + PH]
        wide_p[PH + B :] = high[3 * VH : 3 * VH + PH]
        wide_d[:PH] = low[3 * VH + PH :]
        wide_d[PH + B :] = high[3 * VH + PH :]

    @pl.when(core == 0)
    def _():
        fill(far, near)

    @pl.when(core == 1)
    def _():
        fill(near, far)

    def send(up, down):
        for g in range(8):
            for j in range(4):
                x = 1 + 4 * g + j
                for a in range(3):
                    rows = slice(10 * j + 3 * a, 10 * j + 3 * a + 3)
                    up[g, rows, :] = wide_v[a, x, B - 3 :, :]
                    down[g, rows, :] = wide_v[a, x, :3, :]
                row = slice(10 * j + 9, 10 * j + 10)
                d = min(max(x - 2, 0), PX - 1)
                up[g, row, :] = wide_d[d, B - 1 :, :]
                down[g, row, :] = wide_d[d, 0:1, :]

    @pl.when(odd == 0)
    def _():
        send(near_y, far_y)
        edge_units(P_UNITS, wide_p, near_p, far_p)

    @pl.when(odd == 1)
    def _():
        send(far_y, near_y)
        edge_units(P_UNITS, wide_p, far_p, near_p)


def exact_product(values, matrix):
    flat = values.reshape(-1, 128)
    high = flat.astype(jnp.bfloat16)
    rest = flat - high.astype(F32)
    middle = rest.astype(jnp.bfloat16)
    low = (rest - middle.astype(F32)).astype(jnp.bfloat16)
    parts = jnp.concatenate([high, middle, low], axis=1)
    return jnp.dot(parts, matrix, preferred_element_type=F32).reshape(values.shape)


def column_difference():
    i = lax.broadcasted_iota(jnp.int32, (128, 128), 0)
    j = lax.broadcasted_iota(jnp.int32, (128, 128), 1)
    one = jnp.where(i - j == 1, 1.0, jnp.where(j - i == 1, -1.0, 0.0))
    return jnp.concatenate([one.astype(jnp.bfloat16)] * 3, axis=0)


def advance(place, wide_v, wide_d, near, far, star, source, near_y, far_y, v, dr, tau, part):
    odd = place[1] % 2
    v[:, :, 0:B, :] = wide_v[...]
    dr[2 : 2 + PX, 0:B, :] = wide_d[...]

    def fill(low, high):
        for g in range(8):
            for j in range(4):
                x = 1 + 4 * g + j
                for a in range(3):
                    rows = slice(10 * j + 3 * a, 10 * j + 3 * a + 3)
                    v[a, x, B : B + 3, :] = high[g, rows, :]
                    v[a, x, B + 5 : B + 8, :] = low[g, rows, :]
                if 2 <= x < 2 + PX:
                    row = slice(10 * j + 9, 10 * j + 10)
                    dr[x, B : B + 1, :] = high[g, row, :]
                    dr[x, B + 7 : B + 8, :] = low[g, row, :]

    @pl.when(odd == 0)
    def _():
        fill(far, near)

    @pl.when(odd == 1)
    def _():
        fill(near, far)

    difference = column_difference()

    def along_column(fields):
        n = fields[0].shape[0]
        whole = exact_product(jnp.concatenate(fields, axis=0), difference)
        return [whole[k * n : (k + 1) * n] for k in range(len(fields))]

    def along_row(values):
        return 0.5 * (turn(values, -1, 1) - turn(values, 1, 1))

    for i in range(1, VX - 1, ROWS):
        here = slice(i, i + ROWS)
        u = [v[a, here] for a in range(3)]
        gx = [0.5 * (v[a, i + 1 : i + 1 + ROWS] - v[a, i - 1 : i - 1 + ROWS]) for a in range(3)]
        gy = [along_row(u[a]) for a in range(3)]
        gz = along_column(u)
        e01 = gx[1] + gy[0]
        e02 = gx[2] + gz[0]
        e12 = gy[2] + gz[1]
        total = 2.0 * (gx[0] * gx[0] + gy[1] * gy[1] + gz[2] * gz[2]) + (
            e01 * e01 + e02 * e02 + e12 * e12
        )
        visc = EDDY * jnp.sqrt(total)
        t01 = visc * e01
        t02 = visc * e02
        t12 = visc * e12
        tau[0, here] = 2.0 * visc * gx[0]
        tau[1, here] = t01
        tau[2, here] = t02
        along_y = [along_row(t) for t in (t01, 2.0 * visc * gy[1], t12)]
        along_z = along_column([t02, t12, 2.0 * visc * gz[2]])
        lane = lane_of(u[0])
        flat = u[0] * u[0] + u[1] * u[1]
        edge = jnp.where((lane == 0) | (lane == 127), EDDY * jnp.sqrt(flat + 2.0 * (u[2] * u[2])), 0.0)
        wind = dr[here] * jnp.sqrt(flat)
        for a in range(3):
            change = along_y[a] + (along_z[a] - (edge * u[a] if a < 2 else 2.0 * (edge * u[a])))
            change = change - (u[0] * gx[a] + u[1] * gy[a] + u[2] * gz[a])
            if a < 2:
                change = change - wind * u[a]
            if a == 0:
                change = change + 1.0
            part[a, here] = u[a] + STEP * change
    for i in range(2, VX - 2):
        for a in range(3):
            part[a, i] = part[a, i] + (0.5 * STEP) * (tau[a, i + 1] - tau[a, i - 1])
    for a in range(3):
        star[a] = part[a, VH : VH + B, 0:B, :]
    for i in range(3, VX - 3, 4):
        along_x = 0.5 * (part[0, i + 1 : i + 5] - part[0, i - 1 : i + 3])
        along_y = along_row(part[1, i : i + 4])
        (along_z,) = along_column([part[2, i : i + 4, 0:B, :]])
        source[i - 3 : i + 1] = ((along_x + along_y)[:, 0:B] + along_z) / STEP

    @pl.when(odd == 0)
    def _():
        edge_units(S_UNITS, source, near_y, far_y)

    @pl.when(odd == 1)
    def _():
        edge_units(S_UNITS, source, far_y, near_y)


def column_sum(dz, halves):
    i = lax.broadcasted_iota(jnp.int32, (128, 128), 0)
    j = lax.broadcasted_iota(jnp.int32, (128, 128), 1)
    hit = (i - j == dz) | (j - i == dz) | ((i == j) & ((j < dz) | (j >= 128 - dz)))
    return jnp.concatenate([jnp.where(hit, 4.0, 0.0).astype(jnp.bfloat16)] * halves, axis=0)


def neighbours(ref, start, count, dy, dz, matrix=None):
    p = ref[start : start + count]
    sides = ref[start - 1 : start - 1 + count] + ref[start + 1 : start + 1 + count]
    sides = sides + (turn(p, dy, 1) + turn(p, -dy, 1))
    if matrix is not None:
        return p, sides + exact_product(p, matrix)
    lane = lane_of(p)
    below = jnp.where(lane < dz, p, turn(p, dz, 2))
    above = jnp.where(lane >= 128 - dz, p, turn(p, -dz, 2))
    return p, sides + 4.0 * (below + above)


def chunks(first, last, size=2):
    return [(i, min(size, last - i)) for i in range(first, last, size)]


def sweep(dst, src, right, first, last, dy, dz, offset=0, matrix=None):
    for i, n in chunks(first, last, 2 if matrix is None else 4):
        p, around = neighbours(src, i, n, dy, dz, matrix)
        dst[i : i + n] = 0.2 * p + COEFF * (around - right[i - offset : i - offset + n])


def scaled_residual(src, right, i, n, dy, dz, matrix=None):
    p, around = neighbours(src, i, n, dy, dz, matrix)
    return right[i : i + n] - around + 12.0 * p


def coarsen_pair(pair, dy, dz):
    total = pair[0] + pair[1]
    lane = lane_of(total)
    total = total + jnp.where((lane & dz) == 0, turn(total, -dz, 1), turn(total, dz, 1))
    row = row_of(total)
    total = total + jnp.where((row & dy) == 0, turn(total, -dy, 0), turn(total, dy, 0))
    return 0.5 * total


def presmooth(place, source, wide_p, near, far, near_p, far_p, finest, right, packed_one, packed_two, p, s, q, f1, a1, b1):
    odd = place[1] % 2
    p[:, 0:B, :] = wide_p[...]
    s[1 : PX - 1, 0:B, :] = source[...]

    @pl.when(odd == 0)
    def _():
        place_units(S_UNITS, s, 1, far, near)
        place_units(P_UNITS, p, 0, far_p, near_p)

    @pl.when(odd == 1)
    def _():
        place_units(S_UNITS, s, 1, near, far)
        place_units(P_UNITS, p, 0, near_p, far_p)

    fine = column_sum(1, 3)
    coarse = column_sum(2, 3)
    sweep(q, p, s, 1, PX - 1, 1, 1, 0, fine)
    sweep(p, q, s, 2, PX - 2, 1, 1, 0, fine)
    for out, field, first in ((finest, p, 4), (right, s, 5)):
        out[:, 0:B, :] = field[first : PX - first, 0:B, :]
        out[:, B : B + 4, :] = field[first : PX - first, B : B + 4, :]
        out[:, B + 4 : B + 8, :] = field[first : PX - first, B + 12 : B + 16, :]
    for k in range(0, 12, 2):
        rows = scaled_residual(p, s, 3 + 2 * k, 4, 1, 1, fine)
        f1[k] = coarsen_pair(rows[0:2], 1, 1)
        f1[k + 1] = coarsen_pair(rows[2:4], 1, 1)
    a1[...] = -COEFF * f1[...]
    sweep(b1, a1, f1, 1, 11, 2, 2, 0, coarse)
    rows = scaled_residual(b1, f1, 2, 8, 2, 2, coarse)
    f2 = [coarsen_pair(rows[2 * k : 2 * k + 2], 2, 2) for k in range(4)]
    lane = lane_of(f2[0]) & 3
    two = jnp.where(lane == 0, f2[0], jnp.where(lane == 1, f2[1], jnp.where(lane == 2, f2[2], f2[3])))
    four = jnp.concatenate([two[4 * y : 4 * y + 1, :] for y in range(4)], axis=0)
    for k in range(packed_two.shape[0]):
        packed_two[k] = four
    for g in range(2):
        rows = [f1[2 + 4 * g + j][0:B] for j in range(4)]
        slot = 2 * (row_of(rows[0]) & 1) + (lane_of(rows[0]) & 1)
        packed_one[g] = jnp.where(
            slot == 0, rows[0], jnp.where(slot == 1, rows[1], jnp.where(slot == 2, rows[2], rows[3]))
        )


GROUPS = ((9, 1, 2), (11, 2, 3), (14, 3, 3), (17, 4, 2))
N_STRIP = 19


def pack_y(peers, place, blocks, own, near, far, strips, window):
    core = place[0] % 2
    gy = place[1]
    for j in range(2 * WINDOW + 1):
        piece = blocks[(place[0] + (peers - WINDOW + j)) % peers]
        for k in range(8):
            strips[k, j] = piece
    window[2:4] = own[...]

    def fill(low, high):
        window[0:2] = low[...]
        window[4:6] = high[...]

    @pl.when(core == 0)
    def _():
        fill(far, near)

    @pl.when(core == 1)
    def _():
        fill(near, far)

    for step in range(1, 8):
        peer = (gy + step) % 8
        for unit, group, count in GROUPS:
            for k in range(count):
                first = 4 * k if step == 7 else B - 4 * (count - k)
                strips[peer, unit + k] = window[group, first : first + 4, :]
    for k in range(9, N_STRIP):
        strips[gy, k] = jnp.zeros((4, 128), F32)


def packed_neighbours(ref, b, dx, dy, dz):
    p = ref[b]
    before = ref[max(b - 1, 0)]
    after = ref[min(b + 1, 2 * WINDOW)]
    lane = lane_of(p)
    slot = lane & 3
    left = jnp.where(slot < dx, turn(before, dx - 4, 1), turn(p, dx, 1))
    right = jnp.where(slot >= 4 - dx, turn(after, 4 - dx, 1), turn(p, -dx, 1))
    below = jnp.where(lane < dz, p, turn(p, dz, 1))
    above = jnp.where(lane >= 128 - dz, p, turn(p, -dz, 1))
    return p, (left + right) + (turn(p, dy, 0) + turn(p, -dy, 0)) + 4.0 * (below + above)


def packed_sweep(dst, src, right, blocks, dx, dy, dz):
    for b in blocks:
        p, around = packed_neighbours(src, b, dx, dy, dz)
        dst[b] = 0.2 * p + COEFF * (around - right[b])


def packed_residual(src, right, b, dx, dy, dz):
    p, around = packed_neighbours(src, b, dx, dy, dz)
    return right[b] - around + 12.0 * p


def without_middle(values):
    return jnp.concatenate([values[..., 0:24, :], values[..., 32:40, :]], axis=-2)


def finish(place, strips, window, finest, right, star, velocity_new, pressure_new, f2, a2, b2, f3, a3, b3, g1, f1, a1, b1, c1, d1, e1, p0, q0):
    gy = place[1]
    for j in range(8):
        peer = (gy + j) % 8
        for b in range(2 * WINDOW + 1):
            f2[b, 4 * j : 4 * j + 4, :] = strips[peer, b]
    for b in range(9):
        a2[b] = -COEFF * f2[b]
    packed_sweep(b2, a2, f2, range(9), 1, 1, 4)
    for b in range(1, 8):
        total = packed_residual(b2, f2, b, 1, 1, 4)
        lane = lane_of(total)
        total = total + jnp.where((lane & 1) == 0, turn(total, -1, 1), turn(total, 1, 1))
        total = total + jnp.where((lane & 4) == 0, turn(total, -4, 1), turn(total, 4, 1))
        row = row_of(total)
        total = total + jnp.where((row & 1) == 0, turn(total, -1, 0), turn(total, 1, 0))
        f3[b] = 0.5 * total
        a3[b] = (-0.5 * COEFF) * total
    packed_sweep(b3, a3, f3, range(1, 8), 2, 2, 8)
    packed_sweep(a3, b3, f3, range(2, 7), 2, 2, 8)
    packed_sweep(b3, a3, f3, range(2, 7), 2, 2, 8)
    for b in range(3, 6):
        line = jnp.sum(packed_residual(b3, f3, b, 2, 2, 8), axis=0, keepdims=True) * (COEFF / 32.0)
        a2[b] = b2[b] + (b3[b] - line)
    packed_sweep(b2, a2, f2, range(3, 6), 1, 1, 4)
    packed_sweep(a2, b2, f2, range(3, 6), 1, 1, 4)
    g1[:, 0:B, :] = window[...]
    for unit, group, count in GROUPS:
        for k in range(count):
            first = B + 4 * k
            g1[group, first : first + 4, :] = strips[(gy + 1) % 8, unit + k]
            first = B + 24 - 4 * (count - k)
            g1[group, first : first + 4, :] = strips[(gy + 7) % 8, unit + k]
    for x in range(3, 21):
        packed = g1[x // 4]
        slots = 2 * (row_of(packed) & 1) + (lane_of(packed) & 1)
        slot = x % 4
        part = jnp.where(slots == slot, packed, 0.0)
        part = part + turn(part, 1 if slot % 2 == 0 else -1, 1)
        part = part + turn(part, 1 if slot < 2 else -1, 0)
        f1[x] = part
        a1[x] = -COEFF * part
    sweep(b1, a1, f1, 4, 20, 2, 2)
    for k in range(8):
        block = a2[3 + (k + 2) // 4]
        slot = (k + 2) % 4
        low, high = block[0:8], block[24:32]
        part = jnp.where(row_of(low) < 6, low, high)
        part = jnp.where((lane_of(part) & 3) == slot, part, 0.0)
        part = part + turn(part, 1 if slot % 2 == 0 else -1, 1)
        part = part + turn(part, 2 if slot < 2 else -2, 1)
        for q in range(8):
            e1[k, 4 * q : 4 * q + 4, :] = jnp.broadcast_to(part[q : q + 1, :], (4, 128))
    for r in range(4, 20):
        c1[r] = without_middle(b1[r]) + e1[(r - 4) // 2]
    for dst, src, first, last in ((d1, c1, 5, 19), (c1, d1, 6, 18)):
        for i, n in chunks(first, last):
            p, around = neighbours(src, i, n, 2, 2)
            dst[i : i + n] = 0.2 * p + COEFF * (around - without_middle(f1[i : i + n]))
    for i in range(22):
        coarse = c1[6 + (i + 1) // 2]
        edge = coarse[16:24]
        p0[i, 0:B, :] = finest[i, 0:B, :] + coarse[0:B]
        p0[i, B:, :] = finest[i, B:, :] + jnp.where(row_of(edge) < 4, edge, coarse[24:32])
    sweep(q0, p0, right, 1, 21, 1, 1, 1)
    sweep(p0, q0, right, 2, 20, 1, 1, 1)
    for i in range(B):
        p = p0[3 + i]
        lane = lane_of(p)
        above = jnp.where(lane == 127, p, turn(p, -1, 1))
        below = jnp.where(lane == 0, p, turn(p, 1, 1))
        along_x = p0[4 + i] - p0[2 + i]
        along_y = turn(p, -1, 0) - turn(p, 1, 0)
        velocity_new[0, i] = star[0, i] - (0.5 * STEP) * along_x[0:B]
        velocity_new[1, i] = star[1, i] - (0.5 * STEP) * along_y[0:B]
        velocity_new[2, i] = star[2, i] - STEP * (above - below)[0:B]
        pressure_new[i] = p[0:B]


def swaps(count):
    near = [(i, i ^ 1) for i in range(count)]
    far = [(i, (((i + 1) ^ 1) - 1) % count) for i in range(count)]
    return near, far


def exchange(near_block, far_block, axis):
    near, far = swaps(lax.axis_size(axis))
    far_block = lax.ppermute(far_block, axis, far)
    return lax.ppermute(near_block, axis, near), far_block


def per_device(velocity, pressure, land_type, turbine_cells, surface_drag):
    gx = lax.axis_size("gx")
    gy = lax.axis_size("gy")
    place = jnp.stack([lax.axis_index("gx"), lax.axis_index("gy")]).astype(jnp.int32)
    staged = (surface_drag, land_type, velocity, pressure, turbine_cells)
    near, far = call(
        pack_x,
        [shape(SIDE, B, 128), shape(SIDE, B, 128)],
        [HBM] * 5,
        [
            pltpu.SMEM((16,), F32),
            pltpu.VMEM((B, B), jnp.int32),
            pltpu.VMEM((B, B, 128), jnp.int32),
            (B, B, 128),
            pltpu.SemaphoreType.DMA((11,)),
        ],
    )(*[pltpu.with_memory_space_constraint(x, pltpu.HBM) for x in staged])
    near, far = exchange(near, far, "gx")
    wide_v, wide_p, wide_d, near, far, near_p, far_p = call(
        widen_x,
        [shape(3, VX, B, 128), shape(PX, B, 128), shape(PX, B, 128)]
        + [shape(8, 40, 128)] * 2
        + [shape(N_P, 4, 128)] * 2,
        [SMEM, SMEM] + [VMEM] * 6,
    )(place, surface_drag, land_type, velocity, pressure, turbine_cells, near, far)
    near, far = exchange(near, far, "gy")
    near_p, far_p = exchange(near_p, far_p, "gy")
    star, source, near, far = call(
        advance,
        [shape(3, B, B, 128), shape(PX - 2, B, 128), shape(N_S, 4, 128), shape(N_S, 4, 128)],
        [SMEM] + [VMEM] * 4,
        [(3, VX, 24, 128), (VX, 24, 128), (3, VX, 24, 128), (3, VX, 24, 128)],
    )(place, wide_v, wide_d, near, far)
    near, far = exchange(near, far, "gy")
    finest, right, packed_one, packed_two = call(
        presmooth,
        [shape(22, 24, 128), shape(20, 24, 128), shape(2, B, 128), shape(gx, 4, 128)],
        [SMEM] + [VMEM] * 6,
        [(PX, 32, 128)] * 3 + [(12, 32, 128)] * 3,
    )(place, source, wide_p, near, far, near_p, far_p)
    near, far = exchange(packed_one, packed_one, "gx")
    blocks = lax.all_to_all(packed_two, "gx", 0, 0, tiled=True)
    strips, window = call(
        lambda *refs: pack_y(gx, *refs),
        [shape(gy, N_STRIP, 4, 128), shape(6, B, 128)],
        [SMEM] + [VMEM] * 4,
    )(place, blocks, packed_one, near, far)
    strips = lax.all_to_all(strips, "gy", 0, 0, tiled=True)
    velocity_new, pressure_new = call(
        finish,
        [shape(3, B, B, 128), shape(B, B, 128)],
        [SMEM] + [VMEM] * 5,
        [(9, 32, 128)] * 6
        + [(6, 40, 128)]
        + [(24, 40, 128)] * 3
        + [(24, 32, 128)] * 2
        + [(8, 32, 128)]
        + [(22, 24, 128)] * 2,
    )(place, strips, window, finest, right, star)
    return velocity_new, pressure_new


def solution(mesh):
    in_specs = (
        P(None, "gx", "gy", None),
        P("gx", "gy", None),
        P("gx", "gy"),
        P("gx", "gy", None),
        P(),
    )
    out_specs = (P(None, "gx", "gy", None), P("gx", "gy", None))
    return jax.shard_map(
        per_device, mesh=mesh, in_specs=in_specs, out_specs=out_specs, check_vma=False
    )
```

```python
import jax
import numpy as np
import jax.numpy as jnp
from jax import lax
from jax.experimental import pallas as pl
from jax.experimental.pallas import tpu as pltpu
from jax.sharding import PartitionSpec as P

VH = 9
PH = 7
B = 16
VX = B + 2 * VH
PX = B + 2 * PH
SIDE = 3 * VH + 2 * PH
STEP = 0.1
ROWS = 8
EDDY = 0.03
COEFF = 0.8 / 12.0
WINDOW = 4
VMEM = pl.BlockSpec(memory_space=pltpu.VMEM)
SMEM = pl.BlockSpec(memory_space=pltpu.SMEM)
HBM = pl.BlockSpec(memory_space=pltpu.HBM)
S_ROWS = [(6 * i, 6, 5 + i) for i in range(18)] + [(108 + 4 * i, 4, x) for i, x in enumerate((1, 2, 3, 4, 23, 24, 25, 26))]
P_UNITS = ((0, 5, 20, True), (20, 5, 20, False), (40, 1, 4, False), (44, 25, 4, False))
N_S = 144
N_P = 48
F32 = jnp.float32


def shape(*dims):
    return jax.ShapeDtypeStruct(dims, F32)


def call(body, outs, specs, scratch=(), grant=48, out_space=None):
    return pl.pallas_call(
        body,
        out_shape=outs,
        in_specs=specs,
        out_specs=[out_space or VMEM] * len(outs),
        scratch_shapes=[pltpu.VMEM(s, F32) if isinstance(s, tuple) else s for s in scratch],
        compiler_params=pltpu.CompilerParams(vmem_limit_bytes=grant * 1024 * 1024),
    )


def iota(like, dim):
    return lax.broadcasted_iota(jnp.int32, like.shape, dim)


def lane_of(values):
    return iota(values, values.ndim - 1)


def row_of(values):
    return iota(values, values.ndim - 2)


def turn(values, amount, dim):
    return pltpu.roll(values, amount % values.shape[dim], dim)


def ground_columns(kinds, drag_table):
    ground = jnp.zeros(kinds.shape, F32)
    for kind in range(16):
        ground = jnp.where(kinds == kind, drag_table[kind], ground)
    square = lax.broadcasted_iota(jnp.int32, (B, B), 0) == lax.broadcasted_iota(jnp.int32, (B, B), 1)
    columns = []
    for i in range(B):
        row = jnp.broadcast_to(ground[i : i + 1, :], (B, B))
        columns.append(jnp.sum(jnp.where(square, row, 0.0), axis=1, keepdims=True))
    return columns


def drag_row(cells, column):
    return 2.0 * cells.astype(F32) + jnp.where(lane_of(cells) == 0, column, 0.0)


def edge_units(units, field, up, down):
    for message, outer, inner in ((up, B - 4, B - 8), (down, 0, 4)):
        for unit, start, count, deep in units:
            first = inner if deep else outer
            message[unit : unit + count] = field[start : start + count, first : first + 4, :]


def place_units(units, field, shift, low, high):
    for unit, start, count, deep in units:
        rows = slice(start + shift, start + shift + count)
        first = B + 4 if deep else B
        field[rows, first : first + 4, :] = high[unit : unit + count]
        first = B + 8 if deep else B + 12
        field[rows, first : first + 4, :] = low[unit : unit + count]


def pack_x(drag_hbm, land, velocity, pressure, turbine, near, far, drag_table, kinds_ref, cells_ref, drag, sems):
    core = lax.axis_index("gx") % 2
    copies = [
        pltpu.make_async_copy(turbine, cells_ref, sems.at[0]),
        pltpu.make_async_copy(land, kinds_ref, sems.at[1]),
        pltpu.make_async_copy(drag_hbm, drag_table, sems.at[10]),
    ]
    for side, out in ((0, near), (1, far)):
        high = (core + side) % 2 == 0
        start = jnp.where(high, B - VH, 0)
        for a in range(3):
            copies.append(
                pltpu.make_async_copy(
                    velocity.at[a, pl.ds(start, VH)], out.at[pl.ds(a * VH, VH)], sems.at[2 + 4 * side + a]
                )
            )
        start = jnp.where(high, B - PH, 0)
        copies.append(
            pltpu.make_async_copy(
                pressure.at[pl.ds(start, PH)], out.at[pl.ds(3 * VH, PH)], sems.at[5 + 4 * side]
            )
        )
    for copy in copies:
        copy.start()
    copies[1].wait()
    copies[2].wait()
    columns = ground_columns(kinds_ref[...], drag_table)
    copies[0].wait()
    for i in range(B):
        drag[i] = drag_row(cells_ref[i], columns[i])

    @pl.when(core == 0)
    def _():
        near[3 * VH + PH : SIDE] = drag[B - PH :]
        far[3 * VH + PH : SIDE] = drag[:PH]

    @pl.when(core == 1)
    def _():
        near[3 * VH + PH : SIDE] = drag[:PH]
        far[3 * VH + PH : SIDE] = drag[B - PH :]

    for copy in copies[3:]:
        copy.wait()


def widen_x(place, drag_table, land, velocity, pressure, turbine, near, far, wide_v, wide_p, wide_d, near_y, far_y, near_p, far_p):
    core = place[0] % 2
    odd = place[1] % 2
    columns = ground_columns(land[...], drag_table)
    for i in range(B):
        wide_d[PH + i] = drag_row(turbine[i], columns[i])
    for a in range(3):
        wide_v[a, VH : VH + B] = velocity[a]
    wide_p[PH : PH + B] = pressure[...]

    def fill(low, high):
        for a in range(3):
            wide_v[a, :VH] = low[a * VH : (a + 1) * VH]
            wide_v[a, VH + B :] = high[a * VH : (a + 1) * VH]
        wide_p[:PH] = low[3 * VH : 3 * VH + PH]
        wide_p[PH + B :] = high[3 * VH : 3 * VH + PH]
        wide_d[:PH] = low[3 * VH + PH :]
        wide_d[PH + B :] = high[3 * VH + PH :]

    @pl.when(core == 0)
    def _():
        fill(far, near)

    @pl.when(core == 1)
    def _():
        fill(near, far)

    def send(up, down):
        for g in range(8):
            for j in range(4):
                x = 1 + 4 * g + j
                for a in range(3):
                    rows = slice(10 * j + 3 * a, 10 * j + 3 * a + 3)
                    up[g, rows, :] = wide_v[a, x, B - 3 :, :]
                    down[g, rows, :] = wide_v[a, x, :3, :]
                row = slice(10 * j + 9, 10 * j + 10)
                d = min(max(x - 2, 0), PX - 1)
                up[g, row, :] = wide_d[d, B - 1 :, :]
                down[g, row, :] = wide_d[d, 0:1, :]

    @pl.when(odd == 0)
    def _():
        send(near_y, far_y)
        edge_units(P_UNITS, wide_p, near_p, far_p)

    @pl.when(odd == 1)
    def _():
        send(far_y, near_y)
        edge_units(P_UNITS, wide_p, far_p, near_p)


def three_parts(flat):
    high = flat.astype(jnp.bfloat16)
    rest = flat - high.astype(F32)
    middle = rest.astype(jnp.bfloat16)
    low = (rest - middle.astype(F32)).astype(jnp.bfloat16)
    return jnp.concatenate([high, middle, low], axis=1)


def exact_product(values, matrix):
    parts = three_parts(values.reshape(-1, 128))
    return jnp.dot(parts, matrix, preferred_element_type=F32).reshape(values.shape)


def column_difference():
    i = lax.broadcasted_iota(jnp.int32, (128, 128), 0)
    j = lax.broadcasted_iota(jnp.int32, (128, 128), 1)
    one = jnp.where(i - j == 1, 1.0, jnp.where(j - i == 1, -1.0, 0.0))
    return jnp.concatenate([one.astype(jnp.bfloat16)] * 3, axis=0)


def advance(place, wide_v, wide_d, near, far, star, source, near_y, far_y, v, dr, tau, part):
    odd = place[1] % 2
    v[:, :, 0:B, :] = wide_v[...]
    dr[2 : 2 + PX, 0:B, :] = wide_d[...]

    def fill(low, high):
        for g in range(8):
            for j in range(4):
                x = 1 + 4 * g + j
                for a in range(3):
                    rows = slice(10 * j + 3 * a, 10 * j + 3 * a + 3)
                    v[a, x, B : B + 3, :] = high[g, rows, :]
                    v[a, x, B + 5 : B + 8, :] = low[g, rows, :]
                if 2 <= x < 2 + PX:
                    row = slice(10 * j + 9, 10 * j + 10)
                    dr[x, B : B + 1, :] = high[g, row, :]
                    dr[x, B + 7 : B + 8, :] = low[g, row, :]

    @pl.when(odd == 0)
    def _():
        fill(far, near)

    @pl.when(odd == 1)
    def _():
        fill(near, far)

    difference = column_difference()

    def along_column(fields):
        n = fields[0].shape[0]
        whole = exact_product(jnp.concatenate(fields, axis=0), difference)
        return [whole[k * n : (k + 1) * n] for k in range(len(fields))]

    def along_row(values):
        return 0.5 * (turn(values, -1, 1) - turn(values, 1, 1))

    for i in range(1, VX - 1, ROWS):
        here = slice(i, i + ROWS)
        u = [v[a, here] for a in range(3)]
        gx = [0.5 * (v[a, i + 1 : i + 1 + ROWS] - v[a, i - 1 : i - 1 + ROWS]) for a in range(3)]
        gy = [along_row(u[a]) for a in range(3)]
        gz = along_column(u)
        e01 = gx[1] + gy[0]
        e02 = gx[2] + gz[0]
        e12 = gy[2] + gz[1]
        total = 2.0 * (gx[0] * gx[0] + gy[1] * gy[1] + gz[2] * gz[2]) + (
            e01 * e01 + e02 * e02 + e12 * e12
        )
        visc = EDDY * jnp.sqrt(total)
        t01 = visc * e01
        t02 = visc * e02
        t12 = visc * e12
        tau[0, here] = 2.0 * visc * gx[0]
        tau[1, here] = t01
        tau[2, here] = t02
        along_y = [along_row(t) for t in (t01, 2.0 * visc * gy[1], t12)]
        along_z = along_column([t02, t12, 2.0 * visc * gz[2]])
        lane = lane_of(u[0])
        flat = u[0] * u[0] + u[1] * u[1]
        edge = jnp.where((lane == 0) | (lane == 127), EDDY * jnp.sqrt(flat + 2.0 * (u[2] * u[2])), 0.0)
        wind = dr[here] * jnp.sqrt(flat)
        for a in range(3):
            change = along_y[a] + (along_z[a] - (edge * u[a] if a < 2 else 2.0 * (edge * u[a])))
            change = change - (u[0] * gx[a] + u[1] * gy[a] + u[2] * gz[a])
            if a < 2:
                change = change - wind * u[a]
            if a == 0:
                change = change + 1.0
            part[a, here] = u[a] + STEP * change
    for i in range(2, VX - 2):
        for a in range(3):
            part[a, i] = part[a, i] + (0.5 * STEP) * (tau[a, i + 1] - tau[a, i - 1])
    for a in range(3):
        star[a] = part[a, VH : VH + B, 0:B, :]
    for i in range(3, VX - 3, 4):
        along_x = 0.5 * (part[0, i + 1 : i + 5] - part[0, i - 1 : i + 3])
        along_y = along_row(part[1, i : i + 4])
        (along_z,) = along_column([part[2, i : i + 4, 0:B, :]])
        source[i - 3 : i + 1] = ((along_x + along_y)[:, 0:B] + along_z) / STEP

    def send(up, down):
        for row, count, x in S_ROWS:
            up[row : row + count, :] = source[x, B - count :, :]
            down[row : row + count, :] = source[x, :count, :]

    @pl.when(odd == 0)
    def _():
        send(near_y, far_y)

    @pl.when(odd == 1)
    def _():
        send(far_y, near_y)


def column_sum(dz, halves):
    i = lax.broadcasted_iota(jnp.int32, (128, 128), 0)
    j = lax.broadcasted_iota(jnp.int32, (128, 128), 1)
    hit = (i - j == dz) | (j - i == dz) | ((i == j) & ((j < dz) | (j >= 128 - dz)))
    return jnp.concatenate([jnp.where(hit, 4.0, 0.0).astype(jnp.bfloat16)] * halves, axis=0)


def neighbours(ref, start, count, dy, dz, matrix=None):
    p = ref[start : start + count]
    sides = ref[start - 1 : start - 1 + count] + ref[start + 1 : start + 1 + count]
    sides = sides + (turn(p, dy, 1) + turn(p, -dy, 1))
    if matrix is not None:
        return p, sides + exact_product(p, matrix)
    lane = lane_of(p)
    below = jnp.where(lane < dz, p, turn(p, dz, 2))
    above = jnp.where(lane >= 128 - dz, p, turn(p, -dz, 2))
    return p, sides + 4.0 * (below + above)


def chunks(first, last, size=2):
    return [(i, min(size, last - i)) for i in range(first, last, size)]


def sweep(dst, src, right, first, last, dy, dz, offset=0, matrix=None):
    for i, n in chunks(first, last, 2 if matrix is None else 4):
        p, around = neighbours(src, i, n, dy, dz, matrix)
        dst[i : i + n] = 0.2 * p + COEFF * (around - right[i - offset : i - offset + n])


def scaled_residual(src, right, i, n, dy, dz, matrix=None):
    p, around = neighbours(src, i, n, dy, dz, matrix)
    return right[i : i + n] - around + 12.0 * p


def coarsen_pair(pair, dy, dz):
    total = pair[0] + pair[1]
    lane = lane_of(total)
    total = total + jnp.where((lane & dz) == 0, turn(total, -dz, 1), turn(total, dz, 1))
    row = row_of(total)
    total = total + jnp.where((row & dy) == 0, turn(total, -dy, 0), turn(total, dy, 0))
    return 0.5 * total


def presmooth(place, source, wide_p, near, far, near_p, far_p, finest, right, packed_one, packed_two, p, s, q, f1, a1, b1):
    odd = place[1] % 2
    p[:, 0:B, :] = wide_p[...]
    s[1 : PX - 1, 0:B, :] = source[...]

    def place_source(low, high):
        for row, count, x in S_ROWS:
            s[x + 1, B : B + count, :] = high[row : row + count, :]
            s[x + 1, B + 16 - count : B + 16, :] = low[row : row + count, :]

    @pl.when(odd == 0)
    def _():
        place_source(far, near)
        place_units(P_UNITS, p, 0, far_p, near_p)

    @pl.when(odd == 1)
    def _():
        place_source(near, far)
        place_units(P_UNITS, p, 0, near_p, far_p)

    fine = column_sum(1, 3)
    coarse = column_sum(2, 3)
    sweep(q, p, s, 1, PX - 1, 1, 1, 0, fine)
    sweep(p, q, s, 2, PX - 2, 1, 1, 0, fine)
    for out, field, first in ((finest, p, 4), (right, s, 5)):
        out[:, 0:B, :] = field[first : PX - first, 0:B, :]
        out[:, B : B + 4, :] = field[first : PX - first, B : B + 4, :]
        out[:, B + 4 : B + 8, :] = field[first : PX - first, B + 12 : B + 16, :]
    for k in range(0, 12, 2):
        rows = scaled_residual(p, s, 3 + 2 * k, 4, 1, 1, fine)
        f1[k] = coarsen_pair(rows[0:2], 1, 1)
        f1[k + 1] = coarsen_pair(rows[2:4], 1, 1)
    a1[...] = -COEFF * f1[...]
    sweep(b1, a1, f1, 1, 11, 2, 2, 0, coarse)
    rows = scaled_residual(b1, f1, 2, 8, 2, 2, coarse)
    f2 = [coarsen_pair(rows[2 * k : 2 * k + 2], 2, 2) for k in range(4)]
    lane = lane_of(f2[0]) & 3
    two = jnp.where(lane == 0, f2[0], jnp.where(lane == 1, f2[1], jnp.where(lane == 2, f2[2], f2[3])))
    four = jnp.concatenate([two[4 * y : 4 * y + 1, :] for y in range(4)], axis=0)
    for k in range(packed_two.shape[0]):
        packed_two[k] = four
    for g in range(2):
        rows = [f1[2 + 4 * g + j][0:B] for j in range(4)]
        slot = 2 * (row_of(rows[0]) & 1) + (lane_of(rows[0]) & 1)
        packed_one[g] = jnp.where(
            slot == 0, rows[0], jnp.where(slot == 1, rows[1], jnp.where(slot == 2, rows[2], rows[3]))
        )


GROUPS = ((9, 1, 2), (11, 2, 3), (14, 3, 3), (17, 4, 2))
N_STRIP = 19


def pack_y(peers, place, blocks, own, near, far, strips, window):
    core = place[0] % 2
    gy = place[1]
    for j in range(2 * WINDOW + 1):
        piece = blocks[(place[0] + (peers - WINDOW + j)) % peers]
        for k in range(8):
            strips[k, j] = piece
    window[2:4] = own[...]

    def fill(low, high):
        window[0:2] = low[...]
        window[4:6] = high[...]

    @pl.when(core == 0)
    def _():
        fill(far, near)

    @pl.when(core == 1)
    def _():
        fill(near, far)

    for step in range(1, 8):
        peer = (gy + step) % 8
        for unit, group, count in GROUPS:
            for k in range(count):
                first = 4 * k if step == 7 else B - 4 * (count - k)
                strips[peer, unit + k] = window[group, first : first + 4, :]
    for k in range(9, N_STRIP):
        strips[gy, k] = jnp.zeros((4, 128), F32)


def packed_matrix(dx, dz):
    k = np.arange(128)[:, None]
    j = np.arange(128)[None, :]
    slot = j % 4
    own = (k == j - dx) & (slot >= dx)
    own = own.astype(np.float32) + ((k == j + dx) & (slot < 4 - dx))
    edge = (k == j) & ((j < dz) | (j >= 128 - dz))
    own = own + 4.0 * ((k == j - dz) | (k == j + dz)) + 4.0 * edge
    after = (k == j + 4 - dx) & (slot < dx)
    before = (k == j - 4 + dx) & (slot >= 4 - dx)
    whole = np.concatenate([own, after.astype(np.float32), before.astype(np.float32)], axis=1)
    return jnp.asarray(np.concatenate([whole] * 3, axis=0), jnp.bfloat16)


def packed_around(ref, first, last, dy, matrix):
    low, high = max(first - 1, 0), min(last + 1, 2 * WINDOW + 1)
    p = ref[low:high]
    flat = p.reshape(-1, 128)
    parts = three_parts(flat)
    out = jnp.dot(parts, matrix, preferred_element_type=F32)
    result = []
    for b in range(first, last):
        rows = lambda c: slice(32 * (c - low), 32 * (c - low) + 32)
        before, after = max(b - 1, low), min(b + 1, high - 1)
        sides = out[rows(b), 0:128] + (out[rows(before), 128:256] + out[rows(after), 256:384])
        own = p[b - low]
        result.append((own, sides + (turn(own, dy, 0) + turn(own, -dy, 0))))
    return result


def packed_sweep(dst, src, right, blocks, dy, matrix):
    for b, (p, around) in zip(blocks, packed_around(src, blocks[0], blocks[-1] + 1, dy, matrix)):
        dst[b] = 0.2 * p + COEFF * (around - right[b])


def packed_residual(src, right, blocks, dy, matrix):
    rows = packed_around(src, blocks[0], blocks[-1] + 1, dy, matrix)
    return [right[b] - around + 12.0 * p for b, (p, around) in zip(blocks, rows)]


def without_middle(values):
    return jnp.concatenate([values[..., 0:24, :], values[..., 32:40, :]], axis=-2)


def finish(place, strips, window, finest, right, star, second, third, velocity_new, pressure_new, f2, a2, b2, f3, a3, b3, g1, f1, a1, b1, c1, d1, e1, p0, q0):
    gy = place[1]
    for j in range(8):
        peer = (gy + j) % 8
        for b in range(2 * WINDOW + 1):
            f2[b, 4 * j : 4 * j + 4, :] = strips[peer, b]
    for b in range(9):
        a2[b] = -COEFF * f2[b]
    packed_sweep(b2, a2, f2, range(9), 1, second[...])
    for b, total in zip(range(1, 8), packed_residual(b2, f2, range(1, 8), 1, second[...])):
        lane = lane_of(total)
        total = total + jnp.where((lane & 1) == 0, turn(total, -1, 1), turn(total, 1, 1))
        total = total + jnp.where((lane & 4) == 0, turn(total, -4, 1), turn(total, 4, 1))
        row = row_of(total)
        total = total + jnp.where((row & 1) == 0, turn(total, -1, 0), turn(total, 1, 0))
        f3[b] = 0.5 * total
        a3[b] = (-0.5 * COEFF) * total
    for b in (0, 8):
        a3[b] = jnp.zeros((32, 128), F32)
        b3[b] = jnp.zeros((32, 128), F32)
    packed_sweep(b3, a3, f3, range(1, 8), 2, third[...])
    packed_sweep(a3, b3, f3, range(2, 7), 2, third[...])
    packed_sweep(b3, a3, f3, range(2, 7), 2, third[...])
    for b, total in zip(range(3, 6), packed_residual(b3, f3, range(3, 6), 2, third[...])):
        line = jnp.sum(total, axis=0, keepdims=True) * (COEFF / 32.0)
        a2[b] = b2[b] + (b3[b] - line)
    packed_sweep(b2, a2, f2, range(3, 6), 1, second[...])
    packed_sweep(a2, b2, f2, range(3, 6), 1, second[...])
    g1[:, 0:B, :] = window[...]
    for unit, group, count in GROUPS:
        for k in range(count):
            first = B + 4 * k
            g1[group, first : first + 4, :] = strips[(gy + 1) % 8, unit + k]
            first = B + 24 - 4 * (count - k)
            g1[group, first : first + 4, :] = strips[(gy + 7) % 8, unit + k]
    for x in range(3, 21):
        packed = g1[x // 4]
        slots = 2 * (row_of(packed) & 1) + (lane_of(packed) & 1)
        slot = x % 4
        part = jnp.where(slots == slot, packed, 0.0)
        part = part + turn(part, 1 if slot % 2 == 0 else -1, 1)
        part = part + turn(part, 1 if slot < 2 else -1, 0)
        f1[x] = part
        a1[x] = -COEFF * part
    sweep(b1, a1, f1, 4, 20, 2, 2)
    for k in range(8):
        block = a2[3 + (k + 2) // 4]
        slot = (k + 2) % 4
        low, high = block[0:8], block[24:32]
        part = jnp.where(row_of(low) < 6, low, high)
        part = jnp.where((lane_of(part) & 3) == slot, part, 0.0)
        part = part + turn(part, 1 if slot % 2 == 0 else -1, 1)
        part = part + turn(part, 2 if slot < 2 else -2, 1)
        for q in range(8):
            e1[k, 4 * q : 4 * q + 4, :] = jnp.broadcast_to(part[q : q + 1, :], (4, 128))
    for r in range(4, 20):
        c1[r] = without_middle(b1[r]) + e1[(r - 4) // 2]
    for dst, src, first, last in ((d1, c1, 5, 19), (c1, d1, 6, 18)):
        for i, n in chunks(first, last):
            p, around = neighbours(src, i, n, 2, 2)
            dst[i : i + n] = 0.2 * p + COEFF * (around - without_middle(f1[i : i + n]))
    for i in range(22):
        coarse = c1[6 + (i + 1) // 2]
        edge = coarse[16:24]
        p0[i, 0:B, :] = finest[i, 0:B, :] + coarse[0:B]
        p0[i, B:, :] = finest[i, B:, :] + jnp.where(row_of(edge) < 4, edge, coarse[24:32])
    sweep(q0, p0, right, 1, 21, 1, 1, 1)
    sweep(p0, q0, right, 2, 20, 1, 1, 1)
    for i in range(B):
        p = p0[3 + i]
        lane = lane_of(p)
        above = jnp.where(lane == 127, p, turn(p, -1, 1))
        below = jnp.where(lane == 0, p, turn(p, 1, 1))
        along_x = p0[4 + i] - p0[2 + i]
        along_y = turn(p, -1, 0) - turn(p, 1, 0)
        velocity_new[0, i] = star[0, i] - (0.5 * STEP) * along_x[0:B]
        velocity_new[1, i] = star[1, i] - (0.5 * STEP) * along_y[0:B]
        velocity_new[2, i] = star[2, i] - STEP * (above - below)[0:B]
        pressure_new[i] = p[0:B]


def swaps(count):
    near = [(i, i ^ 1) for i in range(count)]
    far = [(i, (((i + 1) ^ 1) - 1) % count) for i in range(count)]
    return near, far


def exchange(near_block, far_block, axis):
    near, far = swaps(lax.axis_size(axis))
    far_block = lax.ppermute(far_block, axis, far)
    return lax.ppermute(near_block, axis, near), far_block


def per_device(velocity, pressure, land_type, turbine_cells, surface_drag):
    gx = lax.axis_size("gx")
    gy = lax.axis_size("gy")
    place = jnp.stack([lax.axis_index("gx"), lax.axis_index("gy")]).astype(jnp.int32)
    staged = (surface_drag, land_type, velocity, pressure, turbine_cells)
    near, far = call(
        pack_x,
        [shape(SIDE, B, 128), shape(SIDE, B, 128)],
        [HBM] * 5,
        [
            pltpu.SMEM((16,), F32),
            pltpu.VMEM((B, B), jnp.int32),
            pltpu.VMEM((B, B, 128), jnp.int32),
            (B, B, 128),
            pltpu.SemaphoreType.DMA((11,)),
        ],
    )(*[pltpu.with_memory_space_constraint(x, pltpu.HBM) for x in staged])
    near, far = exchange(near, far, "gx")
    wide_v, wide_p, wide_d, near, far, near_p, far_p = call(
        widen_x,
        [shape(3, VX, B, 128), shape(PX, B, 128), shape(PX, B, 128)]
        + [shape(8, 40, 128)] * 2
        + [shape(N_P, 4, 128)] * 2,
        [SMEM, SMEM] + [VMEM] * 6,
    )(place, surface_drag, land_type, velocity, pressure, turbine_cells, near, far)
    near, far = exchange(near, far, "gy")
    near_p, far_p = exchange(near_p, far_p, "gy")
    star, source, near, far = call(
        advance,
        [shape(3, B, B, 128), shape(PX - 2, B, 128), shape(N_S, 128), shape(N_S, 128)],
        [SMEM] + [VMEM] * 4,
        [(3, VX, 24, 128), (VX, 24, 128), (3, VX, 24, 128), (3, VX, 24, 128)],
    )(place, wide_v, wide_d, near, far)
    near, far = exchange(near, far, "gy")
    finest, right, packed_one, packed_two = call(
        presmooth,
        [shape(22, 24, 128), shape(20, 24, 128), shape(2, B, 128), shape(gx, 4, 128)],
        [SMEM] + [VMEM] * 6,
        [(PX, 32, 128)] * 3 + [(12, 32, 128)] * 3,
    )(place, source, wide_p, near, far, near_p, far_p)
    near, far = exchange(packed_one, packed_one, "gx")
    blocks = lax.all_to_all(packed_two, "gx", 0, 0, tiled=True)
    strips, window = call(
        lambda *refs: pack_y(gx, *refs),
        [shape(gy, N_STRIP, 4, 128), shape(6, B, 128)],
        [SMEM] + [VMEM] * 4,
    )(place, blocks, packed_one, near, far)
    strips = lax.all_to_all(strips, "gy", 0, 0, tiled=True)
    velocity_new, pressure_new = call(
        finish,
        [shape(3, B, B, 128), shape(B, B, 128)],
        [SMEM] + [VMEM] * 7,
        [(9, 32, 128)] * 6
        + [(6, 40, 128)]
        + [(24, 40, 128)] * 3
        + [(24, 32, 128)] * 2
        + [(8, 32, 128)]
        + [(22, 24, 128)] * 2,
    )(place, strips, window, finest, right, star, packed_matrix(1, 4), packed_matrix(2, 8))
    return velocity_new, pressure_new


def solution(mesh):
    in_specs = (
        P(None, "gx", "gy", None),
        P("gx", "gy", None),
        P("gx", "gy"),
        P("gx", "gy", None),
        P(),
    )
    out_specs = (P(None, "gx", "gy", None), P("gx", "gy", None))
    return jax.shard_map(
        per_device, mesh=mesh, in_specs=in_specs, out_specs=out_specs, check_vma=False
    )
```

```python
import jax
import numpy as np
import jax.numpy as jnp
from jax import lax
from jax.experimental import pallas as pl
from jax.experimental.pallas import tpu as pltpu
from jax.sharding import PartitionSpec as P

VH = 9
PH = 7
B = 16
VX = B + 2 * VH
PX = B + 2 * PH
SIDE = 3 * VH + 2 * PH
STEP = 0.1
ROWS = 8
EDDY = 0.03
COEFF = 0.8 / 12.0
WINDOW = 4
VMEM = pl.BlockSpec(memory_space=pltpu.VMEM)
SMEM = pl.BlockSpec(memory_space=pltpu.SMEM)
HBM = pl.BlockSpec(memory_space=pltpu.HBM)
S_ROWS = [(6 * i, 6, 5 + i) for i in range(18)] + [(108 + 4 * i, 4, x) for i, x in enumerate((1, 2, 3, 4, 23, 24, 25, 26))]
P_UNITS = ((0, 5, 20, True), (20, 5, 20, False), (40, 1, 4, False), (44, 25, 4, False))
N_S = 144
N_P = 48
F32 = jnp.float32


def shape(*dims):
    return jax.ShapeDtypeStruct(dims, F32)


def call(body, outs, specs, scratch=(), grant=48, out_space=None):
    return pl.pallas_call(
        body,
        out_shape=outs,
        in_specs=specs,
        out_specs=[out_space or VMEM] * len(outs),
        scratch_shapes=[pltpu.VMEM(s, F32) if isinstance(s, tuple) else s for s in scratch],
        compiler_params=pltpu.CompilerParams(vmem_limit_bytes=grant * 1024 * 1024),
    )


def iota(like, dim):
    return lax.broadcasted_iota(jnp.int32, like.shape, dim)


def lane_of(values):
    return iota(values, values.ndim - 1)


def row_of(values):
    return iota(values, values.ndim - 2)


def turn(values, amount, dim):
    return pltpu.roll(values, amount % values.shape[dim], dim)


def ground_columns(kinds, drag_table):
    ground = jnp.zeros(kinds.shape, F32)
    for kind in range(16):
        ground = jnp.where(kinds == kind, drag_table[kind], ground)
    square = lax.broadcasted_iota(jnp.int32, (B, B), 0) == lax.broadcasted_iota(jnp.int32, (B, B), 1)
    columns = []
    for i in range(B):
        row = jnp.broadcast_to(ground[i : i + 1, :], (B, B))
        columns.append(jnp.sum(jnp.where(square, row, 0.0), axis=1, keepdims=True))
    return columns


def drag_row(cells, column):
    return 2.0 * cells.astype(F32) + jnp.where(lane_of(cells) == 0, column, 0.0)


def edge_units(units, field, up, down):
    for message, outer, inner in ((up, B - 4, B - 8), (down, 0, 4)):
        for unit, start, count, deep in units:
            first = inner if deep else outer
            message[unit : unit + count] = field[start : start + count, first : first + 4, :]


def place_units(units, field, shift, low, high):
    for unit, start, count, deep in units:
        rows = slice(start + shift, start + shift + count)
        first = B + 4 if deep else B
        field[rows, first : first + 4, :] = high[unit : unit + count]
        first = B + 8 if deep else B + 12
        field[rows, first : first + 4, :] = low[unit : unit + count]


def pack_x(drag_hbm, land, velocity, pressure, turbine, near, far, drag_table, kinds_ref, cells_ref, drag, sems):
    core = lax.axis_index("gx") % 2
    copies = [
        pltpu.make_async_copy(turbine, cells_ref, sems.at[0]),
        pltpu.make_async_copy(land, kinds_ref, sems.at[1]),
        pltpu.make_async_copy(drag_hbm, drag_table, sems.at[10]),
    ]
    for side, out in ((0, near), (1, far)):
        high = (core + side) % 2 == 0
        start = jnp.where(high, B - VH, 0)
        for a in range(3):
            copies.append(
                pltpu.make_async_copy(
                    velocity.at[a, pl.ds(start, VH)], out.at[pl.ds(a * VH, VH)], sems.at[2 + 4 * side + a]
                )
            )
        start = jnp.where(high, B - PH, 0)
        copies.append(
            pltpu.make_async_copy(
                pressure.at[pl.ds(start, PH)], out.at[pl.ds(3 * VH, PH)], sems.at[5 + 4 * side]
            )
        )
    for copy in copies:
        copy.start()
    copies[1].wait()
    copies[2].wait()
    columns = ground_columns(kinds_ref[...], drag_table)
    copies[0].wait()
    for i in range(B):
        drag[i] = drag_row(cells_ref[i], columns[i])

    @pl.when(core == 0)
    def _():
        near[3 * VH + PH : SIDE] = drag[B - PH :]
        far[3 * VH + PH : SIDE] = drag[:PH]

    @pl.when(core == 1)
    def _():
        near[3 * VH + PH : SIDE] = drag[:PH]
        far[3 * VH + PH : SIDE] = drag[B - PH :]

    for copy in copies[3:]:
        copy.wait()


def widen_x(place, drag_table, land, velocity, pressure, turbine, far, near, wide_v, wide_p, wide_d, near_y, far_y, near_p, far_p):
    core = place[0] % 2
    odd = place[1] % 2
    columns = ground_columns(land[...], drag_table)
    for i in range(B):
        wide_d[PH + i] = drag_row(turbine[i], columns[i])
    for a in range(3):
        wide_v[a, VH : VH + B] = velocity[a]
    wide_p[PH : PH + B] = pressure[...]

    def fill(low, high):
        for a in range(3):
            wide_v[a, :VH] = low[a * VH : (a + 1) * VH]
            wide_v[a, VH + B :] = high[a * VH : (a + 1) * VH]
        wide_p[:PH] = low[3 * VH : 3 * VH + PH]
        wide_p[PH + B :] = high[3 * VH : 3 * VH + PH]
        wide_d[:PH] = low[3 * VH + PH :]
        wide_d[PH + B :] = high[3 * VH + PH :]

    @pl.when(core == 0)
    def _():
        fill(far, near)

    @pl.when(core == 1)
    def _():
        fill(near, far)

    def send(up, down):
        for g in range(8):
            for j in range(4):
                x = 1 + 4 * g + j
                for a in range(3):
                    rows = slice(10 * j + 3 * a, 10 * j + 3 * a + 3)
                    up[g, rows, :] = wide_v[a, x, B - 3 :, :]
                    down[g, rows, :] = wide_v[a, x, :3, :]
                row = slice(10 * j + 9, 10 * j + 10)
                d = min(max(x - 2, 0), PX - 1)
                up[g, row, :] = wide_d[d, B - 1 :, :]
                down[g, row, :] = wide_d[d, 0:1, :]

    @pl.when(odd == 0)
    def _():
        send(near_y, far_y)
        edge_units(P_UNITS, wide_p, near_p, far_p)

    @pl.when(odd == 1)
    def _():
        send(far_y, near_y)
        edge_units(P_UNITS, wide_p, far_p, near_p)


def three_parts(flat):
    high = flat.astype(jnp.bfloat16)
    rest = flat - high.astype(F32)
    middle = rest.astype(jnp.bfloat16)
    low = (rest - middle.astype(F32)).astype(jnp.bfloat16)
    return jnp.concatenate([high, middle, low], axis=1)


def exact_product(values, matrix):
    parts = three_parts(values.reshape(-1, 128))
    return jnp.dot(parts, matrix, preferred_element_type=F32).reshape(values.shape)


def column_difference():
    i = lax.broadcasted_iota(jnp.int32, (128, 128), 0)
    j = lax.broadcasted_iota(jnp.int32, (128, 128), 1)
    one = jnp.where(i - j == 1, 1.0, jnp.where(j - i == 1, -1.0, 0.0))
    return jnp.concatenate([one.astype(jnp.bfloat16)] * 3, axis=0)


def advance(place, wide_v, wide_d, far, near, star, source, near_y, far_y, v, dr, tau, part):
    odd = place[1] % 2
    v[:, :, 0:B, :] = wide_v[...]
    dr[2 : 2 + PX, 0:B, :] = wide_d[...]

    def fill(low, high):
        for g in range(8):
            for j in range(4):
                x = 1 + 4 * g + j
                for a in range(3):
                    rows = slice(10 * j + 3 * a, 10 * j + 3 * a + 3)
                    v[a, x, B : B + 3, :] = high[g, rows, :]
                    v[a, x, B + 5 : B + 8, :] = low[g, rows, :]
                if 2 <= x < 2 + PX:
                    row = slice(10 * j + 9, 10 * j + 10)
                    dr[x, B : B + 1, :] = high[g, row, :]
                    dr[x, B + 7 : B + 8, :] = low[g, row, :]

    @pl.when(odd == 0)
    def _():
        fill(far, near)

    @pl.when(odd == 1)
    def _():
        fill(near, far)

    difference = column_difference()

    def along_column(fields):
        n = fields[0].shape[0]
        whole = exact_product(jnp.concatenate(fields, axis=0), difference)
        return [whole[k * n : (k + 1) * n] for k in range(len(fields))]

    def along_row(values):
        return 0.5 * (turn(values, -1, 1) - turn(values, 1, 1))

    for i in range(1, VX - 1, ROWS):
        here = slice(i, i + ROWS)
        u = [v[a, here] for a in range(3)]
        gx = [0.5 * (v[a, i + 1 : i + 1 + ROWS] - v[a, i - 1 : i - 1 + ROWS]) for a in range(3)]
        gy = [along_row(u[a]) for a in range(3)]
        gz = along_column(u)
        e01 = gx[1] + gy[0]
        e02 = gx[2] + gz[0]
        e12 = gy[2] + gz[1]
        total = 2.0 * (gx[0] * gx[0] + gy[1] * gy[1] + gz[2] * gz[2]) + (
            e01 * e01 + e02 * e02 + e12 * e12
        )
        visc = EDDY * jnp.sqrt(total)
        t01 = visc * e01
        t02 = visc * e02
        t12 = visc * e12
        tau[0, here] = 2.0 * visc * gx[0]
        tau[1, here] = t01
        tau[2, here] = t02
        along_y = [along_row(t) for t in (t01, 2.0 * visc * gy[1], t12)]
        along_z = along_column([t02, t12, 2.0 * visc * gz[2]])
        lane = lane_of(u[0])
        flat = u[0] * u[0] + u[1] * u[1]
        edge = jnp.where((lane == 0) | (lane == 127), EDDY * jnp.sqrt(flat + 2.0 * (u[2] * u[2])), 0.0)
        wind = dr[here] * jnp.sqrt(flat)
        for a in range(3):
            change = along_y[a] + (along_z[a] - (edge * u[a] if a < 2 else 2.0 * (edge * u[a])))
            change = change - (u[0] * gx[a] + u[1] * gy[a] + u[2] * gz[a])
            if a < 2:
                change = change - wind * u[a]
            if a == 0:
                change = change + 1.0
            part[a, here] = u[a] + STEP * change
    for i in range(2, VX - 2):
        for a in range(3):
            part[a, i] = part[a, i] + (0.5 * STEP) * (tau[a, i + 1] - tau[a, i - 1])
    for a in range(3):
        star[a] = part[a, VH : VH + B, 0:B, :]
    for i in range(3, VX - 3, 4):
        along_x = 0.5 * (part[0, i + 1 : i + 5] - part[0, i - 1 : i + 3])
        along_y = along_row(part[1, i : i + 4])
        (along_z,) = along_column([part[2, i : i + 4, 0:B, :]])
        source[i - 3 : i + 1] = ((along_x + along_y)[:, 0:B] + along_z) / STEP

    def send(up, down):
        for row, count, x in S_ROWS:
            up[row : row + count, :] = source[x, B - count :, :]
            down[row : row + count, :] = source[x, :count, :]

    @pl.when(odd == 0)
    def _():
        send(near_y, far_y)

    @pl.when(odd == 1)
    def _():
        send(far_y, near_y)


def column_sum(dz, halves):
    i = lax.broadcasted_iota(jnp.int32, (128, 128), 0)
    j = lax.broadcasted_iota(jnp.int32, (128, 128), 1)
    hit = (i - j == dz) | (j - i == dz) | ((i == j) & ((j < dz) | (j >= 128 - dz)))
    return jnp.concatenate([jnp.where(hit, 4.0, 0.0).astype(jnp.bfloat16)] * halves, axis=0)


def neighbours(ref, start, count, dy, dz, matrix=None):
    p = ref[start : start + count]
    sides = ref[start - 1 : start - 1 + count] + ref[start + 1 : start + 1 + count]
    sides = sides + (turn(p, dy, 1) + turn(p, -dy, 1))
    if matrix is not None:
        return p, sides + exact_product(p, matrix)
    lane = lane_of(p)
    below = jnp.where(lane < dz, p, turn(p, dz, 2))
    above = jnp.where(lane >= 128 - dz, p, turn(p, -dz, 2))
    return p, sides + 4.0 * (below + above)


def chunks(first, last, size=2):
    return [(i, min(size, last - i)) for i in range(first, last, size)]


def sweep(dst, src, right, first, last, dy, dz, offset=0, matrix=None):
    for i, n in chunks(first, last, 2 if matrix is None else 4):
        p, around = neighbours(src, i, n, dy, dz, matrix)
        dst[i : i + n] = 0.2 * p + COEFF * (around - right[i - offset : i - offset + n])


def scaled_residual(src, right, i, n, dy, dz, matrix=None):
    p, around = neighbours(src, i, n, dy, dz, matrix)
    return right[i : i + n] - around + 12.0 * p


def coarsen_pair(pair, dy, dz):
    total = pair[0] + pair[1]
    lane = lane_of(total)
    total = total + jnp.where((lane & dz) == 0, turn(total, -dz, 1), turn(total, dz, 1))
    row = row_of(total)
    total = total + jnp.where((row & dy) == 0, turn(total, -dy, 0), turn(total, dy, 0))
    return 0.5 * total


def presmooth(place, source, wide_p, far, near, far_p, near_p, finest, right, packed_one, packed_two, p, s, q, f1, a1, b1):
    odd = place[1] % 2
    p[:, 0:B, :] = wide_p[...]
    s[1 : PX - 1, 0:B, :] = source[...]

    def place_source(low, high):
        for row, count, x in S_ROWS:
            s[x + 1, B : B + count, :] = high[row : row + count, :]
            s[x + 1, B + 16 - count : B + 16, :] = low[row : row + count, :]

    @pl.when(odd == 0)
    def _():
        place_source(far, near)
        place_units(P_UNITS, p, 0, far_p, near_p)

    @pl.when(odd == 1)
    def _():
        place_source(near, far)
        place_units(P_UNITS, p, 0, near_p, far_p)

    fine = column_sum(1, 3)
    coarse = column_sum(2, 3)
    sweep(q, p, s, 1, PX - 1, 1, 1, 0, fine)
    sweep(p, q, s, 2, PX - 2, 1, 1, 0, fine)
    for out, field, first in ((finest, p, 4), (right, s, 5)):
        out[:, 0:B, :] = field[first : PX - first, 0:B, :]
        out[:, B : B + 4, :] = field[first : PX - first, B : B + 4, :]
        out[:, B + 4 : B + 8, :] = field[first : PX - first, B + 12 : B + 16, :]
    for k in range(0, 12, 2):
        rows = scaled_residual(p, s, 3 + 2 * k, 4, 1, 1, fine)
        f1[k] = coarsen_pair(rows[0:2], 1, 1)
        f1[k + 1] = coarsen_pair(rows[2:4], 1, 1)
    a1[...] = -COEFF * f1[...]
    sweep(b1, a1, f1, 1, 11, 2, 2, 0, coarse)
    rows = scaled_residual(b1, f1, 2, 8, 2, 2, coarse)
    f2 = [coarsen_pair(rows[2 * k : 2 * k + 2], 2, 2) for k in range(4)]
    lane = lane_of(f2[0]) & 3
    two = jnp.where(lane == 0, f2[0], jnp.where(lane == 1, f2[1], jnp.where(lane == 2, f2[2], f2[3])))
    four = jnp.concatenate([two[4 * y : 4 * y + 1, :] for y in range(4)], axis=0)
    for k in range(packed_two.shape[0]):
        packed_two[k] = four
    for g in range(2):
        rows = [f1[2 + 4 * g + j][0:B] for j in range(4)]
        slot = 2 * (row_of(rows[0]) & 1) + (lane_of(rows[0]) & 1)
        packed_one[g] = jnp.where(
            slot == 0, rows[0], jnp.where(slot == 1, rows[1], jnp.where(slot == 2, rows[2], rows[3]))
        )


GROUPS = ((9, 1, 2), (11, 2, 3), (14, 3, 3), (17, 4, 2))
N_STRIP = 19


def pack_y(peers, place, blocks, own, near, far, strips, window):
    core = place[0] % 2
    gy = place[1]
    for j in range(2 * WINDOW + 1):
        piece = blocks[(place[0] + (peers - WINDOW + j)) % peers]
        for k in range(8):
            strips[k, j] = piece
    window[2:4] = own[...]

    def fill(low, high):
        window[0:2] = low[...]
        window[4:6] = high[...]

    @pl.when(core == 0)
    def _():
        fill(far, near)

    @pl.when(core == 1)
    def _():
        fill(near, far)

    for step in range(1, 8):
        peer = (gy + step) % 8
        for unit, group, count in GROUPS:
            for k in range(count):
                first = 4 * k if step == 7 else B - 4 * (count - k)
                strips[peer, unit + k] = window[group, first : first + 4, :]
    for k in range(9, N_STRIP):
        strips[gy, k] = jnp.zeros((4, 128), F32)


def packed_matrix(dx, dz):
    k = np.arange(128)[:, None]
    j = np.arange(128)[None, :]
    slot = j % 4
    own = (k == j - dx) & (slot >= dx)
    own = own.astype(np.float32) + ((k == j + dx) & (slot < 4 - dx))
    edge = (k == j) & ((j < dz) | (j >= 128 - dz))
    own = own + 4.0 * ((k == j - dz) | (k == j + dz)) + 4.0 * edge
    after = (k == j + 4 - dx) & (slot < dx)
    before = (k == j - 4 + dx) & (slot >= 4 - dx)
    whole = np.concatenate([own, after.astype(np.float32), before.astype(np.float32)], axis=1)
    return jnp.asarray(np.concatenate([whole] * 3, axis=0), jnp.bfloat16)


def packed_around(ref, first, last, dy, matrix):
    low, high = max(first - 1, 0), min(last + 1, 2 * WINDOW + 1)
    p = ref[low:high]
    flat = p.reshape(-1, 128)
    parts = three_parts(flat)
    out = jnp.dot(parts, matrix, preferred_element_type=F32)
    result = []
    for b in range(first, last):
        rows = lambda c: slice(32 * (c - low), 32 * (c - low) + 32)
        before, after = max(b - 1, low), min(b + 1, high - 1)
        sides = out[rows(b), 0:128] + (out[rows(before), 128:256] + out[rows(after), 256:384])
        own = p[b - low]
        result.append((own, sides + (turn(own, dy, 0) + turn(own, -dy, 0))))
    return result


def packed_sweep(dst, src, right, blocks, dy, matrix):
    for b, (p, around) in zip(blocks, packed_around(src, blocks[0], blocks[-1] + 1, dy, matrix)):
        dst[b] = 0.2 * p + COEFF * (around - right[b])


def packed_residual(src, right, blocks, dy, matrix):
    rows = packed_around(src, blocks[0], blocks[-1] + 1, dy, matrix)
    return [right[b] - around + 12.0 * p for b, (p, around) in zip(blocks, rows)]


def without_middle(values):
    return jnp.concatenate([values[..., 0:24, :], values[..., 32:40, :]], axis=-2)


def finish(place, strips, window, finest, right, star, second, third, velocity_new, pressure_new, f2, a2, b2, f3, a3, b3, g1, f1, a1, b1, c1, d1, e1, p0, q0):
    gy = place[1]
    for j in range(8):
        peer = (gy + j) % 8
        for b in range(2 * WINDOW + 1):
            f2[b, 4 * j : 4 * j + 4, :] = strips[peer, b]
    for b in range(9):
        a2[b] = -COEFF * f2[b]
    packed_sweep(b2, a2, f2, range(9), 1, second[...])
    for b, total in zip(range(1, 8), packed_residual(b2, f2, range(1, 8), 1, second[...])):
        lane = lane_of(total)
        total = total + jnp.where((lane & 1) == 0, turn(total, -1, 1), turn(total, 1, 1))
        total = total + jnp.where((lane & 4) == 0, turn(total, -4, 1), turn(total, 4, 1))
        row = row_of(total)
        total = total + jnp.where((row & 1) == 0, turn(total, -1, 0), turn(total, 1, 0))
        f3[b] = 0.5 * total
        a3[b] = (-0.5 * COEFF) * total
    for b in (0, 8):
        a3[b] = jnp.zeros((32, 128), F32)
        b3[b] = jnp.zeros((32, 128), F32)
    packed_sweep(b3, a3, f3, range(1, 8), 2, third[...])
    packed_sweep(a3, b3, f3, range(2, 7), 2, third[...])
    packed_sweep(b3, a3, f3, range(2, 7), 2, third[...])
    for b, total in zip(range(3, 6), packed_residual(b3, f3, range(3, 6), 2, third[...])):
        line = jnp.sum(total, axis=0, keepdims=True) * (COEFF / 32.0)
        a2[b] = b2[b] + (b3[b] - line)
    packed_sweep(b2, a2, f2, range(3, 6), 1, second[...])
    packed_sweep(a2, b2, f2, range(3, 6), 1, second[...])
    g1[:, 0:B, :] = window[...]
    for unit, group, count in GROUPS:
        for k in range(count):
            first = B + 4 * k
            g1[group, first : first + 4, :] = strips[(gy + 1) % 8, unit + k]
            first = B + 24 - 4 * (count - k)
            g1[group, first : first + 4, :] = strips[(gy + 7) % 8, unit + k]
    for x in range(3, 21):
        packed = g1[x // 4]
        slots = 2 * (row_of(packed) & 1) + (lane_of(packed) & 1)
        slot = x % 4
        part = jnp.where(slots == slot, packed, 0.0)
        part = part + turn(part, 1 if slot % 2 == 0 else -1, 1)
        part = part + turn(part, 1 if slot < 2 else -1, 0)
        f1[x] = part
        a1[x] = -COEFF * part
    sweep(b1, a1, f1, 4, 20, 2, 2)
    for k in range(8):
        block = a2[3 + (k + 2) // 4]
        slot = (k + 2) % 4
        low, high = block[0:8], block[24:32]
        part = jnp.where(row_of(low) < 6, low, high)
        part = jnp.where((lane_of(part) & 3) == slot, part, 0.0)
        part = part + turn(part, 1 if slot % 2 == 0 else -1, 1)
        part = part + turn(part, 2 if slot < 2 else -2, 1)
        for q in range(8):
            e1[k, 4 * q : 4 * q + 4, :] = jnp.broadcast_to(part[q : q + 1, :], (4, 128))
    for r in range(4, 20):
        c1[r] = without_middle(b1[r]) + e1[(r - 4) // 2]
    for dst, src, first, last in ((d1, c1, 5, 19), (c1, d1, 6, 18)):
        for i, n in chunks(first, last):
            p, around = neighbours(src, i, n, 2, 2)
            dst[i : i + n] = 0.2 * p + COEFF * (around - without_middle(f1[i : i + n]))
    for i in range(22):
        coarse = c1[6 + (i + 1) // 2]
        edge = coarse[16:24]
        p0[i, 0:B, :] = finest[i, 0:B, :] + coarse[0:B]
        p0[i, B:, :] = finest[i, B:, :] + jnp.where(row_of(edge) < 4, edge, coarse[24:32])
    sweep(q0, p0, right, 1, 21, 1, 1, 1)
    sweep(p0, q0, right, 2, 20, 1, 1, 1)
    for i in range(B):
        p = p0[3 + i]
        lane = lane_of(p)
        above = jnp.where(lane == 127, p, turn(p, -1, 1))
        below = jnp.where(lane == 0, p, turn(p, 1, 1))
        along_x = p0[4 + i] - p0[2 + i]
        along_y = turn(p, -1, 0) - turn(p, 1, 0)
        velocity_new[0, i] = star[0, i] - (0.5 * STEP) * along_x[0:B]
        velocity_new[1, i] = star[1, i] - (0.5 * STEP) * along_y[0:B]
        velocity_new[2, i] = star[2, i] - STEP * (above - below)[0:B]
        pressure_new[i] = p[0:B]


def swaps(count):
    near = [(i, i ^ 1) for i in range(count)]
    far = [(i, (((i + 1) ^ 1) - 1) % count) for i in range(count)]
    return near, far


def exchange(near_block, far_block, axis):
    near, far = swaps(lax.axis_size(axis))
    far_block = lax.ppermute(far_block, axis, far)
    return lax.ppermute(near_block, axis, near), far_block


def per_device(velocity, pressure, land_type, turbine_cells, surface_drag):
    gx = lax.axis_size("gx")
    gy = lax.axis_size("gy")
    place = jnp.stack([lax.axis_index("gx"), lax.axis_index("gy")]).astype(jnp.int32)
    staged = (surface_drag, land_type, velocity, pressure, turbine_cells)
    near, far = call(
        pack_x,
        [shape(SIDE, B, 128), shape(SIDE, B, 128)],
        [HBM] * 5,
        [
            pltpu.SMEM((16,), F32),
            pltpu.VMEM((B, B), jnp.int32),
            pltpu.VMEM((B, B, 128), jnp.int32),
            (B, B, 128),
            pltpu.SemaphoreType.DMA((11,)),
        ],
    )(*[pltpu.with_memory_space_constraint(x, pltpu.HBM) for x in staged])
    near, far = exchange(near, far, "gx")
    wide_v, wide_p, wide_d, near, far, near_p, far_p = call(
        widen_x,
        [shape(3, VX, B, 128), shape(PX, B, 128), shape(PX, B, 128)]
        + [shape(8, 40, 128)] * 2
        + [shape(N_P, 4, 128)] * 2,
        [SMEM, SMEM] + [VMEM] * 6,
    )(place, surface_drag, land_type, velocity, pressure, turbine_cells, far, near)
    near, far = exchange(near, far, "gy")
    near_p, far_p = exchange(near_p, far_p, "gy")
    star, source, near, far = call(
        advance,
        [shape(3, B, B, 128), shape(PX - 2, B, 128), shape(N_S, 128), shape(N_S, 128)],
        [SMEM] + [VMEM] * 4,
        [(3, VX, 24, 128), (VX, 24, 128), (3, VX, 24, 128), (3, VX, 24, 128)],
    )(place, wide_v, wide_d, far, near)
    near, far = exchange(near, far, "gy")
    finest, right, packed_one, packed_two = call(
        presmooth,
        [shape(22, 24, 128), shape(20, 24, 128), shape(2, B, 128), shape(gx, 4, 128)],
        [SMEM] + [VMEM] * 6,
        [(PX, 32, 128)] * 3 + [(12, 32, 128)] * 3,
    )(place, source, wide_p, far, near, far_p, near_p)
    near, far = exchange(packed_one, packed_one, "gx")
    blocks = lax.all_to_all(packed_two, "gx", 0, 0, tiled=True)
    strips, window = call(
        lambda *refs: pack_y(gx, *refs),
        [shape(gy, N_STRIP, 4, 128), shape(6, B, 128)],
        [SMEM] + [VMEM] * 4,
    )(place, blocks, packed_one, near, far)
    strips = lax.all_to_all(strips, "gy", 0, 0, tiled=True)
    velocity_new, pressure_new = call(
        finish,
        [shape(3, B, B, 128), shape(B, B, 128)],
        [SMEM] + [VMEM] * 7,
        [(9, 32, 128)] * 6
        + [(6, 40, 128)]
        + [(24, 40, 128)] * 3
        + [(24, 32, 128)] * 2
        + [(8, 32, 128)]
        + [(22, 24, 128)] * 2,
    )(place, strips, window, finest, right, star, packed_matrix(1, 4), packed_matrix(2, 8))
    return velocity_new, pressure_new


def solution(mesh):
    in_specs = (
        P(None, "gx", "gy", None),
        P("gx", "gy", None),
        P("gx", "gy"),
        P("gx", "gy", None),
        P(),
    )
    out_specs = (P(None, "gx", "gy", None), P("gx", "gy", None))
    return jax.shard_map(
        per_device, mesh=mesh, in_specs=in_specs, out_specs=out_specs, check_vma=False
    )
```

```python
import jax
import numpy as np
import jax.numpy as jnp
from jax import lax
from jax.experimental import pallas as pl
from jax.experimental.pallas import tpu as pltpu
from jax.sharding import PartitionSpec as P

VH = 9
PH = 7
B = 16
VX = B + 2 * VH
PX = B + 2 * PH
SIDE = 3 * VH + 2 * PH
STEP = 0.1
ROWS = 8
EDDY = 0.03
COEFF = 0.8 / 12.0
WINDOW = 4
VMEM = pl.BlockSpec(memory_space=pltpu.VMEM)
SMEM = pl.BlockSpec(memory_space=pltpu.SMEM)
HBM = pl.BlockSpec(memory_space=pltpu.HBM)
S_ROWS = [(6 * i, 6, 5 + i) for i in range(18)] + [(108 + 4 * i, 4, x) for i, x in enumerate((1, 2, 3, 4, 23, 24, 25, 26))]
P_UNITS = ((0, 5, 20, True), (20, 5, 20, False), (40, 1, 4, False), (44, 25, 4, False))
N_S = 144
N_P = 48
F32 = jnp.float32


def shape(*dims):
    return jax.ShapeDtypeStruct(dims, F32)


def call(body, outs, specs, scratch=(), grant=48, out_space=None):
    return pl.pallas_call(
        body,
        out_shape=outs,
        in_specs=specs,
        out_specs=[out_space or VMEM] * len(outs),
        scratch_shapes=[pltpu.VMEM(s, F32) if isinstance(s, tuple) else s for s in scratch],
        compiler_params=pltpu.CompilerParams(vmem_limit_bytes=grant * 1024 * 1024),
    )


def iota(like, dim):
    return lax.broadcasted_iota(jnp.int32, like.shape, dim)


def lane_of(values):
    return iota(values, values.ndim - 1)


def row_of(values):
    return iota(values, values.ndim - 2)


def turn(values, amount, dim):
    return pltpu.roll(values, amount % values.shape[dim], dim)


def ground_columns(kinds, drag_table):
    ground = jnp.zeros(kinds.shape, F32)
    for kind in range(16):
        ground = jnp.where(kinds == kind, drag_table[kind], ground)
    square = lax.broadcasted_iota(jnp.int32, (B, B), 0) == lax.broadcasted_iota(jnp.int32, (B, B), 1)
    columns = []
    for i in range(B):
        row = jnp.broadcast_to(ground[i : i + 1, :], (B, B))
        columns.append(jnp.sum(jnp.where(square, row, 0.0), axis=1, keepdims=True))
    return columns


def drag_row(cells, column):
    return 2.0 * cells.astype(F32) + jnp.where(lane_of(cells) == 0, column, 0.0)


def edge_units(units, field, up, down):
    for message, outer, inner in ((up, B - 4, B - 8), (down, 0, 4)):
        for unit, start, count, deep in units:
            first = inner if deep else outer
            message[unit : unit + count] = field[start : start + count, first : first + 4, :]


def place_units(units, field, shift, low, high):
    for unit, start, count, deep in units:
        rows = slice(start + shift, start + shift + count)
        first = B + 4 if deep else B
        field[rows, first : first + 4, :] = high[unit : unit + count]
        first = B + 8 if deep else B + 12
        field[rows, first : first + 4, :] = low[unit : unit + count]


def pack_x(drag_hbm, land, velocity, pressure, turbine, near, far, drag_table, kinds_ref, cells_ref, drag, sems):
    core = lax.axis_index("gx") % 2
    copies = [
        pltpu.make_async_copy(turbine, cells_ref, sems.at[0]),
        pltpu.make_async_copy(land, kinds_ref, sems.at[1]),
        pltpu.make_async_copy(drag_hbm, drag_table, sems.at[10]),
    ]
    for side, out in ((0, near), (1, far)):
        high = (core + side) % 2 == 0
        start = jnp.where(high, B - VH, 0)
        for a in range(3):
            copies.append(
                pltpu.make_async_copy(
                    velocity.at[a, pl.ds(start, VH)], out.at[pl.ds(a * VH, VH)], sems.at[2 + 4 * side + a]
                )
            )
        start = jnp.where(high, B - PH, 0)
        copies.append(
            pltpu.make_async_copy(
                pressure.at[pl.ds(start, PH)], out.at[pl.ds(3 * VH, PH)], sems.at[5 + 4 * side]
            )
        )
    for copy in copies:
        copy.start()
    copies[1].wait()
    copies[2].wait()
    columns = ground_columns(kinds_ref[...], drag_table)
    copies[0].wait()
    for i in range(B):
        drag[i] = drag_row(cells_ref[i], columns[i])

    @pl.when(core == 0)
    def _():
        near[3 * VH + PH : SIDE] = drag[B - PH :]
        far[3 * VH + PH : SIDE] = drag[:PH]

    @pl.when(core == 1)
    def _():
        near[3 * VH + PH : SIDE] = drag[:PH]
        far[3 * VH + PH : SIDE] = drag[B - PH :]

    for copy in copies[3:]:
        copy.wait()


def widen_x(place, drag_table, land, velocity, pressure, turbine, far, near, wide_v, wide_p, wide_d, near_y, far_y, near_p, far_p):
    core = place[0] % 2
    odd = place[1] % 2
    columns = ground_columns(land[...], drag_table)
    for i in range(B):
        wide_d[PH + i] = drag_row(turbine[i], columns[i])
    for a in range(3):
        wide_v[a, VH : VH + B] = velocity[a]
    wide_p[PH : PH + B] = pressure[...]

    def fill(low, high):
        for a in range(3):
            wide_v[a, :VH] = low[a * VH : (a + 1) * VH]
            wide_v[a, VH + B :] = high[a * VH : (a + 1) * VH]
        wide_p[:PH] = low[3 * VH : 3 * VH + PH]
        wide_p[PH + B :] = high[3 * VH : 3 * VH + PH]
        wide_d[:PH] = low[3 * VH + PH :]
        wide_d[PH + B :] = high[3 * VH + PH :]

    @pl.when(core == 0)
    def _():
        fill(far, near)

    @pl.when(core == 1)
    def _():
        fill(near, far)

    def send(up, down):
        for g in range(8):
            for j in range(4):
                x = 1 + 4 * g + j
                for a in range(3):
                    rows = slice(10 * j + 3 * a, 10 * j + 3 * a + 3)
                    up[g, rows, :] = wide_v[a, x, B - 3 :, :]
                    down[g, rows, :] = wide_v[a, x, :3, :]
                row = slice(10 * j + 9, 10 * j + 10)
                d = min(max(x - 2, 0), PX - 1)
                up[g, row, :] = wide_d[d, B - 1 :, :]
                down[g, row, :] = wide_d[d, 0:1, :]

    @pl.when(odd == 0)
    def _():
        send(near_y, far_y)
        edge_units(P_UNITS, wide_p, near_p, far_p)

    @pl.when(odd == 1)
    def _():
        send(far_y, near_y)
        edge_units(P_UNITS, wide_p, far_p, near_p)


def three_parts(flat):
    high = flat.astype(jnp.bfloat16)
    rest = flat - high.astype(F32)
    middle = rest.astype(jnp.bfloat16)
    low = (rest - middle.astype(F32)).astype(jnp.bfloat16)
    return jnp.concatenate([high, middle, low], axis=1)


def exact_product(values, matrix):
    parts = three_parts(values.reshape(-1, 128))
    return jnp.dot(parts, matrix, preferred_element_type=F32).reshape(values.shape)


def column_difference():
    i = lax.broadcasted_iota(jnp.int32, (128, 128), 0)
    j = lax.broadcasted_iota(jnp.int32, (128, 128), 1)
    one = jnp.where(i - j == 1, 1.0, jnp.where(j - i == 1, -1.0, 0.0))
    return jnp.concatenate([one.astype(jnp.bfloat16)] * 3, axis=0)


def advance(place, wide_v, wide_d, far, near, star, source, near_y, far_y, v, dr, tau, part):
    odd = place[1] % 2
    v[:, :, 0:B, :] = wide_v[...]
    dr[2 : 2 + PX, 0:B, :] = wide_d[...]

    def fill(low, high):
        for g in range(8):
            for j in range(4):
                x = 1 + 4 * g + j
                for a in range(3):
                    rows = slice(10 * j + 3 * a, 10 * j + 3 * a + 3)
                    v[a, x, B : B + 3, :] = high[g, rows, :]
                    v[a, x, B + 5 : B + 8, :] = low[g, rows, :]
                if 2 <= x < 2 + PX:
                    row = slice(10 * j + 9, 10 * j + 10)
                    dr[x, B : B + 1, :] = high[g, row, :]
                    dr[x, B + 7 : B + 8, :] = low[g, row, :]

    @pl.when(odd == 0)
    def _():
        fill(far, near)

    @pl.when(odd == 1)
    def _():
        fill(near, far)

    difference = column_difference()

    def along_column(fields):
        n = fields[0].shape[0]
        whole = exact_product(jnp.concatenate(fields, axis=0), difference)
        return [whole[k * n : (k + 1) * n] for k in range(len(fields))]

    def along_row(values):
        return 0.5 * (turn(values, -1, 1) - turn(values, 1, 1))

    for i in range(1, VX - 1, ROWS):
        here = slice(i, i + ROWS)
        u = [v[a, here] for a in range(3)]
        gx = [0.5 * (v[a, i + 1 : i + 1 + ROWS] - v[a, i - 1 : i - 1 + ROWS]) for a in range(3)]
        gy = [along_row(u[a]) for a in range(3)]
        gz = along_column(u)
        e01 = gx[1] + gy[0]
        e02 = gx[2] + gz[0]
        e12 = gy[2] + gz[1]
        total = 2.0 * (gx[0] * gx[0] + gy[1] * gy[1] + gz[2] * gz[2]) + (
            e01 * e01 + e02 * e02 + e12 * e12
        )
        visc = EDDY * jnp.sqrt(total)
        t01 = visc * e01
        t02 = visc * e02
        t12 = visc * e12
        tau[0, here] = 2.0 * visc * gx[0]
        tau[1, here] = t01
        tau[2, here] = t02
        along_y = [along_row(t) for t in (t01, 2.0 * visc * gy[1], t12)]
        along_z = along_column([t02, t12, 2.0 * visc * gz[2]])
        lane = lane_of(u[0])
        flat = u[0] * u[0] + u[1] * u[1]
        edge = jnp.where((lane == 0) | (lane == 127), EDDY * jnp.sqrt(flat + 2.0 * (u[2] * u[2])), 0.0)
        wind = dr[here] * jnp.sqrt(flat)
        for a in range(3):
            change = along_y[a] + (along_z[a] - (edge * u[a] if a < 2 else 2.0 * (edge * u[a])))
            change = change - (u[0] * gx[a] + u[1] * gy[a] + u[2] * gz[a])
            if a < 2:
                change = change - wind * u[a]
            if a == 0:
                change = change + 1.0
            part[a, here] = u[a] + STEP * change
    for i in range(2, VX - 2):
        for a in range(3):
            part[a, i] = part[a, i] + (0.5 * STEP) * (tau[a, i + 1] - tau[a, i - 1])
    for a in range(3):
        star[a] = part[a, VH : VH + B, 0:B, :]
    for i in range(3, VX - 3, 4):
        along_x = 0.5 * (part[0, i + 1 : i + 5] - part[0, i - 1 : i + 3])
        along_y = along_row(part[1, i : i + 4])
        (along_z,) = along_column([part[2, i : i + 4, 0:B, :]])
        source[i - 3 : i + 1] = ((along_x + along_y)[:, 0:B] + along_z) / STEP

    def send(up, down):
        for row, count, x in S_ROWS:
            up[row : row + count, :] = source[x, B - count :, :]
            down[row : row + count, :] = source[x, :count, :]

    @pl.when(odd == 0)
    def _():
        send(near_y, far_y)

    @pl.when(odd == 1)
    def _():
        send(far_y, near_y)


def column_sum(dz, halves):
    i = lax.broadcasted_iota(jnp.int32, (128, 128), 0)
    j = lax.broadcasted_iota(jnp.int32, (128, 128), 1)
    hit = (i - j == dz) | (j - i == dz) | ((i == j) & ((j < dz) | (j >= 128 - dz)))
    return jnp.concatenate([jnp.where(hit, 4.0, 0.0).astype(jnp.bfloat16)] * halves, axis=0)


def neighbours(ref, start, count, dy, dz, matrix=None):
    p = ref[start : start + count]
    sides = ref[start - 1 : start - 1 + count] + ref[start + 1 : start + 1 + count]
    sides = sides + (turn(p, dy, 1) + turn(p, -dy, 1))
    if matrix is not None:
        return p, sides + exact_product(p, matrix)
    lane = lane_of(p)
    below = jnp.where(lane < dz, p, turn(p, dz, 2))
    above = jnp.where(lane >= 128 - dz, p, turn(p, -dz, 2))
    return p, sides + 4.0 * (below + above)


def chunks(first, last, size=2):
    return [(i, min(size, last - i)) for i in range(first, last, size)]


def sweep(dst, src, right, first, last, dy, dz, offset=0, matrix=None):
    for i, n in chunks(first, last, 2 if matrix is None else 4):
        p, around = neighbours(src, i, n, dy, dz, matrix)
        dst[i : i + n] = 0.2 * p + COEFF * (around - right[i - offset : i - offset + n])


def scaled_residual(src, right, i, n, dy, dz, matrix=None):
    p, around = neighbours(src, i, n, dy, dz, matrix)
    return right[i : i + n] - around + 12.0 * p


def coarsen_pair(pair, dy, dz):
    total = pair[0] + pair[1]
    lane = lane_of(total)
    total = total + jnp.where((lane & dz) == 0, turn(total, -dz, 1), turn(total, dz, 1))
    row = row_of(total)
    total = total + jnp.where((row & dy) == 0, turn(total, -dy, 0), turn(total, dy, 0))
    return 0.5 * total


def presmooth(place, source, wide_p, far, near, near_p, far_p, finest, right, packed_one, packed_two, p, s, q, f1, a1, b1):
    odd = place[1] % 2
    p[:, 0:B, :] = wide_p[...]
    s[1 : PX - 1, 0:B, :] = source[...]

    def place_source(low, high):
        for row, count, x in S_ROWS:
            s[x + 1, B : B + count, :] = high[row : row + count, :]
            s[x + 1, B + 16 - count : B + 16, :] = low[row : row + count, :]

    @pl.when(odd == 0)
    def _():
        place_source(far, near)
        place_units(P_UNITS, p, 0, far_p, near_p)

    @pl.when(odd == 1)
    def _():
        place_source(near, far)
        place_units(P_UNITS, p, 0, near_p, far_p)

    fine = column_sum(1, 3)
    coarse = column_sum(2, 3)
    sweep(q, p, s, 1, PX - 1, 1, 1, 0, fine)
    sweep(p, q, s, 2, PX - 2, 1, 1, 0, fine)
    for out, field, first in ((finest, p, 4), (right, s, 5)):
        out[:, 0:B, :] = field[first : PX - first, 0:B, :]
        out[:, B : B + 4, :] = field[first : PX - first, B : B + 4, :]
        out[:, B + 4 : B + 8, :] = field[first : PX - first, B + 12 : B + 16, :]
    for k in range(0, 12, 2):
        rows = scaled_residual(p, s, 3 + 2 * k, 4, 1, 1, fine)
        f1[k] = coarsen_pair(rows[0:2], 1, 1)
        f1[k + 1] = coarsen_pair(rows[2:4], 1, 1)
    a1[...] = -COEFF * f1[...]
    sweep(b1, a1, f1, 1, 11, 2, 2, 0, coarse)
    rows = scaled_residual(b1, f1, 2, 8, 2, 2, coarse)
    f2 = [coarsen_pair(rows[2 * k : 2 * k + 2], 2, 2) for k in range(4)]
    lane = lane_of(f2[0]) & 3
    two = jnp.where(lane == 0, f2[0], jnp.where(lane == 1, f2[1], jnp.where(lane == 2, f2[2], f2[3])))
    four = jnp.concatenate([two[4 * y : 4 * y + 1, :] for y in range(4)], axis=0)
    for k in range(packed_two.shape[0]):
        packed_two[k] = four
    for g in range(2):
        rows = [f1[2 + 4 * g + j][0:B] for j in range(4)]
        slot = 2 * (row_of(rows[0]) & 1) + (lane_of(rows[0]) & 1)
        packed_one[g] = jnp.where(
            slot == 0, rows[0], jnp.where(slot == 1, rows[1], jnp.where(slot == 2, rows[2], rows[3]))
        )


GROUPS = ((9, 1, 2), (11, 2, 3), (14, 3, 3), (17, 4, 2))
N_STRIP = 19


def pack_y(peers, place, blocks, own, near, far, strips, window):
    core = place[0] % 2
    gy = place[1]
    for j in range(2 * WINDOW + 1):
        piece = blocks[(place[0] + (peers - WINDOW + j)) % peers]
        for k in range(8):
            strips[k, j] = piece
    window[2:4] = own[...]

    def fill(low, high):
        window[0:2] = low[...]
        window[4:6] = high[...]

    @pl.when(core == 0)
    def _():
        fill(far, near)

    @pl.when(core == 1)
    def _():
        fill(near, far)

    for step in range(1, 8):
        peer = (gy + step) % 8
        for unit, group, count in GROUPS:
            for k in range(count):
                first = 4 * k if step == 7 else B - 4 * (count - k)
                strips[peer, unit + k] = window[group, first : first + 4, :]
    for k in range(9, N_STRIP):
        strips[gy, k] = jnp.zeros((4, 128), F32)


def packed_matrix(dx, dz):
    k = np.arange(128)[:, None]
    j = np.arange(128)[None, :]
    slot = j % 4
    own = (k == j - dx) & (slot >= dx)
    own = own.astype(np.float32) + ((k == j + dx) & (slot < 4 - dx))
    edge = (k == j) & ((j < dz) | (j >= 128 - dz))
    own = own + 4.0 * ((k == j - dz) | (k == j + dz)) + 4.0 * edge
    after = (k == j + 4 - dx) & (slot < dx)
    before = (k == j - 4 + dx) & (slot >= 4 - dx)
    whole = np.concatenate([own, after.astype(np.float32), before.astype(np.float32)], axis=1)
    return jnp.asarray(np.concatenate([whole] * 3, axis=0), jnp.bfloat16)


def packed_around(ref, first, last, dy, matrix):
    low, high = max(first - 1, 0), min(last + 1, 2 * WINDOW + 1)
    p = ref[low:high]
    flat = p.reshape(-1, 128)
    parts = three_parts(flat)
    out = jnp.dot(parts, matrix, preferred_element_type=F32)
    result = []
    for b in range(first, last):
        rows = lambda c: slice(32 * (c - low), 32 * (c - low) + 32)
        before, after = max(b - 1, low), min(b + 1, high - 1)
        sides = out[rows(b), 0:128] + (out[rows(before), 128:256] + out[rows(after), 256:384])
        own = p[b - low]
        result.append((own, sides + (turn(own, dy, 0) + turn(own, -dy, 0))))
    return result


def packed_sweep(dst, src, right, blocks, dy, matrix):
    for b, (p, around) in zip(blocks, packed_around(src, blocks[0], blocks[-1] + 1, dy, matrix)):
        dst[b] = 0.2 * p + COEFF * (around - right[b])


def packed_residual(src, right, blocks, dy, matrix):
    rows = packed_around(src, blocks[0], blocks[-1] + 1, dy, matrix)
    return [right[b] - around + 12.0 * p for b, (p, around) in zip(blocks, rows)]


def without_middle(values):
    return jnp.concatenate([values[..., 0:24, :], values[..., 32:40, :]], axis=-2)


def finish(place, strips, window, finest, right, star, second, third, velocity_new, pressure_new, f2, a2, b2, f3, a3, b3, g1, f1, a1, b1, c1, d1, e1, p0, q0):
    gy = place[1]
    for j in range(8):
        peer = (gy + j) % 8
        for b in range(2 * WINDOW + 1):
            f2[b, 4 * j : 4 * j + 4, :] = strips[peer, b]
    for b in range(9):
        a2[b] = -COEFF * f2[b]
    packed_sweep(b2, a2, f2, range(9), 1, second[...])
    for b, total in zip(range(1, 8), packed_residual(b2, f2, range(1, 8), 1, second[...])):
        lane = lane_of(total)
        total = total + jnp.where((lane & 1) == 0, turn(total, -1, 1), turn(total, 1, 1))
        total = total + jnp.where((lane & 4) == 0, turn(total, -4, 1), turn(total, 4, 1))
        row = row_of(total)
        total = total + jnp.where((row & 1) == 0, turn(total, -1, 0), turn(total, 1, 0))
        f3[b] = 0.5 * total
        a3[b] = (-0.5 * COEFF) * total
    for b in (0, 8):
        a3[b] = jnp.zeros((32, 128), F32)
        b3[b] = jnp.zeros((32, 128), F32)
    packed_sweep(b3, a3, f3, range(1, 8), 2, third[...])
    packed_sweep(a3, b3, f3, range(2, 7), 2, third[...])
    packed_sweep(b3, a3, f3, range(2, 7), 2, third[...])
    for b, total in zip(range(3, 6), packed_residual(b3, f3, range(3, 6), 2, third[...])):
        line = jnp.sum(total, axis=0, keepdims=True) * (COEFF / 32.0)
        a2[b] = b2[b] + (b3[b] - line)
    packed_sweep(b2, a2, f2, range(3, 6), 1, second[...])
    packed_sweep(a2, b2, f2, range(3, 6), 1, second[...])
    g1[:, 0:B, :] = window[...]
    for unit, group, count in GROUPS:
        for k in range(count):
            first = B + 4 * k
            g1[group, first : first + 4, :] = strips[(gy + 1) % 8, unit + k]
            first = B + 24 - 4 * (count - k)
            g1[group, first : first + 4, :] = strips[(gy + 7) % 8, unit + k]
    for x in range(3, 21):
        packed = g1[x // 4]
        slots = 2 * (row_of(packed) & 1) + (lane_of(packed) & 1)
        slot = x % 4
        part = jnp.where(slots == slot, packed, 0.0)
        part = part + turn(part, 1 if slot % 2 == 0 else -1, 1)
        part = part + turn(part, 1 if slot < 2 else -1, 0)
        f1[x] = part
        a1[x] = -COEFF * part
    sweep(b1, a1, f1, 4, 20, 2, 2)
    for k in range(8):
        block = a2[3 + (k + 2) // 4]
        slot = (k + 2) % 4
        low, high = block[0:8], block[24:32]
        part = jnp.where(row_of(low) < 6, low, high)
        part = jnp.where((lane_of(part) & 3) == slot, part, 0.0)
        part = part + turn(part, 1 if slot % 2 == 0 else -1, 1)
        part = part + turn(part, 2 if slot < 2 else -2, 1)
        for q in range(8):
            e1[k, 4 * q : 4 * q + 4, :] = jnp.broadcast_to(part[q : q + 1, :], (4, 128))
    for r in range(4, 20):
        c1[r] = without_middle(b1[r]) + e1[(r - 4) // 2]
    for dst, src, first, last in ((d1, c1, 5, 19), (c1, d1, 6, 18)):
        for i, n in chunks(first, last):
            p, around = neighbours(src, i, n, 2, 2)
            dst[i : i + n] = 0.2 * p + COEFF * (around - without_middle(f1[i : i + n]))
    for i in range(22):
        coarse = c1[6 + (i + 1) // 2]
        edge = coarse[16:24]
        p0[i, 0:B, :] = finest[i, 0:B, :] + coarse[0:B]
        p0[i, B:, :] = finest[i, B:, :] + jnp.where(row_of(edge) < 4, edge, coarse[24:32])
    sweep(q0, p0, right, 1, 21, 1, 1, 1)
    sweep(p0, q0, right, 2, 20, 1, 1, 1)
    for i in range(B):
        p = p0[3 + i]
        lane = lane_of(p)
        above = jnp.where(lane == 127, p, turn(p, -1, 1))
        below = jnp.where(lane == 0, p, turn(p, 1, 1))
        along_x = p0[4 + i] - p0[2 + i]
        along_y = turn(p, -1, 0) - turn(p, 1, 0)
        velocity_new[0, i] = star[0, i] - (0.5 * STEP) * along_x[0:B]
        velocity_new[1, i] = star[1, i] - (0.5 * STEP) * along_y[0:B]
        velocity_new[2, i] = star[2, i] - STEP * (above - below)[0:B]
        pressure_new[i] = p[0:B]


def swaps(count):
    near = [(i, i ^ 1) for i in range(count)]
    far = [(i, (((i + 1) ^ 1) - 1) % count) for i in range(count)]
    return near, far


def exchange(near_block, far_block, axis):
    near, far = swaps(lax.axis_size(axis))
    far_block = lax.ppermute(far_block, axis, far)
    return lax.ppermute(near_block, axis, near), far_block


def per_device(velocity, pressure, land_type, turbine_cells, surface_drag):
    gx = lax.axis_size("gx")
    gy = lax.axis_size("gy")
    place = jnp.stack([lax.axis_index("gx"), lax.axis_index("gy")]).astype(jnp.int32)
    staged = (surface_drag, land_type, velocity, pressure, turbine_cells)
    near, far = call(
        pack_x,
        [shape(SIDE, B, 128), shape(SIDE, B, 128)],
        [HBM] * 5,
        [
            pltpu.SMEM((16,), F32),
            pltpu.VMEM((B, B), jnp.int32),
            pltpu.VMEM((B, B, 128), jnp.int32),
            (B, B, 128),
            pltpu.SemaphoreType.DMA((11,)),
        ],
    )(*[pltpu.with_memory_space_constraint(x, pltpu.HBM) for x in staged])
    near, far = exchange(near, far, "gx")
    wide_v, wide_p, wide_d, near, far, near_p, far_p = call(
        widen_x,
        [shape(3, VX, B, 128), shape(PX, B, 128), shape(PX, B, 128)]
        + [shape(8, 40, 128)] * 2
        + [shape(N_P, 4, 128)] * 2,
        [SMEM, SMEM] + [VMEM] * 6,
    )(place, surface_drag, land_type, velocity, pressure, turbine_cells, far, near)
    near, far = exchange(near, far, "gy")
    near_p, far_p = exchange(near_p, far_p, "gy")
    star, source, near, far = call(
        advance,
        [shape(3, B, B, 128), shape(PX - 2, B, 128), shape(N_S, 128), shape(N_S, 128)],
        [SMEM] + [VMEM] * 4,
        [(3, VX, 24, 128), (VX, 24, 128), (3, VX, 24, 128), (3, VX, 24, 128)],
    )(place, wide_v, wide_d, far, near)
    near, far = exchange(near, far, "gy")
    finest, right, packed_one, packed_two = call(
        presmooth,
        [shape(22, 24, 128), shape(20, 24, 128), shape(2, B, 128), shape(gx, 4, 128)],
        [SMEM] + [VMEM] * 6,
        [(PX, 32, 128)] * 3 + [(12, 32, 128)] * 3,
    )(place, source, wide_p, far, near, near_p, far_p)
    near, far = exchange(packed_one, packed_one, "gx")
    blocks = lax.all_to_all(packed_two, "gx", 0, 0, tiled=True)
    strips, window = call(
        lambda *refs: pack_y(gx, *refs),
        [shape(gy, N_STRIP, 4, 128), shape(6, B, 128)],
        [SMEM] + [VMEM] * 4,
    )(place, blocks, packed_one, near, far)
    strips = lax.all_to_all(strips, "gy", 0, 0, tiled=True)
    velocity_new, pressure_new = call(
        finish,
        [shape(3, B, B, 128), shape(B, B, 128)],
        [SMEM] + [VMEM] * 7,
        [(9, 32, 128)] * 6
        + [(6, 40, 128)]
        + [(24, 40, 128)] * 3
        + [(24, 32, 128)] * 2
        + [(8, 32, 128)]
        + [(22, 24, 128)] * 2,
    )(place, strips, window, finest, right, star, packed_matrix(1, 4), packed_matrix(2, 8))
    return velocity_new, pressure_new


def solution(mesh):
    in_specs = (
        P(None, "gx", "gy", None),
        P("gx", "gy", None),
        P("gx", "gy"),
        P("gx", "gy", None),
        P(),
    )
    out_specs = (P(None, "gx", "gy", None), P("gx", "gy", None))
    return jax.shard_map(
        per_device, mesh=mesh, in_specs=in_specs, out_specs=out_specs, check_vma=False
    )
```
